32 devices in a mesh: rows: 2 (over core), cols: 16 (over z, y, x).
Axes of the slice: x: 2, y: 2, z: 4, core: 2. Of those that a mesh axis runs over, the one named last changes fastest.
Arguments:
- wind_speed: float32 [16, 2048], P('rows', 'cols'), may hold values from 3 to 25
- wind_dir: float32 [16, 2048], P('rows', 'cols'), may hold values from -3.140625 to 3.140625
- depth_class: int32 [16, 2048], P('rows', 'cols'), may hold values from 0 to 3
- group_speed: float32 [4, 24], replicated, may hold values from 0.3 to 3
- dissipation: float32 [4, 24], replicated, may hold values from 0.02 to 1
- input_rate: float32 [24], replicated, may hold values from 0.02 to 0.2
- outer_spectra: float32 [8192, 864], P(('rows', 'cols')), may hold values from -6 to 6
- dest_cell: int32 [8192], P(('rows', 'cols')), may hold values from 0 to 32767, as said below
- refraction_inverse: float32 [4, 216, 216], replicated, as said below
- sweep_order: int32 [2, 4], replicated, may hold values from 0 to 3, as said below
Outputs:
- wave_action: float32 [864, 16, 2048], P(None, 'rows', 'cols')
The draws below stay inside these ranges and needn't reach their ends.
Inputs may be any that keep to these rules, and one draw needn't show every extreme that they name: `dest_cell`: every boundary point feeds a cell on the grid's outermost rows or columns. Among the points held by one device, at most 16 feed cells held by any one device, and in every draw one device receives exactly 16 points from every device. `refraction_inverse`: each matrix has a diagonal between 0.75 and 1 and off-diagonal entries below 1.2 / 216 in magnitude. `sweep_order`: each row names each of the four quadrants once.
All inputs are finite; a program needn't handle non-finite values.
Results may differ from the reference program's by a relative error of at most 0.0003.
Values sent between devices are 32-bit elements; how exact they have to be, the bound alone decides.
No kernel may reach another device: no remote copies, remote signals or barrier semaphores. Data moves between devices by JAX's collectives and lax.ppermute only.
A program may use at most 192 MiB of HBM per device.

```python
import math
import jax
import jax.numpy as jnp
import numpy as np
from jax import lax

NDIR = 36
NFREQ = 24
NCLASS = 4
CAP = 16
ITERS = 2
R_DEV = 8
C_DEV = 128
NX = 16
NY = 2048
K = 864
KQ = 216
Q_DEV = 256
NPTS = 8192


def draw_dest_cell(key, part):
    row_count = NX // R_DEV
    col_count = NY // C_DEV
    devices = row_count * col_count
    edge_list = [(r_id, c_id) for r_id in range(row_count) for c_id in range(col_count) if r_id == 0 or r_id == row_count - 1 or c_id == 0 or (c_id == col_count - 1)]
    edge_total = len(edge_list)
    edge_row = jnp.array(np.array([item[0] for item in edge_list], np.int32))
    edge_col = jnp.array(np.array([item[1] for item in edge_list], np.int32))
    fixed_row = jnp.array(np.array([0 if item[0] == 0 else R_DEV - 1 if item[0] == row_count - 1 else -1 for item in edge_list], np.int32))
    fixed_col = jnp.array(np.array([-1 if item[0] == 0 or item[0] == row_count - 1 else 0 if item[1] == 0 else C_DEV - 1 for item in edge_list], np.int32))
    forced = jax.random.randint(jax.random.fold_in(key, 1), (), 0, edge_total)

    def one_device(source_key):
        key_pick, key_row, key_col, key_order = jax.random.split(source_key, 4)
        others = jax.random.permutation(key_pick, (edge_total - 1) * CAP)[:Q_DEV - CAP]
        picked = others // CAP
        picked = jnp.where(picked >= forced, picked + 1, picked)
        owner_id = jnp.concatenate([jnp.full((CAP,), forced, jnp.int32), picked.astype(jnp.int32)])
        random_row = jax.random.randint(key_row, (Q_DEV,), 0, R_DEV)
        random_col = jax.random.randint(key_col, (Q_DEV,), 0, C_DEV)
        row_pick = jnp.where(fixed_row[owner_id] >= 0, fixed_row[owner_id], random_row)
        col_pick = jnp.where(fixed_col[owner_id] >= 0, fixed_col[owner_id], random_col)
        cell_id = (edge_row[owner_id] * R_DEV + row_pick) * NY + edge_col[owner_id] * C_DEV + col_pick
        shuffle = jax.random.permutation(key_order, Q_DEV)
        return cell_id[shuffle]
    device_keys = jax.random.split(jax.random.fold_in(key, 2), devices)
    return jax.vmap(one_device)(device_keys).reshape(-1).astype(jnp.int32)


def draw_refraction_inverse(key, part):
    key_diag, key_off = jax.random.split(key, 2)
    diag_vals = jax.random.uniform(key_diag, (4, KQ), jnp.float32, 0.75, 1.0)
    off_diag = jax.random.uniform(key_off, (4, KQ, KQ), jnp.float32, -1.0, 1.0) * (0.8 / KQ)
    identity = jnp.eye(KQ, dtype=jnp.float32)
    return off_diag * (1.0 - identity) + identity * diag_vals[:, :, None]


def draw_sweep_order(key, part):
    order_rows = [jax.random.permutation(jax.random.fold_in(key, 101 + round_id), 4) for round_id in range(ITERS)]
    return jnp.stack(order_rows, axis=0).astype(jnp.int32)


def with_ends(entries, own_key, low, largest):
    index_at = [jax.random.randint(jax.random.fold_in(own_key, axis), (), 0, length) for axis, length in enumerate(entries.shape)]
    longest = entries.shape.index(max(entries.shape))
    beside = index_at[:longest] + [(index_at[longest] + 1) % entries.shape[longest]] + index_at[longest + 1:]
    return entries.at[tuple(index_at)].set(low).at[tuple(beside)].set(largest)


def level_of(own_key, shape, cuts, low, top_value):
    factor_of = 1.0
    for axis_at, blocks in cuts:
        draws = jax.random.uniform(jax.random.fold_in(jax.random.fold_in(own_key, 6), axis_at), (blocks,), jnp.float32, low / len(cuts), top_value / len(cuts))
        factor_of = factor_of * jnp.repeat(jnp.exp(draws), shape[axis_at] // blocks).reshape((-1,) + (1,) * (len(shape) - 1 - axis_at))
    return factor_of


def bell_draw(own_key, extent, deviation, reach, shards=(), kind=jnp.bfloat16):
    drawn = jax.random.normal(own_key, extent, jnp.float32) * deviation
    if len(shards) > 0:
        drawn = level_of(own_key, extent, shards, -0.22, 0.18) * drawn
    return jnp.clip(drawn, min=-reach, max=reach).astype(kind)


def setup_inputs(seed: int = 0) -> dict:
    keys = jax.random.split(jax.random.key(seed), 11)
    return {
        "wind_speed": jnp.clip(jnp.exp(math.log(25.0) - 2.1202635 * jax.random.uniform(keys[0], (NX, NY), jnp.float32) ** level_of(keys[0], (NX, NY), ((0, 2), (1, 16)), -0.2, 0.2)), 3.0, 25.0),
        "wind_dir": jnp.clip(jax.random.uniform(keys[1], (NX, NY), jnp.float32, -3.140625, 3.140625), -3.140625, 3.140625),
        "depth_class": with_ends(jax.random.randint(keys[2], (NX, NY), 0, NCLASS), jax.random.fold_in(keys[2], 1), 0, NCLASS - 1).astype(jnp.int32),
        "group_speed": jnp.clip(jnp.exp(jax.random.uniform(keys[3], (NCLASS, NFREQ), jnp.float32, math.log(0.3), math.log(3.0))), 0.3, 3.0),
        "dissipation": jnp.clip(jnp.exp(jax.random.uniform(keys[4], (NCLASS, NFREQ), jnp.float32, math.log(0.02), math.log(1.0))), 0.02, 1.0),
        "input_rate": jnp.clip(jnp.exp(jax.random.uniform(keys[5], (NFREQ,), jnp.float32, math.log(0.02), math.log(0.2))), 0.02, 0.2),
        "outer_spectra": bell_draw(keys[6], (NPTS, K), 1.0, 6.0, ((0, 32),), jnp.float32),
        "dest_cell": draw_dest_cell(jax.random.fold_in(keys[10], 71), 0),
        "refraction_inverse": draw_refraction_inverse(jax.random.fold_in(keys[10], 71), 0),
        "sweep_order": draw_sweep_order(jax.random.fold_in(keys[10], 71), 0),
    }


whitecap_rate = 0.5


def reference(wind_speed, wind_dir, depth_class, group_speed, dissipation, input_rate, outer_spectra, dest_cell, refraction_inverse, sweep_order):
    angle = (jnp.arange(NDIR, dtype=jnp.float32) + 0.5) * (2.0 * math.pi / NDIR)
    cos_abs = jnp.abs(jnp.cos(angle))
    sin_abs = jnp.abs(jnp.sin(angle))
    quarter = NDIR // 4
    grid_row = dest_cell // NY
    grid_col = dest_cell % NY
    rim_slot = jnp.where(grid_row == 0, grid_col, jnp.where(grid_row == NX - 1, NY + grid_col, jnp.where(grid_col == 0, 2 * NY + grid_row, 2 * NY + NX + grid_row)))
    rim_sums = jax.ops.segment_sum(outer_spectra, rim_slot, num_segments=2 * NY + 2 * NX)
    top_row = rim_sums[:NY].T
    bottom_row = rim_sums[NY:2 * NY].T
    left_col = rim_sums[2 * NY:2 * NY + NX]
    right_col = rim_sums[2 * NY + NX:]
    classes = jnp.arange(NCLASS, dtype=jnp.int32)

    def sweep(state, quadrant):
        step_x = (1, -1, -1, 1)[quadrant]
        step_y = (1, 1, -1, -1)[quadrant]
        comp_low = quadrant * KQ
        comp_high = comp_low + KQ
        energy = jnp.mean(state * state, axis=0)
        previous = state[comp_low:comp_high]
        zero_col = jnp.zeros_like(previous[:, :, :1])
        if step_y == 1:
            beside = jnp.concatenate([zero_col, previous[:, :, :-1]], axis=2)
        else:
            beside = jnp.concatenate([previous[:, :, 1:], zero_col], axis=2)
        dir_cos = cos_abs[quadrant * quarter:(quadrant + 1) * quarter]
        dir_sin = sin_abs[quadrant * quarter:(quadrant + 1) * quarter]
        dir_angle = angle[quadrant * quarter:(quadrant + 1) * quarter]
        matrix = refraction_inverse[quadrant]

        def row_update(upwind, row_id):
            onehot = (depth_class[row_id][None, :] == classes[:, None]).astype(jnp.float32)
            speeds = jnp.sum(group_speed[:, :, None] * onehot[:, None, :], axis=0)
            losses = jnp.sum(dissipation[:, :, None] * onehot[:, None, :], axis=0)
            level = energy[row_id]
            damping = losses + whitecap_rate * level / (1.0 + level)
            along_x = dir_cos[:, None, None] * speeds[None]
            along_y = dir_sin[:, None, None] * speeds[None]
            denominator = (along_x + along_y + damping[None]).reshape(KQ, NY)
            spread = jnp.maximum(jnp.cos(dir_angle[:, None] - wind_dir[row_id][None, :]), 0.0)
            strength = (wind_speed[row_id] * 0.1) ** 2
            wind_input = (input_rate[None, :, None] * strength[None, None] * (spread * spread)[:, None]).reshape(KQ, NY)
            forcing = jnp.where(row_id == 0, top_row, 0.0) + jnp.where(row_id == NX - 1, bottom_row, 0.0)
            forcing = forcing.at[:, 0].add(left_col[row_id]).at[:, NY - 1].add(right_col[row_id])
            source = wind_input + forcing[comp_low:comp_high]
            known = along_y.reshape(KQ, NY) * beside[:, row_id] + source
            balance = (along_x.reshape(KQ, NY) * upwind + known) / denominator
            updated = jnp.dot(matrix, balance, precision=lax.Precision.HIGHEST, preferred_element_type=jnp.float32)
            return updated, updated

        final_row, new_rows = lax.scan(row_update, jnp.zeros((KQ, NY), jnp.float32), jnp.arange(NX, dtype=jnp.int32), reverse=(step_x == -1))
        return state.at[comp_low:comp_high].set(jnp.transpose(new_rows, (1, 0, 2)))

    branches = [lambda state, quad=quad: sweep(state, quad) for quad in range(4)]
    state = jnp.zeros((K, NX, NY), jnp.float32)
    for sweep_round in range(ITERS):
        for turn in range(4):
            state = lax.switch(sweep_order[sweep_round, turn], branches, state)
    return state
```

```python
import math

import jax
import jax.numpy as jnp
import numpy as np
from jax import lax
from jax.experimental import pallas as pl
from jax.experimental.pallas import tpu as pltpu
from jax.sharding import PartitionSpec as P

NDIR = 36
NFREQ = 24
CAP = 16
ITERS = 2
QUADS = 4
LANES = 128
HALO = 8

whitecap_rate = 0.5


def split_bf16(value):
    high = value.astype(jnp.bfloat16)
    low = (value - high.astype(jnp.float32)).astype(jnp.bfloat16)
    return high, low


def split_rounded(value):
    rounded = lax.reduce_precision(value, 8, 7)
    return rounded.astype(jnp.bfloat16), (value - rounded).astype(jnp.bfloat16)


def pad_to(array, axis, size, value=0.0):
    widths = [(0, 0)] * array.ndim
    widths[axis] = (0, size - array.shape[axis])
    return jnp.pad(array, widths, constant_values=value)


def sweeps_kernel(rows, own, cells, quad_size, info, ax_ref, ay_ref, base_ref, wind_ref, mt_ref,
                  own_ref, par_ref, same_ref, cross_ref, keep_ref, send_ref,
                  state, power, rim, side):
    turn = pl.program_id(0)
    quad = info[turn]
    half = info[ITERS * QUADS]
    width = mt_ref.shape[2]
    rows_dev = rows // 2
    down = (quad == 0) | (quad == 3)
    step_x = jnp.where(down, 1, -1)
    first_row = jnp.where(down, 0, rows - 1)
    up_y = quad < 2

    @pl.when(turn == 0)
    def _():
        power[...] = jnp.zeros_like(power)

    rim[0] = own_ref[0, 0:cells]
    rim[0, own:cells] = own_ref[0, own:cells] + same_ref[0]
    rim[1] = par_ref[0, 0:cells]
    rim[1, own:cells] = par_ref[0, own:cells] + cross_ref[0]
    edge_at = jnp.where(half == 0, 0, 2 * HALO - 1)
    at_edge = lax.broadcasted_iota(jnp.int32, (2 * HALO, width), 0) == edge_at
    for j in range(rows_dev):
        mine = jnp.where(at_edge, own_ref[0, cells + j:cells + j + 1], 0.0)
        theirs = jnp.where(at_edge, par_ref[0, cells + j:cells + j + 1], 0.0)
        side[j + rows_dev * half] = mine
        side[j + rows_dev * (1 - half)] = theirs

    def run(count, second):
        def factors(i):
            row = first_row + i * step_x
            total = power[0, row, :count]
            for other in range(1, QUADS):
                total = total + power[other, row, :count]
            level = total * (1.0 / (QUADS * quad_size))
            damping = whitecap_rate * level / (1.0 + level)
            den = base_ref[0, row, :count] + jnp.concatenate([damping] * (width // LANES), axis=1)
            inverse = 1.0 / den
            source = wind_ref[0, row, :count]
            edge = side[row]
            parts = [source[:HALO] + edge[:HALO], source[HALO:own - HALO],
                     source[own - HALO:own] + edge[HALO:]]
            if count > own:
                parts.append(source[own:])
            source = jnp.concatenate(parts, axis=0)
            if i == 0 or i == rows - 1:
                here = jnp.where(row // rows_dev == half, 0, 1)
                source = source + rim[here, :count]
            if second:
                before = state[quad, row]
                shifted = jnp.where(up_y, pltpu.roll(before, 1, 0), pltpu.roll(before, cells - 1, 0))
                source = source + ay_ref[0, row, :count] * shifted[:count]
            return row, ax_ref[0, row, :count] * inverse, source * inverse

        row, along, known = factors(0)
        upwind = None
        for i in range(rows):
            balance = known if upwind is None else along * upwind + known
            high, low = split_bf16(balance)
            updated = jnp.dot(jnp.concatenate([high, high, low], axis=1), mt_ref[0],
                              preferred_element_type=jnp.float32)
            here = row
            if i + 1 < rows:
                row, along, known = factors(i + 1)
            square = updated * updated
            folded = square[:, :LANES]
            for lane in range(LANES, width, LANES):
                folded = folded + square[:, lane:lane + LANES]
            state[quad, here, :count] = updated
            power[quad, here, :count] = jnp.broadcast_to(
                jnp.sum(folded, axis=1, keepdims=True), (count, LANES))
            upwind = updated

    @pl.when(turn < QUADS)
    def _():
        run(cells, False)

    @pl.when(turn >= QUADS)
    def _():
        run(own, True)

    @pl.when(turn == ITERS * QUADS - 1)
    def _():
        for pair in range(QUADS // 2):
            for j in range(rows_dev):
                for out_ref, side_at in ((keep_ref, half), (send_ref, 1 - half)):
                    row = rows_dev * side_at + j
                    both = jnp.concatenate(
                        [state[2 * pair, row, :own], state[2 * pair + 1, row, :own]], axis=0)
                    out_ref[pair, :, j, :] = both.T[:quad_size]


def merge_kernel(own, info, keep_ref, got_ref, out_ref):
    half = info[ITERS * QUADS]
    keep = keep_ref[0]
    got = got_ref[0]
    left = jnp.where(half == 0, keep, got)
    right = jnp.where(half == 0, got, keep)
    low = lax.broadcasted_iota(jnp.int32, keep.shape, 2) < own
    axis = keep.ndim - 1
    out_ref[0, 0] = jnp.where(low, left, pltpu.roll(right, own, axis))
    out_ref[0, 1] = jnp.where(low, pltpu.roll(left, own, axis), right)


def body(
    wind_speed,
    wind_dir,
    depth_class,
    group_speed,
    dissipation,
    input_rate,
    outer_spectra,
    dest_cell,
    refraction_inverse,
    sweep_order,
):
    rows_dev, cols_dev = wind_speed.shape
    row_count = lax.axis_size("rows")
    col_count = lax.axis_size("cols")
    assert row_count == 2
    devices = row_count * col_count
    rows = rows_dev * row_count
    own = cols_dev // 2
    cells = own + HALO
    class_count = group_speed.shape[0]
    comps = outer_spectra.shape[1]
    quad_size = refraction_inverse.shape[1]
    quarter = NDIR // QUADS
    width = -(-quad_size // LANES) * LANES
    axes = ("rows", "cols")
    half = lax.axis_index("rows")

    def device(row_at, col_at):
        return row_at * col_count + col_at

    span = range(col_count)
    swap_route = [(device(1 - h, c), device(h, c)) for h in range(2) for c in span]
    same_route = [(device(0, c - 1), device(0, c)) for c in span if c > 0]
    same_route += [(device(1, c + 1), device(1, c)) for c in span if c + 1 < col_count]
    cross_route = [(device(1, c - 1), device(0, c)) for c in span if c > 0]
    cross_route += [(device(0, c + 1), device(1, c)) for c in span if c + 1 < col_count]

    points = dest_cell.shape[0]
    total_cols = cols_dev * col_count
    grid_row = dest_cell // total_cols
    grid_col = dest_cell % total_cols
    owner = grid_row // rows_dev * col_count + grid_col // cols_dev
    local_row = grid_row % rows_dev
    local_col = grid_col % cols_dev
    rim_code = jnp.where(
        (grid_row == 0) | (grid_row == rows - 1),
        local_col,
        jnp.where(grid_col == 0, cols_dev + local_row, cols_dev + rows_dev + local_row),
    )
    position = jnp.arange(points, dtype=jnp.int32)
    earlier = (owner[:, None] == owner[None, :]) & (position[:, None] > position[None, :])
    slot = owner * CAP + jnp.sum(earlier.astype(jnp.int32), axis=1)
    load = -(-(comps + 1) // LANES) * LANES
    payload = pad_to(
        jnp.concatenate([outer_spectra, (rim_code + 1).astype(jnp.float32)[:, None]], axis=1), 1, load)
    place = (jnp.arange(devices * CAP, dtype=jnp.int32)[:, None] == slot[None, :]).astype(jnp.float32)
    outgoing = jnp.dot(place, payload, precision=lax.Precision.HIGHEST,
                       preferred_element_type=jnp.float32)
    arrived = lax.all_to_all(outgoing.reshape(devices, CAP, load), axes, split_axis=0,
                             concat_axis=0, tiled=True).reshape(devices * CAP, load)

    held = jnp.stack([wind_speed, wind_dir, depth_class.astype(jnp.float32)])
    partner = lax.ppermute(held, axes, swap_route)
    beside_same = lax.ppermute(held, axes, same_route)
    beside_cross = lax.ppermute(held, axes, cross_route)
    is_low = half == 0
    chip = jnp.concatenate(
        [jnp.where(is_low, held, partner), jnp.where(is_low, partner, held)], axis=1)
    near = jnp.concatenate(
        [jnp.where(is_low, beside_same, beside_cross), jnp.where(is_low, beside_cross, beside_same)],
        axis=1)
    mine = jnp.where(is_low, chip[:, :, :own], chip[:, :, own:])
    right = jnp.where(is_low, chip[:, :, own], near[:, :, 0])
    left = jnp.where(is_low, near[:, :, cols_dev - 1], chip[:, :, own - 1])
    grid = jnp.concatenate(
        [mine, right[:, :, None], jnp.zeros((3, rows, HALO - 2), jnp.float32), left[:, :, None]], axis=2)
    speed_here, dir_here, class_here = grid[0], grid[1], grid[2]
    strength = (speed_here * 0.1) ** 2
    cos_here, sin_here = jnp.cos(dir_here), jnp.sin(dir_here)

    angle = (jnp.arange(NDIR, dtype=jnp.float32) + 0.5) * (2.0 * math.pi / NDIR)
    cos_lane = pad_to(jnp.repeat(jnp.cos(angle), NFREQ).reshape(QUADS, quad_size), 1, width)
    sin_lane = pad_to(jnp.repeat(jnp.sin(angle), NFREQ).reshape(QUADS, quad_size), 1, width)
    rate_lane = pad_to(jnp.tile(input_rate, quarter), 0, width)
    speed_lane = pad_to(jnp.tile(group_speed, (1, quarter)), 1, width)
    loss_lane = pad_to(jnp.tile(dissipation, (1, quarter)), 1, width, 1.0)
    ax_table = jnp.abs(cos_lane)[:, None] * speed_lane[None]
    ay_table = jnp.abs(sin_lane)[:, None] * speed_lane[None]
    base_table = ax_table + ay_table + loss_lane[None]

    def by_class(table):
        chosen = jnp.broadcast_to(table[:, None, None, 0], (QUADS, rows, cells, width))
        for kind in range(1, class_count):
            chosen = jnp.where((class_here == kind)[None, :, :, None], table[:, None, None, kind], chosen)
        return chosen

    ax = by_class(ax_table)
    ay = by_class(ay_table)
    base = by_class(base_table)
    spread = jnp.maximum(
        cos_here[None, :, :, None] * cos_lane[:, None, None]
        + sin_here[None, :, :, None] * sin_lane[:, None, None], 0.0)
    wind = (rate_lane[None, None, None] * strength[None, :, :, None]) * (spread * spread)

    flipped = pad_to(pad_to(jnp.swapaxes(refraction_inverse, 1, 2), 1, width), 2, width)
    flip_high, flip_low = split_rounded(flipped)
    matrices = jnp.concatenate([flip_high, flip_low, flip_high], axis=1)

    code = arrived[:, comps].astype(jnp.int32) - 1

    def place_in(side_at):
        col = code - own * side_at
        spot = jnp.where((code < cols_dev) & (code >= 0) & (col >= 0) & (col < own), col, -1)
        spot = jnp.where((side_at == 0) & (code == own), own, spot)
        spot = jnp.where((side_at == 1) & (code == own - 1), cells - 1, spot)
        along = code - cols_dev - rows_dev * side_at
        return jnp.where((along >= 0) & (along < rows_dev) & (code >= cols_dev), cells + along, spot)

    block = cells + rows_dev
    slots = jnp.arange(2 * block + 2 * HALO, dtype=jnp.int32)[:, None]
    to_own = place_in(half)[None, :]
    to_partner = place_in(1 - half)[None, :]
    out_right = code[None, :] == cols_dev - 1
    out_left = code[None, :] == 0
    to_same = jnp.where(is_low, jnp.where(out_right, HALO - 1, -1), jnp.where(out_left, 0, -1))
    to_cross = jnp.where(is_low, jnp.where(out_left, 0, -1), jnp.where(out_right, HALO - 1, -1))
    gather = (
        ((slots == to_own) & (to_own >= 0))
        | ((slots == to_partner + block) & (to_partner >= 0))
        | ((slots == to_same + 2 * block) & (to_same >= 0))
        | ((slots == to_cross + 2 * block + HALO) & (to_cross >= 0))
    ).astype(jnp.float32)
    summed = jnp.dot(gather, arrived, precision=lax.Precision.HIGHEST,
                     preferred_element_type=jnp.float32)[:, :comps]
    summed = jnp.swapaxes(summed.reshape(-1, QUADS, quad_size), 0, 1)
    summed = pad_to(summed, 2, width)
    rim_own = summed[:, :block]
    rim_partner = lax.ppermute(summed[:, block:2 * block], axes, swap_route)
    rim_same = lax.ppermute(summed[:, 2 * block:2 * block + HALO], axes, same_route)
    rim_cross = lax.ppermute(summed[:, 2 * block + HALO:], axes, cross_route)

    info = jnp.concatenate([sweep_order.reshape(-1), half[None].astype(jnp.int32)])
    turns = ITERS * QUADS

    def quad_block(shape):
        zeros = (0,) * len(shape)
        return pl.BlockSpec((1,) + shape, lambda t, info: (info[t],) + zeros)

    packed = (QUADS // 2, quad_size, rows_dev, cols_dev)
    whole = pl.BlockSpec(packed, lambda t, info: (0, 0, 0, 0))
    keep, send = pl.pallas_call(
        lambda *refs: sweeps_kernel(rows, own, cells, quad_size, *refs),
        grid_spec=pltpu.PrefetchScalarGridSpec(
            num_scalar_prefetch=1,
            grid=(turns,),
            in_specs=[quad_block((rows, cells, width))] * 4
            + [quad_block((3 * width, width))]
            + [quad_block((block, width))] * 2
            + [quad_block((HALO, width))] * 2,
            out_specs=[whole, whole],
            scratch_shapes=[
                pltpu.VMEM((QUADS, rows, cells, width), jnp.float32),
                pltpu.VMEM((QUADS, rows, cells, LANES), jnp.float32),
                pltpu.VMEM((2, cells, width), jnp.float32),
                pltpu.VMEM((rows, 2 * HALO, width), jnp.float32),
            ],
        ),
        out_shape=[jax.ShapeDtypeStruct(packed, jnp.float32)] * 2,
        compiler_params=pltpu.CompilerParams(
            dimension_semantics=("arbitrary",), vmem_limit_bytes=44 * 2**20),
    )(info, ax, ay, base, wind, matrices, rim_own, rim_partner, rim_same, rim_cross)

    got = lax.ppermute(send, axes, swap_route)
    chunks = 4
    part = quad_size // chunks
    half_block = pl.BlockSpec((1, part, rows_dev, cols_dev), lambda p, c, info: (p, c, 0, 0))
    merged = pl.pallas_call(
        lambda *refs: merge_kernel(own, *refs),
        grid_spec=pltpu.PrefetchScalarGridSpec(
            num_scalar_prefetch=1,
            grid=(QUADS // 2, chunks),
            in_specs=[half_block, half_block],
            out_specs=pl.BlockSpec(
                (1, 2, part, rows_dev, cols_dev), lambda p, c, info: (p, 0, c, 0, 0)),
        ),
        out_shape=jax.ShapeDtypeStruct((QUADS // 2, 2, quad_size, rows_dev, cols_dev), jnp.float32),
        compiler_params=pltpu.CompilerParams(vmem_limit_bytes=16 * 2**20),
    )(info, keep, got)
    return merged.reshape(comps, rows_dev, cols_dev)


def solution(mesh):
    placed = (
        P("rows", "cols"),
        P("rows", "cols"),
        P("rows", "cols"),
        P(),
        P(),
        P(),
        P(("rows", "cols"), None),
        P(("rows", "cols")),
        P(),
        P(),
    )
    return jax.shard_map(
        body, mesh=mesh, in_specs=placed, out_specs=P(None, "rows", "cols"), check_vma=False
    )
```

```python
import math

import jax
import jax.numpy as jnp
import numpy as np
from jax import lax
from jax.experimental import pallas as pl
from jax.experimental.pallas import tpu as pltpu
from jax.sharding import PartitionSpec as P

NDIR = 36
NFREQ = 24
CAP = 16
ITERS = 2
QUADS = 4
LANES = 128
HALO = 8

whitecap_rate = 0.5


def split_bf16(value):
    high = value.astype(jnp.bfloat16)
    low = (value - high.astype(jnp.float32)).astype(jnp.bfloat16)
    return high, low


def split_rounded(value):
    rounded = lax.reduce_precision(value, 8, 7)
    return rounded.astype(jnp.bfloat16), (value - rounded).astype(jnp.bfloat16)


def pad_to(array, axis, size, value=0.0):
    widths = [(0, 0)] * array.ndim
    widths[axis] = (0, size - array.shape[axis])
    return jnp.pad(array, widths, constant_values=value)


def pack_kernel(shifts, col_count, rows, comps, dest_ref, spectra_ref, out_ref, high, low, slots):
    step = pl.program_id(0)
    points = dest_ref.shape[1]
    load = out_ref.shape[1]
    total_bits, row_bits, col_bits = shifts

    @pl.when(step == 0)
    def _():
        dest = dest_ref[...]
        grid_row = lax.shift_right_logical(dest, total_bits)
        grid_col = dest & (2**total_bits - 1)
        local_row = grid_row & (2**row_bits - 1)
        local_col = grid_col & (2**col_bits - 1)
        owner = (lax.shift_right_logical(grid_row, row_bits) * col_count
                 + lax.shift_right_logical(grid_col, col_bits))
        on_row = (grid_row == 0) | (grid_row == rows - 1)
        on_left = jnp.where(grid_col == 0, 2**col_bits, 2**col_bits + 2**row_bits) + local_row
        code = jnp.where(on_row, local_col, on_left) + 1
        lanes = jnp.concatenate(
            [owner.astype(jnp.float32), code.astype(jnp.float32), jnp.zeros((6, points), jnp.float32)],
            axis=0)
        columns = lanes.T
        same = columns[:, 0:1] == lanes[0:1]
        above = (lax.broadcasted_iota(jnp.int32, (points, points), 0)
                 < lax.broadcasted_iota(jnp.int32, (points, points), 1))
        rank = jnp.sum(jnp.where(same & above, 1.0, 0.0), axis=0, keepdims=True)
        slots[...] = owner * CAP + rank.astype(jnp.int32)
        spectra = jnp.concatenate(
            [spectra_ref[...], jnp.broadcast_to(columns[:, 1:2], (points, load - comps))], axis=1)
        high[...], low[...] = split_bf16(spectra)

    place = jnp.where(
        lax.broadcasted_iota(jnp.int32, (out_ref.shape[0], points), 0) + step * out_ref.shape[0]
        == slots[...], 1.0, 0.0).astype(jnp.bfloat16)
    out_ref[...] = (jnp.dot(place, high[...], preferred_element_type=jnp.float32)
                    + jnp.dot(place, low[...], preferred_element_type=jnp.float32))


def rim_kernel(own, rows_dev, comps, quad_size, info, arrived_ref, own_ref, send_ref, same_ref,
               cross_ref):
    half = info[ITERS * QUADS]
    cols_dev = 2 * own
    cells = own + HALO
    block = cells + rows_dev
    width = own_ref.shape[2]
    load = arrived_ref.shape[1]
    spots = -(-(2 * block + 2 * HALO) // LANES) * LANES
    lane = lax.broadcasted_iota(jnp.int32, (1, spots), 1)
    at_send = lane >= block
    spot = jnp.where(at_send, lane - block, lane)
    side_at = jnp.where(at_send, 1 - half, half)
    want = jnp.where(spot < own, own * side_at + spot, -1)
    want = jnp.where((spot == own) & (side_at == 0), own, want)
    want = jnp.where((spot == cells - 1) & (side_at == 1), own - 1, want)
    want = jnp.where(spot >= cells, cols_dev + rows_dev * side_at + spot - cells, want)
    rest = lane - 2 * block
    to_left = jnp.where((rest == HALO - 1) & (half == 0), cols_dev - 1, -1)
    to_left = jnp.where((rest == 0) & (half == 1), 0, to_left)
    to_left = jnp.where((rest == HALO) & (half == 0), 0, to_left)
    to_left = jnp.where((rest == 2 * HALO - 1) & (half == 1), cols_dev - 1, to_left)
    want = jnp.where(rest >= 0, to_left, want)
    code = arrived_ref[:, comps:comps + 1]
    gather = jnp.where(code == (want + 1).astype(jnp.float32), 1.0, 0.0)
    gather = jnp.where(want >= 0, gather, 0.0).astype(jnp.bfloat16)
    high, low = split_bf16(arrived_ref[...])
    over_points = (((0,), (0,)), ((), ()))
    summed = (lax.dot_general(gather, high, over_points, preferred_element_type=jnp.float32)
              + lax.dot_general(gather, low, over_points, preferred_element_type=jnp.float32))
    for quad in range(QUADS):
        start = quad * quad_size
        part = summed if quad == 0 else pltpu.roll(summed, load - start, 1)
        own_ref[quad] = part[:block, :width]
        send_ref[quad] = part[block:2 * block, :width]
        same_ref[quad] = part[2 * block:2 * block + HALO, :width]
        cross_ref[quad] = part[2 * block + HALO:2 * block + 2 * HALO, :width]


def sweeps_kernel(rows, own, cells, quad_size, info, ax_ref, ay_ref, base_ref, wind_ref, mt_ref,
                  own_ref, par_ref, same_ref, cross_ref, keep_ref, send_ref,
                  state, power, rim, side):
    turn = pl.program_id(0)
    quad = info[turn]
    half = info[ITERS * QUADS]
    width = mt_ref.shape[2]
    rows_dev = rows // 2
    down = (quad == 0) | (quad == 3)
    step_x = jnp.where(down, 1, -1)
    first_row = jnp.where(down, 0, rows - 1)
    up_y = quad < 2

    @pl.when(turn == 0)
    def _():
        power[...] = jnp.zeros_like(power)

    rim[0] = own_ref[0, 0:cells]
    rim[0, own:cells] = own_ref[0, own:cells] + same_ref[0]
    rim[1] = par_ref[0, 0:cells]
    rim[1, own:cells] = par_ref[0, own:cells] + cross_ref[0]
    edge_at = jnp.where(half == 0, 0, 2 * HALO - 1)
    at_edge = lax.broadcasted_iota(jnp.int32, (2 * HALO, width), 0) == edge_at
    for j in range(rows_dev):
        mine = jnp.where(at_edge, own_ref[0, cells + j:cells + j + 1], 0.0)
        theirs = jnp.where(at_edge, par_ref[0, cells + j:cells + j + 1], 0.0)
        side[j + rows_dev * half] = mine
        side[j + rows_dev * (1 - half)] = theirs

    def run(count, second):
        chains = [(0, own // 2), (own // 2, count)]

        def factors(i, low, high):
            row = first_row + i * step_x
            total = power[0, row, low:high]
            for other in range(1, QUADS):
                total = total + power[other, row, low:high]
            level = total * (1.0 / (QUADS * quad_size))
            damping = whitecap_rate * level / (1.0 + level)
            den = base_ref[0, row, low:high] + jnp.concatenate([damping] * (width // LANES), axis=1)
            inverse = 1.0 / den
            source = wind_ref[0, row, low:high]
            if low == 0:
                source = jnp.concatenate([source[:HALO] + side[row, :HALO], source[HALO:]], axis=0)
            else:
                last = own - HALO - low
                parts = [source[:last], source[last:own - low] + side[row, HALO:]]
                if high > own:
                    parts.append(source[own - low:])
                source = jnp.concatenate(parts, axis=0)
            if i == 0 or i == rows - 1:
                here = jnp.where(row // rows_dev == half, 0, 1)
                source = source + rim[here, low:high]
            if second:
                before = state[quad, row]
                shifted = jnp.where(up_y, pltpu.roll(before, 1, 0), pltpu.roll(before, cells - 1, 0))
                source = source + ay_ref[0, row, low:high] * shifted[low:high]
            return ax_ref[0, row, low:high] * inverse, source * inverse

        ready = [factors(0, *chain) for chain in chains]
        upwind = [None] * len(chains)
        for i in range(rows):
            updated = []
            for (along, known), before in zip(ready, upwind):
                balance = known if before is None else along * before + known
                high, low = split_bf16(balance)
                updated.append(jnp.dot(jnp.concatenate([high, high, low], axis=1), mt_ref[0],
                                       preferred_element_type=jnp.float32))
            if i + 1 < rows:
                ready = [factors(i + 1, *chain) for chain in chains]
            row = first_row + i * step_x
            for (start, stop), value in zip(chains, updated):
                square = value * value
                folded = square[:, :LANES]
                for lane in range(LANES, width, LANES):
                    folded = folded + square[:, lane:lane + LANES]
                state[quad, row, start:stop] = value
                power[quad, row, start:stop] = jnp.broadcast_to(
                    jnp.sum(folded, axis=1, keepdims=True), (stop - start, LANES))
            upwind = updated

    @pl.when(turn < QUADS)
    def _():
        run(cells, False)

    @pl.when(turn >= QUADS)
    def _():
        run(own, True)

    @pl.when(turn == ITERS * QUADS - 1)
    def _():
        for pair in range(QUADS // 2):
            for j in range(rows_dev):
                for out_ref, side_at in ((keep_ref, half), (send_ref, 1 - half)):
                    row = rows_dev * side_at + j
                    both = jnp.concatenate(
                        [state[2 * pair, row, :own], state[2 * pair + 1, row, :own]], axis=0)
                    out_ref[pair, :, j, :] = both.T[:quad_size]


def merge_kernel(own, info, keep_ref, got_ref, out_ref):
    half = info[ITERS * QUADS]
    keep = keep_ref[0]
    got = got_ref[0]
    left = jnp.where(half == 0, keep, got)
    right = jnp.where(half == 0, got, keep)
    low = lax.broadcasted_iota(jnp.int32, keep.shape, 2) < own
    axis = keep.ndim - 1
    out_ref[0, 0] = jnp.where(low, left, pltpu.roll(right, own, axis))
    out_ref[0, 1] = jnp.where(low, pltpu.roll(left, own, axis), right)


def body(
    wind_speed,
    wind_dir,
    depth_class,
    group_speed,
    dissipation,
    input_rate,
    outer_spectra,
    dest_cell,
    refraction_inverse,
    sweep_order,
):
    rows_dev, cols_dev = wind_speed.shape
    row_count = lax.axis_size("rows")
    col_count = lax.axis_size("cols")
    assert row_count == 2
    devices = row_count * col_count
    rows = rows_dev * row_count
    own = cols_dev // 2
    cells = own + HALO
    class_count = group_speed.shape[0]
    comps = outer_spectra.shape[1]
    quad_size = refraction_inverse.shape[1]
    quarter = NDIR // QUADS
    width = -(-quad_size // LANES) * LANES
    axes = ("rows", "cols")
    half = lax.axis_index("rows")

    def device(row_at, col_at):
        return row_at * col_count + col_at

    span = range(col_count)
    swap_route = [(device(1 - h, c), device(h, c)) for h in range(2) for c in span]
    same_route = [(device(0, c - 1), device(0, c)) for c in span if c > 0]
    same_route += [(device(1, c + 1), device(1, c)) for c in span if c + 1 < col_count]
    cross_route = [(device(1, c - 1), device(0, c)) for c in span if c > 0]
    cross_route += [(device(0, c + 1), device(1, c)) for c in span if c + 1 < col_count]

    points = dest_cell.shape[0]
    load = -(-(comps + 1) // LANES) * LANES
    sizes = (cols_dev * col_count, rows_dev, cols_dev)
    shifts = tuple(size.bit_length() - 1 for size in sizes)
    assert all(size == 2**shift for size, shift in zip(sizes, shifts))
    slot_total = devices * CAP
    steps = 4
    outgoing = pl.pallas_call(
        lambda *refs: pack_kernel(shifts, col_count, rows, comps, *refs),
        grid=(steps,),
        in_specs=[pl.BlockSpec((1, points), lambda s: (0, 0)),
                  pl.BlockSpec((points, comps), lambda s: (0, 0))],
        out_specs=pl.BlockSpec((slot_total // steps, load), lambda s: (s, 0)),
        scratch_shapes=[pltpu.VMEM((points, load), jnp.bfloat16),
                        pltpu.VMEM((points, load), jnp.bfloat16),
                        pltpu.VMEM((1, points), jnp.int32)],
        out_shape=jax.ShapeDtypeStruct((slot_total, load), jnp.float32),
        compiler_params=pltpu.CompilerParams(
            dimension_semantics=("arbitrary",), vmem_limit_bytes=48 * 2**20),
    )(dest_cell.reshape(1, points), outer_spectra)
    held = jnp.stack([wind_speed, wind_dir, depth_class.astype(jnp.float32)])
    outgoing, held, refraction_inverse = lax.optimization_barrier(
        (outgoing, held, refraction_inverse))
    arrived = lax.all_to_all(outgoing.reshape(devices, CAP, load), axes, split_axis=0,
                             concat_axis=0, tiled=True).reshape(slot_total, load)

    partner = lax.ppermute(held, axes, swap_route)
    beside_same = lax.ppermute(held, axes, same_route)
    beside_cross = lax.ppermute(held, axes, cross_route)
    is_low = half == 0
    chip = jnp.concatenate(
        [jnp.where(is_low, held, partner), jnp.where(is_low, partner, held)], axis=1)
    near = jnp.concatenate(
        [jnp.where(is_low, beside_same, beside_cross), jnp.where(is_low, beside_cross, beside_same)],
        axis=1)
    mine = jnp.where(is_low, chip[:, :, :own], chip[:, :, own:])
    right = jnp.where(is_low, chip[:, :, own], near[:, :, 0])
    left = jnp.where(is_low, near[:, :, cols_dev - 1], chip[:, :, own - 1])
    grid = jnp.concatenate(
        [mine, right[:, :, None], jnp.zeros((3, rows, HALO - 2), jnp.float32), left[:, :, None]], axis=2)
    speed_here, dir_here, class_here = grid[0], grid[1], grid[2]
    strength = (speed_here * 0.1) ** 2
    cos_here, sin_here = jnp.cos(dir_here), jnp.sin(dir_here)

    angle = (jnp.arange(NDIR, dtype=jnp.float32) + 0.5) * (2.0 * math.pi / NDIR)
    cos_lane = pad_to(jnp.repeat(jnp.cos(angle), NFREQ).reshape(QUADS, quad_size), 1, width)
    sin_lane = pad_to(jnp.repeat(jnp.sin(angle), NFREQ).reshape(QUADS, quad_size), 1, width)
    rate_lane = pad_to(jnp.tile(input_rate, quarter), 0, width)
    speed_lane = pad_to(jnp.tile(group_speed, (1, quarter)), 1, width)
    loss_lane = pad_to(jnp.tile(dissipation, (1, quarter)), 1, width, 1.0)
    ax_table = jnp.abs(cos_lane)[:, None] * speed_lane[None]
    ay_table = jnp.abs(sin_lane)[:, None] * speed_lane[None]
    base_table = ax_table + ay_table + loss_lane[None]

    def by_class(table):
        chosen = jnp.broadcast_to(table[:, None, None, 0], (QUADS, rows, cells, width))
        for kind in range(1, class_count):
            chosen = jnp.where((class_here == kind)[None, :, :, None], table[:, None, None, kind], chosen)
        return chosen

    ax = by_class(ax_table)
    ay = by_class(ay_table)
    base = by_class(base_table)
    spread = jnp.maximum(
        cos_here[None, :, :, None] * cos_lane[:, None, None]
        + sin_here[None, :, :, None] * sin_lane[:, None, None], 0.0)
    wind = (rate_lane[None, None, None] * strength[None, :, :, None]) * (spread * spread)

    flipped = pad_to(pad_to(jnp.swapaxes(refraction_inverse, 1, 2), 1, width), 2, width)
    flip_high, flip_low = split_rounded(flipped)
    matrices = jnp.concatenate([flip_high, flip_low, flip_high], axis=1)

    arrived, ax, ay, base, wind, matrices = lax.optimization_barrier(
        (arrived, ax, ay, base, wind, matrices))

    info = jnp.concatenate([sweep_order.reshape(-1), half[None].astype(jnp.int32)])
    block = cells + rows_dev
    rim_shapes = [jax.ShapeDtypeStruct((QUADS, size, width), jnp.float32)
                  for size in (block, block, HALO, HALO)]
    rim_own, rim_send, out_same, out_cross = pl.pallas_call(
        lambda *refs: rim_kernel(own, rows_dev, comps, quad_size, *refs),
        grid_spec=pltpu.PrefetchScalarGridSpec(
            num_scalar_prefetch=1,
            grid=(1,),
            in_specs=[pl.BlockSpec((slot_total, load), lambda s, info: (0, 0))],
            out_specs=[pl.BlockSpec(shape.shape, lambda s, info: (0, 0, 0)) for shape in rim_shapes],
        ),
        out_shape=rim_shapes,
        compiler_params=pltpu.CompilerParams(vmem_limit_bytes=48 * 2**20),
    )(info, arrived)
    rim_partner = lax.ppermute(rim_send, axes, swap_route)
    rim_same = lax.ppermute(out_same, axes, same_route)
    rim_cross = lax.ppermute(out_cross, axes, cross_route)

    turns = ITERS * QUADS

    def quad_block(shape):
        zeros = (0,) * len(shape)
        return pl.BlockSpec((1,) + shape, lambda t, info: (info[t],) + zeros)

    packed = (QUADS // 2, quad_size, rows_dev, cols_dev)
    whole = pl.BlockSpec(packed, lambda t, info: (0, 0, 0, 0))
    keep, send = pl.pallas_call(
        lambda *refs: sweeps_kernel(rows, own, cells, quad_size, *refs),
        grid_spec=pltpu.PrefetchScalarGridSpec(
            num_scalar_prefetch=1,
            grid=(turns,),
            in_specs=[quad_block((rows, cells, width))] * 4
            + [quad_block((3 * width, width))]
            + [quad_block((block, width))] * 2
            + [quad_block((HALO, width))] * 2,
            out_specs=[whole, whole],
            scratch_shapes=[
                pltpu.VMEM((QUADS, rows, cells, width), jnp.float32),
                pltpu.VMEM((QUADS, rows, cells, LANES), jnp.float32),
                pltpu.VMEM((2, cells, width), jnp.float32),
                pltpu.VMEM((rows, 2 * HALO, width), jnp.float32),
            ],
        ),
        out_shape=[jax.ShapeDtypeStruct(packed, jnp.float32)] * 2,
        compiler_params=pltpu.CompilerParams(
            dimension_semantics=("arbitrary",), vmem_limit_bytes=44 * 2**20),
    )(info, ax, ay, base, wind, matrices, rim_own, rim_partner, rim_same, rim_cross)

    got = lax.ppermute(send, axes, swap_route)
    chunks = 4
    part = quad_size // chunks
    half_block = pl.BlockSpec((1, part, rows_dev, cols_dev), lambda p, c, info: (p, c, 0, 0))
    merged = pl.pallas_call(
        lambda *refs: merge_kernel(own, *refs),
        grid_spec=pltpu.PrefetchScalarGridSpec(
            num_scalar_prefetch=1,
            grid=(QUADS // 2, chunks),
            in_specs=[half_block, half_block],
            out_specs=pl.BlockSpec(
                (1, 2, part, rows_dev, cols_dev), lambda p, c, info: (p, 0, c, 0, 0)),
        ),
        out_shape=jax.ShapeDtypeStruct((QUADS // 2, 2, quad_size, rows_dev, cols_dev), jnp.float32),
        compiler_params=pltpu.CompilerParams(vmem_limit_bytes=16 * 2**20),
    )(info, keep, got)
    return merged.reshape(comps, rows_dev, cols_dev)


def solution(mesh):
    placed = (
        P("rows", "cols"),
        P("rows", "cols"),
        P("rows", "cols"),
        P(),
        P(),
        P(),
        P(("rows", "cols"), None),
        P(("rows", "cols")),
        P(),
        P(),
    )
    return jax.shard_map(
        body, mesh=mesh, in_specs=placed, out_specs=P(None, "rows", "cols"), check_vma=False
    )
```

```python
from functools import partial
import math

import jax
import jax.numpy as jnp
import numpy as np
from jax import lax
from jax.experimental import pallas as pl
from jax.experimental.pallas import tpu as pltpu
from jax.sharding import PartitionSpec as P

NDIR = 36
NFREQ = 24
CAP = 16
ITERS = 2
QUADS = 4
LANES = 128
HALO = 8

whitecap_rate = 0.5


def split_bf16(value):
    high = value.astype(jnp.bfloat16)
    low = (value - high.astype(jnp.float32)).astype(jnp.bfloat16)
    return high, low


def split_rounded(value):
    rounded = lax.reduce_precision(value, 8, 7)
    return rounded.astype(jnp.bfloat16), (value - rounded).astype(jnp.bfloat16)


def pad_to(array, axis, size, value=0.0):
    widths = [(0, 0)] * array.ndim
    widths[axis] = (0, size - array.shape[axis])
    return jnp.pad(array, widths, constant_values=value)


def pack_kernel(shifts, col_count, rows, comps, dest_ref, spectra_ref, out_ref, high, low, slots):
    step = pl.program_id(0)
    points = dest_ref.shape[1]
    load = out_ref.shape[1]
    total_bits, row_bits, col_bits = shifts

    @pl.when(step == 0)
    def _():
        dest = dest_ref[...]
        grid_row = lax.shift_right_logical(dest, total_bits)
        grid_col = dest & (2**total_bits - 1)
        local_row = grid_row & (2**row_bits - 1)
        local_col = grid_col & (2**col_bits - 1)
        owner = (lax.shift_right_logical(grid_row, row_bits) * col_count
                 + lax.shift_right_logical(grid_col, col_bits))
        on_row = (grid_row == 0) | (grid_row == rows - 1)
        on_left = jnp.where(grid_col == 0, 2**col_bits, 2**col_bits + 2**row_bits) + local_row
        code = jnp.where(on_row, local_col, on_left) + 1
        lanes = jnp.concatenate(
            [owner.astype(jnp.float32), code.astype(jnp.float32), jnp.zeros((6, points), jnp.float32)],
            axis=0)
        columns = lanes.T
        same = columns[:, 0:1] == lanes[0:1]
        above = (lax.broadcasted_iota(jnp.int32, (points, points), 0)
                 < lax.broadcasted_iota(jnp.int32, (points, points), 1))
        rank = jnp.sum(jnp.where(same & above, 1.0, 0.0), axis=0, keepdims=True)
        slots[...] = owner * CAP + rank.astype(jnp.int32)
        spectra = jnp.concatenate(
            [spectra_ref[...], jnp.broadcast_to(columns[:, 1:2], (points, load - comps))], axis=1)
        high[...], low[...] = split_bf16(spectra)

    place = jnp.where(
        lax.broadcasted_iota(jnp.int32, (out_ref.shape[0], points), 0) + step * out_ref.shape[0]
        == slots[...], 1.0, 0.0).astype(jnp.bfloat16)
    out_ref[...] = (jnp.dot(place, high[...], preferred_element_type=jnp.float32)
                    + jnp.dot(place, low[...], preferred_element_type=jnp.float32))


def rim_kernel(own, rows_dev, comps, quad_size, info, arrived_ref, own_ref, send_ref, same_ref,
               cross_ref):
    half = info[ITERS * QUADS]
    cols_dev = 2 * own
    cells = own + HALO
    block = cells + rows_dev
    width = own_ref.shape[2]
    load = arrived_ref.shape[1]
    spots = -(-(2 * block + 2 * HALO) // LANES) * LANES
    lane = lax.broadcasted_iota(jnp.int32, (1, spots), 1)
    at_send = lane >= block
    spot = jnp.where(at_send, lane - block, lane)
    side_at = jnp.where(at_send, 1 - half, half)
    want = jnp.where(spot < own, own * side_at + spot, -1)
    want = jnp.where((spot == own) & (side_at == 0), own, want)
    want = jnp.where((spot == cells - 1) & (side_at == 1), own - 1, want)
    want = jnp.where(spot >= cells, cols_dev + rows_dev * side_at + spot - cells, want)
    rest = lane - 2 * block
    to_left = jnp.where((rest == HALO - 1) & (half == 0), cols_dev - 1, -1)
    to_left = jnp.where((rest == 0) & (half == 1), 0, to_left)
    to_left = jnp.where((rest == HALO) & (half == 0), 0, to_left)
    to_left = jnp.where((rest == 2 * HALO - 1) & (half == 1), cols_dev - 1, to_left)
    want = jnp.where(rest >= 0, to_left, want)
    code = arrived_ref[:, comps:comps + 1]
    gather = jnp.where(code == (want + 1).astype(jnp.float32), 1.0, 0.0)
    gather = jnp.where(want >= 0, gather, 0.0).astype(jnp.bfloat16)
    high, low = split_bf16(arrived_ref[...])
    over_points = (((0,), (0,)), ((), ()))
    summed = (lax.dot_general(gather, high, over_points, preferred_element_type=jnp.float32)
              + lax.dot_general(gather, low, over_points, preferred_element_type=jnp.float32))
    for quad in range(QUADS):
        start = quad * quad_size
        part = summed if quad == 0 else pltpu.roll(summed, load - start, 1)
        own_ref[quad] = part[:block, :width]
        send_ref[quad] = part[block:2 * block, :width]
        same_ref[quad] = part[2 * block:2 * block + HALO, :width]
        cross_ref[quad] = part[2 * block + HALO:2 * block + 2 * HALO, :width]


def sweeps_kernel(rows, own, cells, quad_size, info, ax_ref, ay_ref, base_ref, wind_ref, mt_ref,
                  own_ref, par_ref, same_ref, cross_ref, keep_ref, send_ref,
                  state, power, rim, side):
    turn = pl.program_id(0)
    quad = info[turn]
    half = info[ITERS * QUADS]
    width = mt_ref.shape[3]
    rows_dev = rows // 2
    down = (quad == 0) | (quad == 3)
    step_x = jnp.where(down, 1, -1)
    first_row = jnp.where(down, 0, rows - 1)
    up_y = quad < 2

    @pl.when(turn == 0)
    def _():
        power[...] = jnp.zeros_like(power)

    rim[0] = own_ref[0, 0:cells]
    rim[0, own:cells] = own_ref[0, own:cells] + same_ref[0]
    rim[1] = par_ref[0, 0:cells]
    rim[1, own:cells] = par_ref[0, own:cells] + cross_ref[0]
    edge_at = jnp.where(half == 0, 0, 2 * HALO - 1)
    at_edge = lax.broadcasted_iota(jnp.int32, (2 * HALO, width), 0) == edge_at
    for j in range(rows_dev):
        mine = jnp.where(at_edge, own_ref[0, cells + j:cells + j + 1], 0.0)
        theirs = jnp.where(at_edge, par_ref[0, cells + j:cells + j + 1], 0.0)
        side[j + rows_dev * half] = mine
        side[j + rows_dev * (1 - half)] = theirs

    def run(count, second):
        chains = [(0, count)]

        def factors(i, low, high):
            row = first_row + i * step_x
            total = power[0, row, low:high]
            for other in range(1, QUADS):
                total = total + power[other, row, low:high]
            level = total * (1.0 / (QUADS * quad_size))
            damping = whitecap_rate * level / (1.0 + level)
            den = base_ref[0, row, low:high] + jnp.concatenate([damping] * (width // LANES), axis=1)
            inverse = 1.0 / den
            source = wind_ref[0, row, low:high]
            edge = side[row]
            parts = [source[:HALO] + edge[:HALO], source[HALO:own - HALO],
                     source[own - HALO:own] + edge[HALO:]]
            if high > own:
                parts.append(source[own:])
            source = jnp.concatenate(parts, axis=0)
            if i == 0 or i == rows - 1:
                here = jnp.where(row // rows_dev == half, 0, 1)
                source = source + rim[here, low:high]
            if second:
                before = state[quad, row]
                shifted = jnp.where(up_y, pltpu.roll(before, 1, 0), pltpu.roll(before, cells - 1, 0))
                source = source + ay_ref[0, row, low:high] * shifted[low:high]
            return ax_ref[0, row, low:high] * inverse, source * inverse

        ready = [factors(0, *chain) for chain in chains]
        upwind = [None] * len(chains)
        for i in range(rows):
            updated = []
            for (along, known), before in zip(ready, upwind):
                balance = known if before is None else along * before + known
                high, low = split_bf16(balance)
                product = partial(jnp.dot, preferred_element_type=jnp.float32)
                fine = product(high, mt_ref[0, 1]) + product(low, mt_ref[0, 0])
                updated.append(product(high, mt_ref[0, 0]) + fine)
            if i + 1 < rows:
                ready = [factors(i + 1, *chain) for chain in chains]
            row = first_row + i * step_x
            for (start, stop), value in zip(chains, updated):
                square = value * value
                folded = square[:, :LANES]
                for lane in range(LANES, width, LANES):
                    folded = folded + square[:, lane:lane + LANES]
                state[quad, row, start:stop] = value
                power[quad, row, start:stop] = jnp.broadcast_to(
                    jnp.sum(folded, axis=1, keepdims=True), (stop - start, LANES))
            upwind = updated

    @pl.when(turn < QUADS)
    def _():
        run(cells, False)

    @pl.when(turn >= QUADS)
    def _():
        run(own, True)

    @pl.when(turn == ITERS * QUADS - 1)
    def _():
        for pair in range(QUADS // 2):
            for j in range(rows_dev):
                for out_ref, side_at in ((keep_ref, half), (send_ref, 1 - half)):
                    row = rows_dev * side_at + j
                    both = jnp.concatenate(
                        [state[2 * pair, row, :own], state[2 * pair + 1, row, :own]], axis=0)
                    out_ref[pair, :, j, :] = both.T[:quad_size]


def merge_kernel(own, info, keep_ref, got_ref, out_ref):
    half = info[ITERS * QUADS]
    keep = keep_ref[0]
    got = got_ref[0]
    left = jnp.where(half == 0, keep, got)
    right = jnp.where(half == 0, got, keep)
    low = lax.broadcasted_iota(jnp.int32, keep.shape, 2) < own
    axis = keep.ndim - 1
    out_ref[0, 0] = jnp.where(low, left, pltpu.roll(right, own, axis))
    out_ref[0, 1] = jnp.where(low, pltpu.roll(left, own, axis), right)


def body(
    wind_speed,
    wind_dir,
    depth_class,
    group_speed,
    dissipation,
    input_rate,
    outer_spectra,
    dest_cell,
    refraction_inverse,
    sweep_order,
):
    rows_dev, cols_dev = wind_speed.shape
    row_count = lax.axis_size("rows")
    col_count = lax.axis_size("cols")
    assert row_count == 2
    devices = row_count * col_count
    rows = rows_dev * row_count
    own = cols_dev // 2
    cells = own + HALO
    class_count = group_speed.shape[0]
    comps = outer_spectra.shape[1]
    quad_size = refraction_inverse.shape[1]
    quarter = NDIR // QUADS
    width = -(-quad_size // LANES) * LANES
    axes = ("rows", "cols")
    half = lax.axis_index("rows")

    def device(row_at, col_at):
        return row_at * col_count + col_at

    span = range(col_count)
    swap_route = [(device(1 - h, c), device(h, c)) for h in range(2) for c in span]
    same_route = [(device(0, c - 1), device(0, c)) for c in span if c > 0]
    same_route += [(device(1, c + 1), device(1, c)) for c in span if c + 1 < col_count]
    cross_route = [(device(1, c - 1), device(0, c)) for c in span if c > 0]
    cross_route += [(device(0, c + 1), device(1, c)) for c in span if c + 1 < col_count]

    points = dest_cell.shape[0]
    load = -(-(comps + 1) // LANES) * LANES
    sizes = (cols_dev * col_count, rows_dev, cols_dev)
    shifts = tuple(size.bit_length() - 1 for size in sizes)
    assert all(size == 2**shift for size, shift in zip(sizes, shifts))
    slot_total = devices * CAP
    steps = 4
    outgoing = pl.pallas_call(
        lambda *refs: pack_kernel(shifts, col_count, rows, comps, *refs),
        grid=(steps,),
        in_specs=[pl.BlockSpec((1, points), lambda s: (0, 0)),
                  pl.BlockSpec((points, comps), lambda s: (0, 0))],
        out_specs=pl.BlockSpec((slot_total // steps, load), lambda s: (s, 0)),
        scratch_shapes=[pltpu.VMEM((points, load), jnp.bfloat16),
                        pltpu.VMEM((points, load), jnp.bfloat16),
                        pltpu.VMEM((1, points), jnp.int32)],
        out_shape=jax.ShapeDtypeStruct((slot_total, load), jnp.float32),
        compiler_params=pltpu.CompilerParams(
            dimension_semantics=("arbitrary",), vmem_limit_bytes=48 * 2**20),
    )(dest_cell.reshape(1, points), outer_spectra)
    outgoing, refraction_inverse = lax.optimization_barrier((outgoing, refraction_inverse))
    flipped = pad_to(pad_to(jnp.swapaxes(refraction_inverse, 1, 2), 1, width), 2, width)
    flip_high, flip_low = split_rounded(flipped)
    matrices = jnp.stack([flip_high, flip_low], axis=1)
    held = jnp.stack([wind_speed, wind_dir, depth_class.astype(jnp.float32)])
    held, matrices = lax.optimization_barrier((held, matrices))
    arrived = lax.all_to_all(outgoing.reshape(devices, CAP, load), axes, split_axis=0,
                             concat_axis=0, tiled=True).reshape(slot_total, load)

    partner = lax.ppermute(held, axes, swap_route)
    beside_same = lax.ppermute(held, axes, same_route)
    beside_cross = lax.ppermute(held, axes, cross_route)
    is_low = half == 0
    chip = jnp.concatenate(
        [jnp.where(is_low, held, partner), jnp.where(is_low, partner, held)], axis=1)
    near = jnp.concatenate(
        [jnp.where(is_low, beside_same, beside_cross), jnp.where(is_low, beside_cross, beside_same)],
        axis=1)
    mine = jnp.where(is_low, chip[:, :, :own], chip[:, :, own:])
    right = jnp.where(is_low, chip[:, :, own], near[:, :, 0])
    left = jnp.where(is_low, near[:, :, cols_dev - 1], chip[:, :, own - 1])
    grid = jnp.concatenate(
        [mine, right[:, :, None], jnp.zeros((3, rows, HALO - 2), jnp.float32), left[:, :, None]], axis=2)
    speed_here, dir_here, class_here = grid[0], grid[1], grid[2]
    strength = (speed_here * 0.1) ** 2
    cos_here, sin_here = jnp.cos(dir_here), jnp.sin(dir_here)

    angle = (jnp.arange(NDIR, dtype=jnp.float32) + 0.5) * (2.0 * math.pi / NDIR)
    cos_lane = pad_to(jnp.repeat(jnp.cos(angle), NFREQ).reshape(QUADS, quad_size), 1, width)
    sin_lane = pad_to(jnp.repeat(jnp.sin(angle), NFREQ).reshape(QUADS, quad_size), 1, width)
    rate_lane = pad_to(jnp.tile(input_rate, quarter), 0, width)
    speed_lane = pad_to(jnp.tile(group_speed, (1, quarter)), 1, width)
    loss_lane = pad_to(jnp.tile(dissipation, (1, quarter)), 1, width, 1.0)
    ax_table = jnp.abs(cos_lane)[:, None] * speed_lane[None]
    ay_table = jnp.abs(sin_lane)[:, None] * speed_lane[None]
    base_table = ax_table + ay_table + loss_lane[None]

    def by_class(table):
        chosen = jnp.broadcast_to(table[:, None, None, 0], (QUADS, rows, cells, width))
        for kind in range(1, class_count):
            chosen = jnp.where((class_here == kind)[None, :, :, None], table[:, None, None, kind], chosen)
        return chosen

    ax = by_class(ax_table)
    ay = by_class(ay_table)
    base = by_class(base_table)
    spread = jnp.maximum(
        cos_here[None, :, :, None] * cos_lane[:, None, None]
        + sin_here[None, :, :, None] * sin_lane[:, None, None], 0.0)
    wind = (rate_lane[None, None, None] * strength[None, :, :, None]) * (spread * spread)

    arrived, ax, ay, base, wind, matrices = lax.optimization_barrier(
        (arrived, ax, ay, base, wind, matrices))

    info = jnp.concatenate([sweep_order.reshape(-1), half[None].astype(jnp.int32)])
    block = cells + rows_dev
    rim_shapes = [jax.ShapeDtypeStruct((QUADS, size, width), jnp.float32)
                  for size in (block, block, HALO, HALO)]
    rim_own, rim_send, out_same, out_cross = pl.pallas_call(
        lambda *refs: rim_kernel(own, rows_dev, comps, quad_size, *refs),
        grid_spec=pltpu.PrefetchScalarGridSpec(
            num_scalar_prefetch=1,
            grid=(1,),
            in_specs=[pl.BlockSpec((slot_total, load), lambda s, info: (0, 0))],
            out_specs=[pl.BlockSpec(shape.shape, lambda s, info: (0, 0, 0)) for shape in rim_shapes],
        ),
        out_shape=rim_shapes,
        compiler_params=pltpu.CompilerParams(vmem_limit_bytes=48 * 2**20),
    )(info, arrived)
    rim_partner = lax.ppermute(rim_send, axes, swap_route)
    rim_same = lax.ppermute(out_same, axes, same_route)
    rim_cross = lax.ppermute(out_cross, axes, cross_route)

    turns = ITERS * QUADS

    def quad_block(shape):
        zeros = (0,) * len(shape)
        return pl.BlockSpec((1,) + shape, lambda t, info: (info[t],) + zeros)

    packed = (QUADS // 2, quad_size, rows_dev, cols_dev)
    whole = pl.BlockSpec(packed, lambda t, info: (0, 0, 0, 0))
    keep, send = pl.pallas_call(
        lambda *refs: sweeps_kernel(rows, own, cells, quad_size, *refs),
        grid_spec=pltpu.PrefetchScalarGridSpec(
            num_scalar_prefetch=1,
            grid=(turns,),
            in_specs=[quad_block((rows, cells, width))] * 4
            + [quad_block((2, width, width))]
            + [quad_block((block, width))] * 2
            + [quad_block((HALO, width))] * 2,
            out_specs=[whole, whole],
            scratch_shapes=[
                pltpu.VMEM((QUADS, rows, cells, width), jnp.float32),
                pltpu.VMEM((QUADS, rows, cells, LANES), jnp.float32),
                pltpu.VMEM((2, cells, width), jnp.float32),
                pltpu.VMEM((rows, 2 * HALO, width), jnp.float32),
            ],
        ),
        out_shape=[jax.ShapeDtypeStruct(packed, jnp.float32)] * 2,
        compiler_params=pltpu.CompilerParams(
            dimension_semantics=("arbitrary",), vmem_limit_bytes=44 * 2**20),
    )(info, ax, ay, base, wind, matrices, rim_own, rim_partner, rim_same, rim_cross)

    got = lax.ppermute(send, axes, swap_route)
    chunks = 4
    part = quad_size // chunks
    half_block = pl.BlockSpec((1, part, rows_dev, cols_dev), lambda p, c, info: (p, c, 0, 0))
    merged = pl.pallas_call(
        lambda *refs: merge_kernel(own, *refs),
        grid_spec=pltpu.PrefetchScalarGridSpec(
            num_scalar_prefetch=1,
            grid=(QUADS // 2, chunks),
            in_specs=[half_block, half_block],
            out_specs=pl.BlockSpec(
                (1, 2, part, rows_dev, cols_dev), lambda p, c, info: (p, 0, c, 0, 0)),
        ),
        out_shape=jax.ShapeDtypeStruct((QUADS // 2, 2, quad_size, rows_dev, cols_dev), jnp.float32),
        compiler_params=pltpu.CompilerParams(vmem_limit_bytes=16 * 2**20),
    )(info, keep, got)
    return merged.reshape(comps, rows_dev, cols_dev)


def solution(mesh):
    placed = (
        P("rows", "cols"),
        P("rows", "cols"),
        P("rows", "cols"),
        P(),
        P(),
        P(),
        P(("rows", "cols"), None),
        P(("rows", "cols")),
        P(),
        P(),
    )
    return jax.shard_map(
        body, mesh=mesh, in_specs=placed, out_specs=P(None, "rows", "cols"), check_vma=False
    )
```

```python
from functools import partial
import math

import jax
import jax.numpy as jnp
import numpy as np
from jax import lax
from jax.experimental import pallas as pl
from jax.experimental.pallas import tpu as pltpu
from jax.sharding import PartitionSpec as P

NDIR = 36
NFREQ = 24
CAP = 16
ITERS = 2
QUADS = 4
LANES = 128
HALO = 8

whitecap_rate = 0.5


def split_bf16(value):
    high = value.astype(jnp.bfloat16)
    low = (value - high.astype(jnp.float32)).astype(jnp.bfloat16)
    return high, low


def split_rounded(value):
    rounded = lax.reduce_precision(value, 8, 7)
    return rounded.astype(jnp.bfloat16), (value - rounded).astype(jnp.bfloat16)


def pad_to(array, axis, size, value=0.0):
    widths = [(0, 0)] * array.ndim
    widths[axis] = (0, size - array.shape[axis])
    return jnp.pad(array, widths, constant_values=value)


def pack_kernel(shifts, col_count, rows, comps, dest_ref, spectra_ref, out_ref, high, low, slots):
    step = pl.program_id(0)
    points = dest_ref.shape[1]
    load = out_ref.shape[1]
    total_bits, row_bits, col_bits = shifts

    @pl.when(step == 0)
    def _():
        dest = dest_ref[...]
        grid_row = lax.shift_right_logical(dest, total_bits)
        grid_col = dest & (2**total_bits - 1)
        local_row = grid_row & (2**row_bits - 1)
        local_col = grid_col & (2**col_bits - 1)
        owner = (lax.shift_right_logical(grid_row, row_bits) * col_count
                 + lax.shift_right_logical(grid_col, col_bits))
        on_row = (grid_row == 0) | (grid_row == rows - 1)
        on_left = jnp.where(grid_col == 0, 2**col_bits, 2**col_bits + 2**row_bits) + local_row
        code = jnp.where(on_row, local_col, on_left) + 1
        lanes = jnp.concatenate(
            [owner.astype(jnp.float32), code.astype(jnp.float32), jnp.zeros((6, points), jnp.float32)],
            axis=0)
        columns = lanes.T
        same = columns[:, 0:1] == lanes[0:1]
        above = (lax.broadcasted_iota(jnp.int32, (points, points), 0)
                 < lax.broadcasted_iota(jnp.int32, (points, points), 1))
        rank = jnp.sum(jnp.where(same & above, 1.0, 0.0), axis=0, keepdims=True)
        slots[...] = owner * CAP + rank.astype(jnp.int32)
        spectra = jnp.concatenate(
            [spectra_ref[...], jnp.broadcast_to(lanes[1:2], (load - comps, points))], axis=0)
        high[...], low[...] = split_bf16(spectra)

    place = jnp.where(
        lax.broadcasted_iota(jnp.int32, (out_ref.shape[0], points), 0) + step * out_ref.shape[0]
        == slots[...], 1.0, 0.0).astype(jnp.bfloat16)
    over_points = (((1,), (1,)), ((), ()))
    out_ref[...] = (lax.dot_general(place, high[...], over_points, preferred_element_type=jnp.float32)
                    + lax.dot_general(place, low[...], over_points, preferred_element_type=jnp.float32))


def rim_kernel(own, rows_dev, comps, quad_size, info, arrived_ref, own_ref, send_ref, same_ref,
               cross_ref):
    half = info[ITERS * QUADS]
    cols_dev = 2 * own
    cells = own + HALO
    block = cells + rows_dev
    width = own_ref.shape[2]
    load = arrived_ref.shape[1]
    spots = -(-(2 * block + 2 * HALO) // LANES) * LANES
    lane = lax.broadcasted_iota(jnp.int32, (1, spots), 1)
    at_send = lane >= block
    spot = jnp.where(at_send, lane - block, lane)
    side_at = jnp.where(at_send, 1 - half, half)
    want = jnp.where(spot < own, own * side_at + spot, -1)
    want = jnp.where((spot == own) & (side_at == 0), own, want)
    want = jnp.where((spot == cells - 1) & (side_at == 1), own - 1, want)
    want = jnp.where(spot >= cells, cols_dev + rows_dev * side_at + spot - cells, want)
    rest = lane - 2 * block
    to_left = jnp.where((rest == HALO - 1) & (half == 0), cols_dev - 1, -1)
    to_left = jnp.where((rest == 0) & (half == 1), 0, to_left)
    to_left = jnp.where((rest == HALO) & (half == 0), 0, to_left)
    to_left = jnp.where((rest == 2 * HALO - 1) & (half == 1), cols_dev - 1, to_left)
    want = jnp.where(rest >= 0, to_left, want)
    code = arrived_ref[:, comps:comps + 1]
    gather = jnp.where(code == (want + 1).astype(jnp.float32), 1.0, 0.0)
    gather = jnp.where(want >= 0, gather, 0.0).astype(jnp.bfloat16)
    high, low = split_bf16(arrived_ref[...])
    over_points = (((0,), (0,)), ((), ()))
    summed = (lax.dot_general(gather, high, over_points, preferred_element_type=jnp.float32)
              + lax.dot_general(gather, low, over_points, preferred_element_type=jnp.float32))
    for quad in range(QUADS):
        start = quad * quad_size
        part = summed if quad == 0 else pltpu.roll(summed, load - start, 1)
        own_ref[quad] = part[:block, :width]
        send_ref[quad] = part[block:2 * block, :width]
        same_ref[quad] = part[2 * block:2 * block + HALO, :width]
        cross_ref[quad] = part[2 * block + HALO:2 * block + 2 * HALO, :width]


def sweeps_kernel(rows, own, cells, quad_size, info, ax_ref, ay_ref, base_ref, wind_ref, mt_ref,
                  own_ref, par_ref, same_ref, cross_ref, keep_ref, send_ref,
                  state, power, rim, side):
    turn = pl.program_id(0)
    quad = info[turn]
    half = info[ITERS * QUADS]
    width = mt_ref.shape[3]
    rows_dev = rows // 2
    down = (quad == 0) | (quad == 3)
    step_x = jnp.where(down, 1, -1)
    first_row = jnp.where(down, 0, rows - 1)
    up_y = quad < 2

    @pl.when(turn == 0)
    def _():
        power[...] = jnp.zeros_like(power)

    rim[0] = own_ref[0, 0:cells]
    rim[0, own:cells] = own_ref[0, own:cells] + same_ref[0]
    rim[1] = par_ref[0, 0:cells]
    rim[1, own:cells] = par_ref[0, own:cells] + cross_ref[0]
    edge_at = jnp.where(half == 0, 0, 2 * HALO - 1)
    at_edge = lax.broadcasted_iota(jnp.int32, (2 * HALO, width), 0) == edge_at
    for j in range(rows_dev):
        mine = jnp.where(at_edge, own_ref[0, cells + j:cells + j + 1], 0.0)
        theirs = jnp.where(at_edge, par_ref[0, cells + j:cells + j + 1], 0.0)
        side[j + rows_dev * half] = mine
        side[j + rows_dev * (1 - half)] = theirs

    def run(count, second):
        def factors(i, at_rim):
            row = first_row + i * step_x
            total = power[0, row, :count]
            for other in range(1, QUADS):
                total = total + power[other, row, :count]
            level = total * (1.0 / (QUADS * quad_size))
            damping = whitecap_rate * level / (1.0 + level)
            den = base_ref[0, row, :count] + jnp.concatenate([damping] * (width // LANES), axis=1)
            inverse = 1.0 / den
            source = wind_ref[0, row, :count]
            edge = side[row]
            parts = [source[:HALO] + edge[:HALO], source[HALO:own - HALO],
                     source[own - HALO:own] + edge[HALO:]]
            if count > own:
                parts.append(source[own:])
            source = jnp.concatenate(parts, axis=0)
            if at_rim:
                here = jnp.where(row // rows_dev == half, 0, 1)
                source = source + rim[here, :count]
            if second:
                before = state[quad, row]
                shifted = jnp.where(up_y, pltpu.roll(before, 1, 0), pltpu.roll(before, cells - 1, 0))
                source = source + ay_ref[0, row, :count] * shifted[:count]
            return ax_ref[0, row, :count] * inverse, source * inverse

        def times_matrix(balance):
            high, low = split_bf16(balance)
            product = partial(jnp.dot, preferred_element_type=jnp.float32)
            fine = product(high, mt_ref[0, 1]) + product(low, mt_ref[0, 0])
            return product(high, mt_ref[0, 0]) + fine

        def store(i, value):
            row = first_row + i * step_x
            square = value * value
            folded = square[:, :LANES]
            for lane in range(LANES, width, LANES):
                folded = folded + square[:, lane:lane + LANES]
            state[quad, row, :count] = value
            power[quad, row, :count] = jnp.broadcast_to(
                jnp.sum(folded, axis=1, keepdims=True), (count, LANES))

        def step(i, carry):
            along, known, before = carry
            value = times_matrix(along * before + known)
            along, known = factors(i + 1, False)
            store(i - 1, before)
            return along, known, value

        first = times_matrix(factors(0, True)[1])
        along, known, before = lax.fori_loop(1, rows - 2, step, (*factors(1, False), first))
        value = times_matrix(along * before + known)
        along, known = factors(rows - 1, True)
        store(rows - 3, before)
        last = times_matrix(along * value + known)
        store(rows - 2, value)
        store(rows - 1, last)

    @pl.when(turn < QUADS)
    def _():
        run(cells, False)

    @pl.when(turn >= QUADS)
    def _():
        run(own, True)

    @pl.when(turn == ITERS * QUADS - 1)
    def _():
        for pair in range(QUADS // 2):
            for j in range(rows_dev):
                for out_ref, side_at in ((keep_ref, half), (send_ref, 1 - half)):
                    row = rows_dev * side_at + j
                    both = jnp.concatenate(
                        [state[2 * pair, row, :own], state[2 * pair + 1, row, :own]], axis=0)
                    out_ref[pair, :, j, :] = both.T[:quad_size]


def merge_kernel(own, info, keep_ref, got_ref, out_ref):
    half = info[ITERS * QUADS]
    keep = keep_ref[0]
    got = got_ref[0]
    left = jnp.where(half == 0, keep, got)
    right = jnp.where(half == 0, got, keep)
    low = lax.broadcasted_iota(jnp.int32, keep.shape, 2) < own
    axis = keep.ndim - 1
    out_ref[0, 0] = jnp.where(low, left, pltpu.roll(right, own, axis))
    out_ref[0, 1] = jnp.where(low, pltpu.roll(left, own, axis), right)


def body(
    wind_speed,
    wind_dir,
    depth_class,
    group_speed,
    dissipation,
    input_rate,
    outer_spectra,
    dest_cell,
    refraction_inverse,
    sweep_order,
):
    rows_dev, cols_dev = wind_speed.shape
    row_count = lax.axis_size("rows")
    col_count = lax.axis_size("cols")
    assert row_count == 2
    devices = row_count * col_count
    rows = rows_dev * row_count
    own = cols_dev // 2
    cells = own + HALO
    class_count = group_speed.shape[0]
    comps = outer_spectra.shape[1]
    quad_size = refraction_inverse.shape[1]
    quarter = NDIR // QUADS
    width = -(-quad_size // LANES) * LANES
    axes = ("rows", "cols")
    half = lax.axis_index("rows")

    def device(row_at, col_at):
        return row_at * col_count + col_at

    span = range(col_count)
    swap_route = [(device(1 - h, c), device(h, c)) for h in range(2) for c in span]
    same_route = [(device(0, c - 1), device(0, c)) for c in span if c > 0]
    same_route += [(device(1, c + 1), device(1, c)) for c in span if c + 1 < col_count]
    cross_route = [(device(1, c - 1), device(0, c)) for c in span if c > 0]
    cross_route += [(device(0, c + 1), device(1, c)) for c in span if c + 1 < col_count]

    points = dest_cell.shape[0]
    load = -(-(comps + 1) // LANES) * LANES
    sizes = (cols_dev * col_count, rows_dev, cols_dev)
    shifts = tuple(size.bit_length() - 1 for size in sizes)
    assert all(size == 2**shift for size, shift in zip(sizes, shifts))
    slot_total = devices * CAP
    steps = 4
    outgoing = pl.pallas_call(
        lambda *refs: pack_kernel(shifts, col_count, rows, comps, *refs),
        grid=(steps,),
        in_specs=[pl.BlockSpec((1, points), lambda s: (0, 0)),
                  pl.BlockSpec((comps, points), lambda s: (0, 0))],
        out_specs=pl.BlockSpec((slot_total // steps, load), lambda s: (s, 0)),
        scratch_shapes=[pltpu.VMEM((load, points), jnp.bfloat16),
                        pltpu.VMEM((load, points), jnp.bfloat16),
                        pltpu.VMEM((1, points), jnp.int32)],
        out_shape=jax.ShapeDtypeStruct((slot_total, load), jnp.float32),
        compiler_params=pltpu.CompilerParams(
            dimension_semantics=("arbitrary",), vmem_limit_bytes=48 * 2**20),
    )(dest_cell.reshape(1, points), outer_spectra.T)
    outgoing, refraction_inverse = lax.optimization_barrier((outgoing, refraction_inverse))
    flipped = pad_to(pad_to(jnp.swapaxes(refraction_inverse, 1, 2), 1, width), 2, width)
    flip_high, flip_low = split_rounded(flipped)
    matrices = jnp.stack([flip_high, flip_low], axis=1)
    held = jnp.stack([wind_speed, wind_dir, depth_class.astype(jnp.float32)])
    arrived = lax.all_to_all(outgoing.reshape(devices, CAP, load), axes, split_axis=0,
                             concat_axis=0, tiled=True).reshape(slot_total, load)

    everywhere = lax.all_gather(held, axes).reshape((row_count, col_count) + held.shape)
    is_low = half == 0
    col_at = lax.axis_index("cols")
    near_at = jnp.where(is_low, col_at - 1, col_at + 1)
    inside = (near_at >= 0) & (near_at < col_count)

    def chip_at(index):
        both = lax.dynamic_index_in_dim(everywhere, index, axis=1, keepdims=False)
        return jnp.concatenate([both[0], both[1]], axis=1)

    chip = chip_at(col_at)
    near = jnp.where(inside, chip_at(jnp.clip(near_at, 0, col_count - 1)), 0.0)
    mine = jnp.where(is_low, chip[:, :, :own], chip[:, :, own:])
    right = jnp.where(is_low, chip[:, :, own], near[:, :, 0])
    left = jnp.where(is_low, near[:, :, cols_dev - 1], chip[:, :, own - 1])
    grid = jnp.concatenate(
        [mine, right[:, :, None], jnp.zeros((3, rows, HALO - 2), jnp.float32), left[:, :, None]], axis=2)
    speed_here, dir_here, class_here = grid[0], grid[1], grid[2]
    strength = (speed_here * 0.1) ** 2
    cos_here, sin_here = jnp.cos(dir_here), jnp.sin(dir_here)

    angle = (jnp.arange(NDIR, dtype=jnp.float32) + 0.5) * (2.0 * math.pi / NDIR)
    cos_lane = pad_to(jnp.repeat(jnp.cos(angle), NFREQ).reshape(QUADS, quad_size), 1, width)
    sin_lane = pad_to(jnp.repeat(jnp.sin(angle), NFREQ).reshape(QUADS, quad_size), 1, width)
    rate_lane = pad_to(jnp.tile(input_rate, quarter), 0, width)
    speed_lane = pad_to(jnp.tile(group_speed, (1, quarter)), 1, width)
    loss_lane = pad_to(jnp.tile(dissipation, (1, quarter)), 1, width, 1.0)
    ax_table = jnp.abs(cos_lane)[:, None] * speed_lane[None]
    ay_table = jnp.abs(sin_lane)[:, None] * speed_lane[None]
    base_table = ax_table + ay_table + loss_lane[None]

    def by_class(table):
        chosen = jnp.broadcast_to(table[:, None, None, 0], (QUADS, rows, cells, width))
        for kind in range(1, class_count):
            chosen = jnp.where((class_here == kind)[None, :, :, None], table[:, None, None, kind], chosen)
        return chosen

    ax = by_class(ax_table)
    ay = by_class(ay_table)
    base = by_class(base_table)
    spread = jnp.maximum(
        cos_here[None, :, :, None] * cos_lane[:, None, None]
        + sin_here[None, :, :, None] * sin_lane[:, None, None], 0.0)
    wind = (rate_lane[None, None, None] * strength[None, :, :, None]) * (spread * spread)

    arrived, ax, ay, base, wind, matrices = lax.optimization_barrier(
        (arrived, ax, ay, base, wind, matrices))

    info = jnp.concatenate([sweep_order.reshape(-1), half[None].astype(jnp.int32)])
    block = cells + rows_dev
    rim_shapes = [jax.ShapeDtypeStruct((QUADS, size, width), jnp.float32)
                  for size in (block, block, HALO, HALO)]
    rim_own, rim_send, out_same, out_cross = pl.pallas_call(
        lambda *refs: rim_kernel(own, rows_dev, comps, quad_size, *refs),
        grid_spec=pltpu.PrefetchScalarGridSpec(
            num_scalar_prefetch=1,
            grid=(1,),
            in_specs=[pl.BlockSpec((slot_total, load), lambda s, info: (0, 0))],
            out_specs=[pl.BlockSpec(shape.shape, lambda s, info: (0, 0, 0)) for shape in rim_shapes],
        ),
        out_shape=rim_shapes,
        compiler_params=pltpu.CompilerParams(vmem_limit_bytes=48 * 2**20),
    )(info, arrived)
    rim_partner = lax.ppermute(rim_send, axes, swap_route)
    rim_same = lax.ppermute(out_same, axes, same_route)
    rim_cross = lax.ppermute(out_cross, axes, cross_route)

    turns = ITERS * QUADS

    def quad_block(shape):
        zeros = (0,) * len(shape)
        return pl.BlockSpec((1,) + shape, lambda t, info: (info[t],) + zeros)

    packed = (QUADS // 2, quad_size, rows_dev, cols_dev)
    whole = pl.BlockSpec(packed, lambda t, info: (0, 0, 0, 0))
    keep, send = pl.pallas_call(
        lambda *refs: sweeps_kernel(rows, own, cells, quad_size, *refs),
        grid_spec=pltpu.PrefetchScalarGridSpec(
            num_scalar_prefetch=1,
            grid=(turns,),
            in_specs=[quad_block((rows, cells, width))] * 4
            + [quad_block((2, width, width))]
            + [quad_block((block, width))] * 2
            + [quad_block((HALO, width))] * 2,
            out_specs=[whole, whole],
            scratch_shapes=[
                pltpu.VMEM((QUADS, rows, cells, width), jnp.float32),
                pltpu.VMEM((QUADS, rows, cells, LANES), jnp.float32),
                pltpu.VMEM((2, cells, width), jnp.float32),
                pltpu.VMEM((rows, 2 * HALO, width), jnp.float32),
            ],
        ),
        out_shape=[jax.ShapeDtypeStruct(packed, jnp.float32)] * 2,
        compiler_params=pltpu.CompilerParams(
            dimension_semantics=("arbitrary",), vmem_limit_bytes=56 * 2**20),
    )(info, ax, ay, base, wind, matrices, rim_own, rim_partner, rim_same, rim_cross)

    got = lax.ppermute(send, axes, swap_route)
    chunks = 4
    part = quad_size // chunks
    half_block = pl.BlockSpec((1, part, rows_dev, cols_dev), lambda p, c, info: (p, c, 0, 0))
    merged = pl.pallas_call(
        lambda *refs: merge_kernel(own, *refs),
        grid_spec=pltpu.PrefetchScalarGridSpec(
            num_scalar_prefetch=1,
            grid=(QUADS // 2, chunks),
            in_specs=[half_block, half_block],
            out_specs=pl.BlockSpec(
                (1, 2, part, rows_dev, cols_dev), lambda p, c, info: (p, 0, c, 0, 0)),
        ),
        out_shape=jax.ShapeDtypeStruct((QUADS // 2, 2, quad_size, rows_dev, cols_dev), jnp.float32),
        compiler_params=pltpu.CompilerParams(vmem_limit_bytes=16 * 2**20),
    )(info, keep, got)
    return merged.reshape(comps, rows_dev, cols_dev)


def solution(mesh):
    placed = (
        P("rows", "cols"),
        P("rows", "cols"),
        P("rows", "cols"),
        P(),
        P(),
        P(),
        P(("rows", "cols"), None),
        P(("rows", "cols")),
        P(),
        P(),
    )
    return jax.shard_map(
        body, mesh=mesh, in_specs=placed, out_specs=P(None, "rows", "cols"), check_vma=False
    )
```

```python
import math

import jax
import jax.numpy as jnp
import numpy as np
from jax import lax
from jax.experimental import pallas as pl
from jax.experimental.pallas import tpu as pltpu
from jax.sharding import PartitionSpec as P

NDIR = 36
NFREQ = 24
CAP = 16
ITERS = 2
QUADS = 4
LANES = 128
HALO = 8

whitecap_rate = 0.5


def split_bf16(value):
    high = value.astype(jnp.bfloat16)
    low = (value - high.astype(jnp.float32)).astype(jnp.bfloat16)
    return high, low


def lane_scale(width):
    golden = (math.sqrt(5.0) - 1.0) / 2.0
    return np.exp2(np.mod(np.arange(width) * golden, 1.0)).astype(np.float32)


def pad_to(array, axis, size, value=0.0):
    widths = [(0, 0)] * array.ndim
    widths[axis] = (0, size - array.shape[axis])
    return jnp.pad(array, widths, constant_values=value)


def pack_kernel(shifts, col_count, rows, comps, dest_ref, spectra_ref, out_ref, high, low, slots):
    step = pl.program_id(0)
    points = dest_ref.shape[1]
    load = out_ref.shape[1]
    total_bits, row_bits, col_bits = shifts

    @pl.when(step == 0)
    def _():
        dest = dest_ref[...]
        grid_row = lax.shift_right_logical(dest, total_bits)
        grid_col = dest & (2**total_bits - 1)
        local_row = grid_row & (2**row_bits - 1)
        local_col = grid_col & (2**col_bits - 1)
        owner = (lax.shift_right_logical(grid_row, row_bits) * col_count
                 + lax.shift_right_logical(grid_col, col_bits))
        on_row = (grid_row == 0) | (grid_row == rows - 1)
        on_left = jnp.where(grid_col == 0, 2**col_bits, 2**col_bits + 2**row_bits) + local_row
        code = jnp.where(on_row, local_col, on_left) + 1
        lanes = jnp.concatenate(
            [owner.astype(jnp.float32), code.astype(jnp.float32), jnp.zeros((6, points), jnp.float32)],
            axis=0)
        columns = lanes.T
        same = columns[:, 0:1] == lanes[0:1]
        above = (lax.broadcasted_iota(jnp.int32, (points, points), 0)
                 < lax.broadcasted_iota(jnp.int32, (points, points), 1))
        rank = jnp.sum(jnp.where(same & above, 1.0, 0.0), axis=0, keepdims=True)
        slots[...] = owner * CAP + rank.astype(jnp.int32)
        spectra = jnp.concatenate(
            [spectra_ref[...], jnp.broadcast_to(lanes[1:2], (load - comps, points))], axis=0)
        high[...], low[...] = split_bf16(spectra)

    place = jnp.where(
        lax.broadcasted_iota(jnp.int32, (out_ref.shape[0], points), 0) + step * out_ref.shape[0]
        == slots[...], 1.0, 0.0).astype(jnp.bfloat16)
    over_points = (((1,), (1,)), ((), ()))
    out_ref[...] = (lax.dot_general(place, high[...], over_points, preferred_element_type=jnp.float32)
                    + lax.dot_general(place, low[...], over_points, preferred_element_type=jnp.float32))


def rim_kernel(own, rows_dev, comps, quad_size, info, arrived_ref, own_ref, send_ref, same_ref,
               cross_ref):
    half = info[ITERS * QUADS]
    cols_dev = 2 * own
    cells = own + HALO
    block = cells + rows_dev
    width = own_ref.shape[2]
    load = arrived_ref.shape[1]
    spots = -(-(2 * block + 2 * HALO) // LANES) * LANES
    lane = lax.broadcasted_iota(jnp.int32, (1, spots), 1)
    at_send = lane >= block
    spot = jnp.where(at_send, lane - block, lane)
    side_at = jnp.where(at_send, 1 - half, half)
    want = jnp.where(spot < own, own * side_at + spot, -1)
    want = jnp.where((spot == own) & (side_at == 0), own, want)
    want = jnp.where((spot == cells - 1) & (side_at == 1), own - 1, want)
    want = jnp.where(spot >= cells, cols_dev + rows_dev * side_at + spot - cells, want)
    rest = lane - 2 * block
    to_left = jnp.where((rest == HALO - 1) & (half == 0), cols_dev - 1, -1)
    to_left = jnp.where((rest == 0) & (half == 1), 0, to_left)
    to_left = jnp.where((rest == HALO) & (half == 0), 0, to_left)
    to_left = jnp.where((rest == 2 * HALO - 1) & (half == 1), cols_dev - 1, to_left)
    want = jnp.where(rest >= 0, to_left, want)
    code = arrived_ref[:, comps:comps + 1]
    gather = jnp.where(code == (want + 1).astype(jnp.float32), 1.0, 0.0)
    gather = jnp.where(want >= 0, gather, 0.0).astype(jnp.bfloat16)
    high, low = split_bf16(arrived_ref[...])
    over_points = (((0,), (0,)), ((), ()))
    summed = (lax.dot_general(gather, high, over_points, preferred_element_type=jnp.float32)
              + lax.dot_general(gather, low, over_points, preferred_element_type=jnp.float32))
    for quad in range(QUADS):
        start = quad * quad_size
        part = summed if quad == 0 else pltpu.roll(summed, load - start, 1)
        own_ref[quad] = part[:block, :width]
        send_ref[quad] = part[block:2 * block, :width]
        same_ref[quad] = part[2 * block:2 * block + HALO, :width]
        cross_ref[quad] = part[2 * block + HALO:2 * block + 2 * HALO, :width]


def sweeps_kernel(rows, own, cells, quad_size, info, ax_ref, ay_ref, base_ref, wind_ref, mt_ref, diag_ref, scale_ref,
                  own_ref, par_ref, same_ref, cross_ref, keep_ref, send_ref,
                  state, power, rim, side):
    turn = pl.program_id(0)
    quad = info[turn]
    half = info[ITERS * QUADS]
    width = mt_ref.shape[2]
    rows_dev = rows // 2
    down = (quad == 0) | (quad == 3)
    step_x = jnp.where(down, 1, -1)
    first_row = jnp.where(down, 0, rows - 1)
    up_y = quad < 2

    @pl.when(turn == 0)
    def _():
        power[...] = jnp.zeros_like(power)

    rim[0] = own_ref[0, 0:cells]
    rim[0, own:cells] = own_ref[0, own:cells] + same_ref[0]
    rim[1] = par_ref[0, 0:cells]
    rim[1, own:cells] = par_ref[0, own:cells] + cross_ref[0]
    edge_at = jnp.where(half == 0, 0, 2 * HALO - 1)
    at_edge = lax.broadcasted_iota(jnp.int32, (2 * HALO, width), 0) == edge_at
    for j in range(rows_dev):
        mine = jnp.where(at_edge, own_ref[0, cells + j:cells + j + 1], 0.0)
        theirs = jnp.where(at_edge, par_ref[0, cells + j:cells + j + 1], 0.0)
        side[j + rows_dev * half] = mine
        side[j + rows_dev * (1 - half)] = theirs

    def run(count, second):
        chains = [(0, count)]

        def factors(i, low, high):
            row = first_row + i * step_x
            total = power[0, row, low:high]
            for other in range(1, QUADS):
                total = total + power[other, row, low:high]
            level = total * (1.0 / (QUADS * quad_size))
            damping = whitecap_rate * level / (1.0 + level)
            den = base_ref[0, row, low:high] + jnp.concatenate([damping] * (width // LANES), axis=1)
            inverse = scale_ref[...] / den
            source = wind_ref[0, row, low:high]
            edge = side[row]
            parts = [source[:HALO] + edge[:HALO], source[HALO:own - HALO],
                     source[own - HALO:own] + edge[HALO:]]
            if high > own:
                parts.append(source[own:])
            source = jnp.concatenate(parts, axis=0)
            if i == 0 or i == rows - 1:
                here = jnp.where(row // rows_dev == half, 0, 1)
                source = source + rim[here, low:high]
            if second:
                before = state[quad, row]
                shifted = jnp.where(up_y, pltpu.roll(before, 1, 0), pltpu.roll(before, cells - 1, 0))
                source = source + ay_ref[0, row, low:high] * shifted[low:high]
            return ax_ref[0, row, low:high] * inverse, source * inverse

        ready = [factors(0, *chain) for chain in chains]
        upwind = [None] * len(chains)
        for i in range(rows):
            updated = []
            for (along, known), before in zip(ready, upwind):
                balance = known if before is None else along * before + known
                mixed = jnp.dot(balance.astype(jnp.bfloat16), mt_ref[0],
                                preferred_element_type=jnp.float32)
                updated.append(diag_ref[0] * balance + mixed)
            if i + 1 < rows:
                ready = [factors(i + 1, *chain) for chain in chains]
            row = first_row + i * step_x
            for (start, stop), value in zip(chains, updated):
                square = value * value
                folded = square[:, :LANES]
                for lane in range(LANES, width, LANES):
                    folded = folded + square[:, lane:lane + LANES]
                state[quad, row, start:stop] = value
                power[quad, row, start:stop] = jnp.broadcast_to(
                    jnp.sum(folded, axis=1, keepdims=True), (stop - start, LANES))
            upwind = updated

    @pl.when(turn < QUADS)
    def _():
        run(cells, False)

    @pl.when(turn >= QUADS)
    def _():
        run(own, True)

    @pl.when(turn == ITERS * QUADS - 1)
    def _():
        for pair in range(QUADS // 2):
            for j in range(rows_dev):
                for out_ref, side_at in ((keep_ref, half), (send_ref, 1 - half)):
                    row = rows_dev * side_at + j
                    both = jnp.concatenate(
                        [state[2 * pair, row, :own], state[2 * pair + 1, row, :own]], axis=0)
                    out_ref[pair, :, j, :] = both.T[:quad_size]


def merge_kernel(own, info, keep_ref, got_ref, out_ref):
    half = info[ITERS * QUADS]
    keep = keep_ref[0]
    got = got_ref[0]
    left = jnp.where(half == 0, keep, got)
    right = jnp.where(half == 0, got, keep)
    low = lax.broadcasted_iota(jnp.int32, keep.shape, 2) < own
    axis = keep.ndim - 1
    out_ref[0, 0] = jnp.where(low, left, pltpu.roll(right, own, axis))
    out_ref[0, 1] = jnp.where(low, pltpu.roll(left, own, axis), right)


def body(
    wind_speed,
    wind_dir,
    depth_class,
    group_speed,
    dissipation,
    input_rate,
    outer_spectra,
    dest_cell,
    refraction_inverse,
    sweep_order,
):
    rows_dev, cols_dev = wind_speed.shape
    row_count = lax.axis_size("rows")
    col_count = lax.axis_size("cols")
    assert row_count == 2
    devices = row_count * col_count
    rows = rows_dev * row_count
    own = cols_dev // 2
    cells = own + HALO
    class_count = group_speed.shape[0]
    comps = outer_spectra.shape[1]
    quad_size = refraction_inverse.shape[1]
    quarter = NDIR // QUADS
    width = -(-quad_size // LANES) * LANES
    axes = ("rows", "cols")
    half = lax.axis_index("rows")

    def device(row_at, col_at):
        return row_at * col_count + col_at

    span = range(col_count)
    swap_route = [(device(1 - h, c), device(h, c)) for h in range(2) for c in span]
    same_route = [(device(0, c - 1), device(0, c)) for c in span if c > 0]
    same_route += [(device(1, c + 1), device(1, c)) for c in span if c + 1 < col_count]
    cross_route = [(device(1, c - 1), device(0, c)) for c in span if c > 0]
    cross_route += [(device(0, c + 1), device(1, c)) for c in span if c + 1 < col_count]

    points = dest_cell.shape[0]
    load = -(-(comps + 1) // LANES) * LANES
    sizes = (cols_dev * col_count, rows_dev, cols_dev)
    shifts = tuple(size.bit_length() - 1 for size in sizes)
    assert all(size == 2**shift for size, shift in zip(sizes, shifts))
    slot_total = devices * CAP
    steps = 4
    outgoing = pl.pallas_call(
        lambda *refs: pack_kernel(shifts, col_count, rows, comps, *refs),
        grid=(steps,),
        in_specs=[pl.BlockSpec((1, points), lambda s: (0, 0)),
                  pl.BlockSpec((comps, points), lambda s: (0, 0))],
        out_specs=pl.BlockSpec((slot_total // steps, load), lambda s: (s, 0)),
        scratch_shapes=[pltpu.VMEM((load, points), jnp.bfloat16),
                        pltpu.VMEM((load, points), jnp.bfloat16),
                        pltpu.VMEM((1, points), jnp.int32)],
        out_shape=jax.ShapeDtypeStruct((slot_total, load), jnp.float32),
        compiler_params=pltpu.CompilerParams(
            dimension_semantics=("arbitrary",), vmem_limit_bytes=48 * 2**20),
    )(dest_cell.reshape(1, points), outer_spectra.T)
    outgoing, refraction_inverse = lax.optimization_barrier((outgoing, refraction_inverse))
    scale = jnp.asarray(lane_scale(width))
    flipped = pad_to(pad_to(jnp.swapaxes(refraction_inverse, 1, 2), 1, width), 2, width)
    scaled = flipped / scale[None, :, None]
    on_diag = jnp.eye(width, dtype=bool)[None]
    matrices = jnp.where(on_diag, 0.0, scaled).astype(jnp.bfloat16)
    diagonal = jnp.sum(jnp.where(on_diag, scaled, 0.0), axis=1, keepdims=True)
    held = jnp.stack([wind_speed, wind_dir, depth_class.astype(jnp.float32)])
    arrived = lax.all_to_all(outgoing.reshape(devices, CAP, load), axes, split_axis=0,
                             concat_axis=0, tiled=True).reshape(slot_total, load)

    partner = lax.ppermute(held, axes, swap_route)
    beside_same = lax.ppermute(held, axes, same_route)
    beside_cross = lax.ppermute(held, axes, cross_route)
    is_low = half == 0
    chip = jnp.concatenate(
        [jnp.where(is_low, held, partner), jnp.where(is_low, partner, held)], axis=1)
    near = jnp.concatenate(
        [jnp.where(is_low, beside_same, beside_cross), jnp.where(is_low, beside_cross, beside_same)],
        axis=1)
    mine = jnp.where(is_low, chip[:, :, :own], chip[:, :, own:])
    right = jnp.where(is_low, chip[:, :, own], near[:, :, 0])
    left = jnp.where(is_low, near[:, :, cols_dev - 1], chip[:, :, own - 1])
    grid = jnp.concatenate(
        [mine, right[:, :, None], jnp.zeros((3, rows, HALO - 2), jnp.float32), left[:, :, None]], axis=2)
    speed_here, dir_here, class_here = grid[0], grid[1], grid[2]
    strength = (speed_here * 0.1) ** 2
    cos_here, sin_here = jnp.cos(dir_here), jnp.sin(dir_here)

    angle = (jnp.arange(NDIR, dtype=jnp.float32) + 0.5) * (2.0 * math.pi / NDIR)
    cos_lane = pad_to(jnp.repeat(jnp.cos(angle), NFREQ).reshape(QUADS, quad_size), 1, width)
    sin_lane = pad_to(jnp.repeat(jnp.sin(angle), NFREQ).reshape(QUADS, quad_size), 1, width)
    rate_lane = pad_to(jnp.tile(input_rate, quarter), 0, width)
    speed_lane = pad_to(jnp.tile(group_speed, (1, quarter)), 1, width)
    loss_lane = pad_to(jnp.tile(dissipation, (1, quarter)), 1, width, 1.0)
    ax_table = jnp.abs(cos_lane)[:, None] * speed_lane[None]
    ay_table = jnp.abs(sin_lane)[:, None] * speed_lane[None]
    base_table = ax_table + ay_table + loss_lane[None]

    def by_class(table):
        chosen = jnp.broadcast_to(table[:, None, None, 0], (QUADS, rows, cells, width))
        for kind in range(1, class_count):
            chosen = jnp.where((class_here == kind)[None, :, :, None], table[:, None, None, kind], chosen)
        return chosen

    ax = by_class(ax_table)
    ay = by_class(ay_table)
    base = by_class(base_table)
    spread = jnp.maximum(
        cos_here[None, :, :, None] * cos_lane[:, None, None]
        + sin_here[None, :, :, None] * sin_lane[:, None, None], 0.0)
    wind = (rate_lane[None, None, None] * strength[None, :, :, None]) * (spread * spread)

    arrived, ax, ay, base, wind, matrices = lax.optimization_barrier(
        (arrived, ax, ay, base, wind, matrices))

    info = jnp.concatenate([sweep_order.reshape(-1), half[None].astype(jnp.int32)])
    block = cells + rows_dev
    rim_shapes = [jax.ShapeDtypeStruct((QUADS, size, width), jnp.float32)
                  for size in (block, block, HALO, HALO)]
    rim_own, rim_send, out_same, out_cross = pl.pallas_call(
        lambda *refs: rim_kernel(own, rows_dev, comps, quad_size, *refs),
        grid_spec=pltpu.PrefetchScalarGridSpec(
            num_scalar_prefetch=1,
            grid=(1,),
            in_specs=[pl.BlockSpec((slot_total, load), lambda s, info: (0, 0))],
            out_specs=[pl.BlockSpec(shape.shape, lambda s, info: (0, 0, 0)) for shape in rim_shapes],
        ),
        out_shape=rim_shapes,
        compiler_params=pltpu.CompilerParams(vmem_limit_bytes=48 * 2**20),
    )(info, arrived)
    rim_partner = lax.ppermute(rim_send, axes, swap_route)
    rim_same = lax.ppermute(out_same, axes, same_route)
    rim_cross = lax.ppermute(out_cross, axes, cross_route)

    turns = ITERS * QUADS

    def quad_block(shape):
        zeros = (0,) * len(shape)
        return pl.BlockSpec((1,) + shape, lambda t, info: (info[t],) + zeros)

    packed = (QUADS // 2, quad_size, rows_dev, cols_dev)
    whole = pl.BlockSpec(packed, lambda t, info: (0, 0, 0, 0))
    keep, send = pl.pallas_call(
        lambda *refs: sweeps_kernel(rows, own, cells, quad_size, *refs),
        grid_spec=pltpu.PrefetchScalarGridSpec(
            num_scalar_prefetch=1,
            grid=(turns,),
            in_specs=[quad_block((rows, cells, width))] * 4
            + [quad_block((width, width)), quad_block((1, width))]
            + [pl.BlockSpec((1, width), lambda t, info: (0, 0))]
            + [quad_block((block, width))] * 2
            + [quad_block((HALO, width))] * 2,
            out_specs=[whole, whole],
            scratch_shapes=[
                pltpu.VMEM((QUADS, rows, cells, width), jnp.float32),
                pltpu.VMEM((QUADS, rows, cells, LANES), jnp.float32),
                pltpu.VMEM((2, cells, width), jnp.float32),
                pltpu.VMEM((rows, 2 * HALO, width), jnp.float32),
            ],
        ),
        out_shape=[jax.ShapeDtypeStruct(packed, jnp.float32)] * 2,
        compiler_params=pltpu.CompilerParams(
            dimension_semantics=("arbitrary",), vmem_limit_bytes=56 * 2**20),
    )(info, ax, ay, base, wind, matrices, diagonal, scale[None], rim_own, rim_partner, rim_same, rim_cross)

    got = lax.ppermute(send, axes, swap_route)
    chunks = 4
    part = quad_size // chunks
    half_block = pl.BlockSpec((1, part, rows_dev, cols_dev), lambda p, c, info: (p, c, 0, 0))
    merged = pl.pallas_call(
        lambda *refs: merge_kernel(own, *refs),
        grid_spec=pltpu.PrefetchScalarGridSpec(
            num_scalar_prefetch=1,
            grid=(QUADS // 2, chunks),
            in_specs=[half_block, half_block],
            out_specs=pl.BlockSpec(
                (1, 2, part, rows_dev, cols_dev), lambda p, c, info: (p, 0, c, 0, 0)),
        ),
        out_shape=jax.ShapeDtypeStruct((QUADS // 2, 2, quad_size, rows_dev, cols_dev), jnp.float32),
        compiler_params=pltpu.CompilerParams(vmem_limit_bytes=16 * 2**20),
    )(info, keep, got)
    return merged.reshape(comps, rows_dev, cols_dev)


def solution(mesh):
    placed = (
        P("rows", "cols"),
        P("rows", "cols"),
        P("rows", "cols"),
        P(),
        P(),
        P(),
        P(("rows", "cols"), None),
        P(("rows", "cols")),
        P(),
        P(),
    )
    return jax.shard_map(
        body, mesh=mesh, in_specs=placed, out_specs=P(None, "rows", "cols"), check_vma=False
    )
```

```python
from functools import partial
import math

import jax
import jax.numpy as jnp
import numpy as np
from jax import lax
from jax.experimental import pallas as pl
from jax.experimental.pallas import tpu as pltpu
from jax.sharding import PartitionSpec as P

NDIR = 36
NFREQ = 24
CAP = 16
ITERS = 2
QUADS = 4
LANES = 128
HALO = 8

whitecap_rate = 0.5


def split_bf16(value):
    high = value.astype(jnp.bfloat16)
    low = (value - high.astype(jnp.float32)).astype(jnp.bfloat16)
    return high, low


def lane_scale(width):
    golden = (math.sqrt(5.0) - 1.0) / 2.0
    return np.exp2(np.mod(np.arange(width) * golden, 1.0)).astype(np.float32)


def pad_to(array, axis, size, value=0.0):
    widths = [(0, 0)] * array.ndim
    widths[axis] = (0, size - array.shape[axis])
    return jnp.pad(array, widths, constant_values=value)


def pack_kernel(shifts, col_count, rows, comps, dest_ref, spectra_ref, out_ref, high, low, slots):
    step = pl.program_id(0)
    points = dest_ref.shape[1]
    load = out_ref.shape[1]
    total_bits, row_bits, col_bits = shifts

    @pl.when(step == 0)
    def _():
        dest = dest_ref[...]
        grid_row = lax.shift_right_logical(dest, total_bits)
        grid_col = dest & (2**total_bits - 1)
        local_row = grid_row & (2**row_bits - 1)
        local_col = grid_col & (2**col_bits - 1)
        owner = (lax.shift_right_logical(grid_row, row_bits) * col_count
                 + lax.shift_right_logical(grid_col, col_bits))
        on_row = (grid_row == 0) | (grid_row == rows - 1)
        on_left = jnp.where(grid_col == 0, 2**col_bits, 2**col_bits + 2**row_bits) + local_row
        code = jnp.where(on_row, local_col, on_left) + 1
        lanes = jnp.concatenate(
            [owner.astype(jnp.float32), code.astype(jnp.float32), jnp.zeros((6, points), jnp.float32)],
            axis=0)
        columns = lanes.T
        same = columns[:, 0:1] == lanes[0:1]
        above = (lax.broadcasted_iota(jnp.int32, (points, points), 0)
                 < lax.broadcasted_iota(jnp.int32, (points, points), 1))
        rank = jnp.sum(jnp.where(same & above, 1.0, 0.0), axis=0, keepdims=True)
        slots[...] = owner * CAP + rank.astype(jnp.int32)
        spectra = jnp.concatenate(
            [spectra_ref[...], jnp.broadcast_to(lanes[1:2], (load - comps, points))], axis=0)
        high[...], low[...] = split_bf16(spectra)

    place = jnp.where(
        lax.broadcasted_iota(jnp.int32, (out_ref.shape[0], points), 0) + step * out_ref.shape[0]
        == slots[...], 1.0, 0.0).astype(jnp.bfloat16)
    over_points = (((1,), (1,)), ((), ()))
    out_ref[...] = (lax.dot_general(place, high[...], over_points, preferred_element_type=jnp.float32)
                    + lax.dot_general(place, low[...], over_points, preferred_element_type=jnp.float32))


def rim_kernel(own, rows_dev, comps, quad_size, info, arrived_ref, own_ref, send_ref, same_ref,
               cross_ref):
    half = info[ITERS * QUADS]
    cols_dev = 2 * own
    cells = own + HALO
    block = cells + rows_dev
    width = own_ref.shape[2]
    load = arrived_ref.shape[1]
    spots = -(-(2 * block + 2 * HALO) // LANES) * LANES
    lane = lax.broadcasted_iota(jnp.int32, (1, spots), 1)
    at_send = lane >= block
    spot = jnp.where(at_send, lane - block, lane)
    side_at = jnp.where(at_send, 1 - half, half)
    want = jnp.where(spot < own, own * side_at + spot, -1)
    want = jnp.where((spot == own) & (side_at == 0), own, want)
    want = jnp.where((spot == cells - 1) & (side_at == 1), own - 1, want)
    want = jnp.where(spot >= cells, cols_dev + rows_dev * side_at + spot - cells, want)
    rest = lane - 2 * block
    to_left = jnp.where((rest == HALO - 1) & (half == 0), cols_dev - 1, -1)
    to_left = jnp.where((rest == 0) & (half == 1), 0, to_left)
    to_left = jnp.where((rest == HALO) & (half == 0), 0, to_left)
    to_left = jnp.where((rest == 2 * HALO - 1) & (half == 1), cols_dev - 1, to_left)
    want = jnp.where(rest >= 0, to_left, want)
    code = arrived_ref[:, comps:comps + 1]
    gather = jnp.where(code == (want + 1).astype(jnp.float32), 1.0, 0.0)
    gather = jnp.where(want >= 0, gather, 0.0).astype(jnp.bfloat16)
    high, low = split_bf16(arrived_ref[...])
    over_points = (((0,), (0,)), ((), ()))
    summed = (lax.dot_general(gather, high, over_points, preferred_element_type=jnp.float32)
              + lax.dot_general(gather, low, over_points, preferred_element_type=jnp.float32))
    for quad in range(QUADS):
        start = quad * quad_size
        part = summed if quad == 0 else pltpu.roll(summed, load - start, 1)
        own_ref[quad] = part[:block, :width]
        send_ref[quad] = part[block:2 * block, :width]
        same_ref[quad] = part[2 * block:2 * block + HALO, :width]
        cross_ref[quad] = part[2 * block + HALO:2 * block + 2 * HALO, :width]


def sweeps_kernel(rows, own, cells, quad_size, info, ax_ref, ay_ref, base_ref, wind_ref, mt_ref, diag_ref, scale_ref,
                  own_ref, par_ref, same_ref, cross_ref, *rest):
    pairs = QUADS // 2
    keep_refs, send_refs = rest[:pairs], rest[pairs:2 * pairs]
    state, power, rim, side = rest[2 * pairs:]
    turn = pl.program_id(0)
    quad = info[turn]
    half = info[ITERS * QUADS]
    width = mt_ref.shape[2]
    rows_dev = rows // 2
    down = (quad == 0) | (quad == 3)
    step_x = jnp.where(down, 1, -1)
    first_row = jnp.where(down, 0, rows - 1)
    up_y = quad < 2

    @pl.when(turn == 0)
    def _():
        power[...] = jnp.zeros_like(power)

    rim[0] = own_ref[0, 0:cells]
    rim[0, own:cells] = own_ref[0, own:cells] + same_ref[0]
    rim[1] = par_ref[0, 0:cells]
    rim[1, own:cells] = par_ref[0, own:cells] + cross_ref[0]
    edge_at = jnp.where(half == 0, 0, 2 * HALO - 1)
    at_edge = lax.broadcasted_iota(jnp.int32, (2 * HALO, width), 0) == edge_at
    for j in range(rows_dev):
        mine = jnp.where(at_edge, own_ref[0, cells + j:cells + j + 1], 0.0)
        theirs = jnp.where(at_edge, par_ref[0, cells + j:cells + j + 1], 0.0)
        side[j + rows_dev * half] = mine
        side[j + rows_dev * (1 - half)] = theirs

    def run(count, second):
        chains = [(0, own // 2), (own // 2, count)]

        def factors(i, low, high):
            row = first_row + i * step_x
            total = power[0, row, low:high]
            for other in range(1, QUADS):
                total = total + power[other, row, low:high]
            level = total * (1.0 / (QUADS * quad_size))
            damping = whitecap_rate * level / (1.0 + level)
            den = base_ref[0, row, low:high] + jnp.concatenate([damping] * (width // LANES), axis=1)
            inverse = scale_ref[...] / den
            source = wind_ref[0, row, low:high]
            if low == 0:
                source = jnp.concatenate([source[:HALO] + side[row, :HALO], source[HALO:]], axis=0)
            else:
                last = own - HALO - low
                parts = [source[:last], source[last:own - low] + side[row, HALO:]]
                if high > own:
                    parts.append(source[own - low:])
                source = jnp.concatenate(parts, axis=0)
            if i == 0 or i == rows - 1:
                here = jnp.where(row // rows_dev == half, 0, 1)
                source = source + rim[here, low:high]
            if second:
                before = state[quad, row]
                shifted = jnp.where(up_y, pltpu.roll(before, 1, 0), pltpu.roll(before, cells - 1, 0))
                source = source + ay_ref[0, row, low:high] * shifted[low:high]
            return ax_ref[0, row, low:high] * inverse, source * inverse

        ready = [factors(0, *chain) for chain in chains]
        upwind = [None] * len(chains)
        for i in range(rows):
            updated = []
            for (along, known), before in zip(ready, upwind):
                balance = known if before is None else along * before + known
                mixed = jnp.dot(balance.astype(jnp.bfloat16), mt_ref[0],
                                preferred_element_type=jnp.float32)
                updated.append(diag_ref[0] * balance + mixed)
            if i + 1 < rows:
                ready = [factors(i + 1, *chain) for chain in chains]
            row = first_row + i * step_x
            for (start, stop), value in zip(chains, updated):
                square = value * value
                folded = square[:, :LANES]
                for lane in range(LANES, width, LANES):
                    folded = folded + square[:, lane:lane + LANES]
                state[quad, row, start:stop] = value
                power[quad, row, start:stop] = jnp.broadcast_to(
                    jnp.sum(folded, axis=1, keepdims=True), (stop - start, LANES))
            upwind = updated

    @pl.when(turn < QUADS)
    def _():
        run(cells, False)

    @pl.when(turn >= QUADS)
    def _():
        run(own, True)

    @pl.when(turn == ITERS * QUADS - 1)
    def _():
        for pair in range(pairs):
            for j in range(rows_dev):
                for out_ref, side_at in ((keep_refs[pair], half), (send_refs[pair], 1 - half)):
                    row = rows_dev * side_at + j
                    both = jnp.concatenate(
                        [state[2 * pair, row, :own], state[2 * pair + 1, row, :own]], axis=0)
                    out_ref[:, j, :] = both.T[:quad_size]


def merge_kernel(own, pair, chunks, info, keep_ref, got_ref, *rest):
    out_ref, stage, sems = rest[-3:]
    half = info[ITERS * QUADS]
    part = keep_ref.shape[0] // chunks
    copies = []
    for chunk in range(chunks):
        span = pl.ds(chunk * part, part)
        keep = keep_ref[span]
        got = got_ref[span]
        left = jnp.where(half == 0, keep, got)
        right = jnp.where(half == 0, got, keep)
        low = lax.broadcasted_iota(jnp.int32, keep.shape, 2) < own
        stage[chunk, 0] = jnp.where(low, left, pltpu.roll(right, own, 2))
        stage[chunk, 1] = jnp.where(low, pltpu.roll(left, own, 2), right)
        for member in range(2):
            copies.append(pltpu.make_async_copy(
                stage.at[chunk, member], out_ref.at[2 * pair + member, span], sems.at[chunk, member]))
            copies[-1].start()
    for copy in copies:
        copy.wait()


def body(
    wind_speed,
    wind_dir,
    depth_class,
    group_speed,
    dissipation,
    input_rate,
    outer_spectra,
    dest_cell,
    refraction_inverse,
    sweep_order,
):
    rows_dev, cols_dev = wind_speed.shape
    row_count = lax.axis_size("rows")
    col_count = lax.axis_size("cols")
    assert row_count == 2
    devices = row_count * col_count
    rows = rows_dev * row_count
    own = cols_dev // 2
    cells = own + HALO
    class_count = group_speed.shape[0]
    comps = outer_spectra.shape[1]
    quad_size = refraction_inverse.shape[1]
    quarter = NDIR // QUADS
    width = -(-quad_size // LANES) * LANES
    axes = ("rows", "cols")
    half = lax.axis_index("rows")

    def device(row_at, col_at):
        return row_at * col_count + col_at

    span = range(col_count)
    swap_route = [(device(1 - h, c), device(h, c)) for h in range(2) for c in span]
    same_route = [(device(0, c - 1), device(0, c)) for c in span if c > 0]
    same_route += [(device(1, c + 1), device(1, c)) for c in span if c + 1 < col_count]
    cross_route = [(device(1, c - 1), device(0, c)) for c in span if c > 0]
    cross_route += [(device(0, c + 1), device(1, c)) for c in span if c + 1 < col_count]

    points = dest_cell.shape[0]
    load = -(-(comps + 1) // LANES) * LANES
    sizes = (cols_dev * col_count, rows_dev, cols_dev)
    shifts = tuple(size.bit_length() - 1 for size in sizes)
    assert all(size == 2**shift for size, shift in zip(sizes, shifts))
    slot_total = devices * CAP
    steps = 4
    outgoing = pl.pallas_call(
        lambda *refs: pack_kernel(shifts, col_count, rows, comps, *refs),
        grid=(steps,),
        in_specs=[pl.BlockSpec((1, points), lambda s: (0, 0)),
                  pl.BlockSpec((comps, points), lambda s: (0, 0))],
        out_specs=pl.BlockSpec((slot_total // steps, load), lambda s: (s, 0)),
        scratch_shapes=[pltpu.VMEM((load, points), jnp.bfloat16),
                        pltpu.VMEM((load, points), jnp.bfloat16),
                        pltpu.VMEM((1, points), jnp.int32)],
        out_shape=jax.ShapeDtypeStruct((slot_total, load), jnp.float32),
        compiler_params=pltpu.CompilerParams(
            dimension_semantics=("arbitrary",), vmem_limit_bytes=48 * 2**20),
    )(dest_cell.reshape(1, points), outer_spectra.T)
    outgoing, refraction_inverse = lax.optimization_barrier((outgoing, refraction_inverse))
    scale = jnp.asarray(lane_scale(width))
    flipped = pad_to(pad_to(jnp.swapaxes(refraction_inverse, 1, 2), 1, width), 2, width)
    scaled = flipped / scale[None, :, None]
    on_diag = jnp.eye(width, dtype=bool)[None]
    matrices = jnp.where(on_diag, 0.0, scaled).astype(jnp.bfloat16)
    diagonal = jnp.sum(jnp.where(on_diag, scaled, 0.0), axis=1, keepdims=True)
    held = jnp.stack([wind_speed, wind_dir, depth_class.astype(jnp.float32)])
    arrived = lax.all_to_all(outgoing.reshape(devices, CAP, load), axes, split_axis=0,
                             concat_axis=0, tiled=True).reshape(slot_total, load)

    partner = lax.ppermute(held, axes, swap_route)
    is_low = half == 0
    chip = jnp.concatenate(
        [jnp.where(is_low, held, partner), jnp.where(is_low, partner, held)], axis=1)
    near = lax.ppermute(chip, axes, same_route)
    mine = jnp.where(is_low, chip[:, :, :own], chip[:, :, own:])
    right = jnp.where(is_low, chip[:, :, own], near[:, :, 0])
    left = jnp.where(is_low, near[:, :, cols_dev - 1], chip[:, :, own - 1])
    grid = jnp.concatenate(
        [mine, right[:, :, None], jnp.zeros((3, rows, HALO - 2), jnp.float32), left[:, :, None]], axis=2)
    speed_here, dir_here, class_here = grid[0], grid[1], grid[2]
    strength = (speed_here * 0.1) ** 2
    cos_here, sin_here = jnp.cos(dir_here), jnp.sin(dir_here)

    angle = (jnp.arange(NDIR, dtype=jnp.float32) + 0.5) * (2.0 * math.pi / NDIR)
    cos_lane = pad_to(jnp.repeat(jnp.cos(angle), NFREQ).reshape(QUADS, quad_size), 1, width)
    sin_lane = pad_to(jnp.repeat(jnp.sin(angle), NFREQ).reshape(QUADS, quad_size), 1, width)
    rate_lane = pad_to(jnp.tile(input_rate, quarter), 0, width)
    speed_lane = pad_to(jnp.tile(group_speed, (1, quarter)), 1, width)
    loss_lane = pad_to(jnp.tile(dissipation, (1, quarter)), 1, width, 1.0)
    ax_table = jnp.abs(cos_lane)[:, None] * speed_lane[None]
    ay_table = jnp.abs(sin_lane)[:, None] * speed_lane[None]
    base_table = ax_table + ay_table + loss_lane[None]

    def by_class(table):
        chosen = jnp.broadcast_to(table[:, None, None, 0], (QUADS, rows, cells, width))
        for kind in range(1, class_count):
            chosen = jnp.where((class_here == kind)[None, :, :, None], table[:, None, None, kind], chosen)
        return chosen

    ax = by_class(ax_table)
    ay = by_class(ay_table)
    base = by_class(base_table)
    spread = jnp.maximum(
        cos_here[None, :, :, None] * cos_lane[:, None, None]
        + sin_here[None, :, :, None] * sin_lane[:, None, None], 0.0)
    wind = (rate_lane[None, None, None] * strength[None, :, :, None]) * (spread * spread)

    arrived, ax, ay, base, wind, matrices = lax.optimization_barrier(
        (arrived, ax, ay, base, wind, matrices))

    info = jnp.concatenate([sweep_order.reshape(-1), half[None].astype(jnp.int32)])
    block = cells + rows_dev
    rim_shapes = [jax.ShapeDtypeStruct((QUADS, size, width), jnp.float32)
                  for size in (block, block, HALO, HALO)]
    rim_own, rim_send, out_same, out_cross = pl.pallas_call(
        lambda *refs: rim_kernel(own, rows_dev, comps, quad_size, *refs),
        grid_spec=pltpu.PrefetchScalarGridSpec(
            num_scalar_prefetch=1,
            grid=(1,),
            in_specs=[pl.BlockSpec((slot_total, load), lambda s, info: (0, 0))],
            out_specs=[pl.BlockSpec(shape.shape, lambda s, info: (0, 0, 0)) for shape in rim_shapes],
        ),
        out_shape=rim_shapes,
        compiler_params=pltpu.CompilerParams(vmem_limit_bytes=48 * 2**20),
    )(info, arrived)
    rim_partner = lax.ppermute(rim_send, axes, swap_route)
    rim_same = lax.ppermute(out_same, axes, same_route)
    rim_cross = lax.ppermute(out_cross, axes, cross_route)

    turns = ITERS * QUADS

    def quad_block(shape):
        zeros = (0,) * len(shape)
        return pl.BlockSpec((1,) + shape, lambda t, info: (info[t],) + zeros)

    pairs = QUADS // 2
    packed = jax.ShapeDtypeStruct((quad_size, rows_dev, cols_dev), jnp.float32)
    in_vmem = pl.BlockSpec(memory_space=pltpu.VMEM)
    halves = pl.pallas_call(
        lambda *refs: sweeps_kernel(rows, own, cells, quad_size, *refs),
        grid_spec=pltpu.PrefetchScalarGridSpec(
            num_scalar_prefetch=1,
            grid=(turns,),
            in_specs=[quad_block((rows, cells, width))] * 4
            + [quad_block((width, width)), quad_block((1, width))]
            + [pl.BlockSpec((1, width), lambda t, info: (0, 0))]
            + [quad_block((block, width))] * 2
            + [quad_block((HALO, width))] * 2,
            out_specs=[in_vmem] * (2 * pairs),
            scratch_shapes=[
                pltpu.VMEM((QUADS, rows, cells, width), jnp.float32),
                pltpu.VMEM((QUADS, rows, cells, LANES), jnp.float32),
                pltpu.VMEM((2, cells, width), jnp.float32),
                pltpu.VMEM((rows, 2 * HALO, width), jnp.float32),
            ],
        ),
        out_shape=[packed] * (2 * pairs),
        compiler_params=pltpu.CompilerParams(
            dimension_semantics=("arbitrary",), vmem_limit_bytes=56 * 2**20),
    )(info, ax, ay, base, wind, matrices, diagonal, scale[None], rim_own, rim_partner, rim_same, rim_cross)

    got = [lax.ppermute(half_out, axes, swap_route) for half_out in halves[pairs:]]
    chunks = 4
    merged = []
    for pair in range(pairs):
        merged = [pl.pallas_call(
            partial(merge_kernel, own, pair, chunks),
            in_specs=[pl.BlockSpec(memory_space=pltpu.SMEM), in_vmem, in_vmem]
            + [pl.BlockSpec(memory_space=pl.ANY)] * len(merged),
            out_specs=pl.BlockSpec(memory_space=pl.ANY),
            scratch_shapes=[
                pltpu.VMEM((chunks, 2, quad_size // chunks, rows_dev, cols_dev), jnp.float32),
                pltpu.SemaphoreType.DMA((chunks, 2))],
            out_shape=jax.ShapeDtypeStruct((QUADS, quad_size, rows_dev, cols_dev), jnp.float32),
            input_output_aliases={3: 0} if merged else {},
            compiler_params=pltpu.CompilerParams(vmem_limit_bytes=16 * 2**20),
        )(info, halves[pair], got[pair], *merged)]
    return merged[0].reshape(comps, rows_dev, cols_dev)


def solution(mesh):
    placed = (
        P("rows", "cols"),
        P("rows", "cols"),
        P("rows", "cols"),
        P(),
        P(),
        P(),
        P(("rows", "cols"), None),
        P(("rows", "cols")),
        P(),
        P(),
    )
    return jax.shard_map(
        body, mesh=mesh, in_specs=placed, out_specs=P(None, "rows", "cols"), check_vma=False
    )
```

```python
from functools import partial
import math

import jax
import jax.numpy as jnp
import numpy as np
from jax import lax
from jax.experimental import pallas as pl
from jax.experimental.pallas import tpu as pltpu
from jax.sharding import PartitionSpec as P

NDIR = 36
NFREQ = 24
CAP = 16
ITERS = 2
QUADS = 4
LANES = 128
HALO = 8

whitecap_rate = 0.5


def split_bf16(value):
    high = value.astype(jnp.bfloat16)
    low = (value - high.astype(jnp.float32)).astype(jnp.bfloat16)
    return high, low


def lane_scale(width):
    golden = (math.sqrt(5.0) - 1.0) / 2.0
    return np.exp2(np.mod(np.arange(width) * golden, 1.0)).astype(np.float32)


def pad_to(array, axis, size, value=0.0):
    widths = [(0, 0)] * array.ndim
    widths[axis] = (0, size - array.shape[axis])
    return jnp.pad(array, widths, constant_values=value)


def pack_kernel(shifts, col_count, rows, comps, dest_ref, spectra_ref, out_ref, high, low, slots):
    step = pl.program_id(0)
    points = dest_ref.shape[1]
    load = out_ref.shape[1]
    total_bits, row_bits, col_bits = shifts

    @pl.when(step == 0)
    def _():
        dest = dest_ref[...]
        grid_row = lax.shift_right_logical(dest, total_bits)
        grid_col = dest & (2**total_bits - 1)
        local_row = grid_row & (2**row_bits - 1)
        local_col = grid_col & (2**col_bits - 1)
        owner = (lax.shift_right_logical(grid_row, row_bits) * col_count
                 + lax.shift_right_logical(grid_col, col_bits))
        on_row = (grid_row == 0) | (grid_row == rows - 1)
        on_left = jnp.where(grid_col == 0, 2**col_bits, 2**col_bits + 2**row_bits) + local_row
        code = jnp.where(on_row, local_col, on_left) + 1
        lanes = jnp.concatenate(
            [owner.astype(jnp.float32), code.astype(jnp.float32), jnp.zeros((6, points), jnp.float32)],
            axis=0)
        columns = lanes.T
        same = columns[:, 0:1] == lanes[0:1]
        above = (lax.broadcasted_iota(jnp.int32, (points, points), 0)
                 < lax.broadcasted_iota(jnp.int32, (points, points), 1))
        rank = jnp.sum(jnp.where(same & above, 1.0, 0.0), axis=0, keepdims=True)
        slots[...] = owner * CAP + rank.astype(jnp.int32)
        spectra = jnp.concatenate(
            [spectra_ref[...], jnp.broadcast_to(lanes[1:2], (load - comps, points))], axis=0)
        high[...], low[...] = split_bf16(spectra)

    place = jnp.where(
        lax.broadcasted_iota(jnp.int32, (out_ref.shape[0], points), 0) + step * out_ref.shape[0]
        == slots[...], 1.0, 0.0).astype(jnp.bfloat16)
    over_points = (((1,), (1,)), ((), ()))
    out_ref[...] = (lax.dot_general(place, high[...], over_points, preferred_element_type=jnp.float32)
                    + lax.dot_general(place, low[...], over_points, preferred_element_type=jnp.float32))


def rim_kernel(own, rows_dev, comps, quad_size, info, arrived_ref, own_ref, send_ref, same_ref,
               cross_ref):
    half = info[ITERS * QUADS]
    cols_dev = 2 * own
    cells = own + HALO
    block = cells + rows_dev
    width = own_ref.shape[2]
    load = arrived_ref.shape[1]
    spots = -(-(2 * block + 2 * HALO) // LANES) * LANES
    lane = lax.broadcasted_iota(jnp.int32, (1, spots), 1)
    at_send = lane >= block
    spot = jnp.where(at_send, lane - block, lane)
    side_at = jnp.where(at_send, 1 - half, half)
    want = jnp.where(spot < own, own * side_at + spot, -1)
    want = jnp.where((spot == own) & (side_at == 0), own, want)
    want = jnp.where((spot == cells - 1) & (side_at == 1), own - 1, want)
    want = jnp.where(spot >= cells, cols_dev + rows_dev * side_at + spot - cells, want)
    rest = lane - 2 * block
    to_left = jnp.where((rest == HALO - 1) & (half == 0), cols_dev - 1, -1)
    to_left = jnp.where((rest == 0) & (half == 1), 0, to_left)
    to_left = jnp.where((rest == HALO) & (half == 0), 0, to_left)
    to_left = jnp.where((rest == 2 * HALO - 1) & (half == 1), cols_dev - 1, to_left)
    want = jnp.where(rest >= 0, to_left, want)
    code = arrived_ref[:, comps:comps + 1]
    gather = jnp.where(code == (want + 1).astype(jnp.float32), 1.0, 0.0)
    gather = jnp.where(want >= 0, gather, 0.0).astype(jnp.bfloat16)
    high, low = split_bf16(arrived_ref[...])
    over_points = (((0,), (0,)), ((), ()))
    summed = (lax.dot_general(gather, high, over_points, preferred_element_type=jnp.float32)
              + lax.dot_general(gather, low, over_points, preferred_element_type=jnp.float32))
    for quad in range(QUADS):
        start = quad * quad_size
        part = summed if quad == 0 else pltpu.roll(summed, load - start, 1)
        own_ref[quad] = part[:block, :width]
        send_ref[quad] = part[block:2 * block, :width]
        same_ref[quad] = part[2 * block:2 * block + HALO, :width]
        cross_ref[quad] = part[2 * block + HALO:2 * block + 2 * HALO, :width]


def sweeps_kernel(rows, own, cells, quad_size, info, ax_ref, ay_ref, base_ref, wind_ref, mt_ref, diag_ref, scale_ref,
                  ax_table, base_table, lane_table, far_ref,
                  own_ref, par_ref, same_ref, cross_ref, *rest):
    pairs = QUADS // 2
    keep_refs, send_refs = rest[:pairs], rest[pairs:2 * pairs]
    state, power, rim, side = rest[2 * pairs:]
    turn = pl.program_id(0)
    quad = info[turn]
    half = info[ITERS * QUADS]
    width = mt_ref.shape[2]
    rows_dev = rows // 2
    down = (quad == 0) | (quad == 3)
    step_x = jnp.where(down, 1, -1)
    first_row = jnp.where(down, 0, rows - 1)
    up_y = quad < 2

    @pl.when(turn == 0)
    def _():
        power[...] = jnp.zeros_like(power)

    rim[0] = own_ref[0, 0:cells]
    rim[0, own:cells] = own_ref[0, own:cells] + same_ref[0]
    rim[1] = par_ref[0, 0:cells]
    rim[1, own:cells] = par_ref[0, own:cells] + cross_ref[0]
    far_at = jnp.where(half == 0, HALO - 1, 0)
    at_far = lax.broadcasted_iota(jnp.int32, (HALO, width), 0) == far_at
    edge_at = jnp.where(half == 0, 0, 2 * HALO - 1)
    at_edge = lax.broadcasted_iota(jnp.int32, (2 * HALO, width), 0) == edge_at
    for j in range(rows_dev):
        mine = jnp.where(at_edge, own_ref[0, cells + j:cells + j + 1], 0.0)
        theirs = jnp.where(at_edge, par_ref[0, cells + j:cells + j + 1], 0.0)
        side[j + rows_dev * half] = mine
        side[j + rows_dev * (1 - half)] = theirs

    def run(count, second):
        chains = [(0, count)]

        def patched(block, far_row):
            if second:
                return block
            return jnp.concatenate([block[:own], jnp.where(at_far, far_row, block[own:])], axis=0)

        def factors(i, low, high):
            row = first_row + i * step_x
            kind = far_ref[0, row]
            far_ax = jnp.zeros((1, width), jnp.float32)
            far_base = jnp.zeros((1, width), jnp.float32)
            for each in range(ax_table.shape[1]):
                far_ax = jnp.where(kind == each, ax_table[0, each:each + 1], far_ax)
                far_base = jnp.where(kind == each, base_table[0, each:each + 1], far_base)
            spread = jnp.maximum(
                far_ref[2, row] * lane_table[0, 1:2] + far_ref[3, row] * lane_table[0, 2:3], 0.0)
            far_wind = (lane_table[0, 0:1] * far_ref[1, row]) * (spread * spread)
            total = power[0, row, low:high]
            for other in range(1, QUADS):
                total = total + power[other, row, low:high]
            level = total * (1.0 / (QUADS * quad_size))
            damping = whitecap_rate * level / (1.0 + level)
            den = patched(base_ref[0, row, low:high], far_base) + jnp.concatenate([damping] * (width // LANES), axis=1)
            inverse = scale_ref[...] / den
            source = patched(wind_ref[0, row, low:high], far_wind)
            edge = side[row]
            parts = [source[:HALO] + edge[:HALO], source[HALO:own - HALO],
                     source[own - HALO:own] + edge[HALO:]]
            if high > own:
                parts.append(source[own:])
            source = jnp.concatenate(parts, axis=0)
            if i == 0 or i == rows - 1:
                here = jnp.where(row // rows_dev == half, 0, 1)
                source = source + rim[here, low:high]
            if second:
                before = state[quad, row]
                shifted = jnp.where(up_y, pltpu.roll(before, 1, 0), pltpu.roll(before, cells - 1, 0))
                source = source + ay_ref[0, row, low:high] * shifted[low:high]
            return patched(ax_ref[0, row, low:high], far_ax) * inverse, source * inverse

        ready = [factors(0, *chain) for chain in chains]
        upwind = [None] * len(chains)
        for i in range(rows):
            updated = []
            for (along, known), before in zip(ready, upwind):
                balance = known if before is None else along * before + known
                mixed = jnp.dot(balance.astype(jnp.bfloat16), mt_ref[0],
                                preferred_element_type=jnp.float32)
                updated.append(diag_ref[0] * balance + mixed)
            if i + 1 < rows:
                ready = [factors(i + 1, *chain) for chain in chains]
            row = first_row + i * step_x
            for (start, stop), value in zip(chains, updated):
                square = value * value
                folded = square[:, :LANES]
                for lane in range(LANES, width, LANES):
                    folded = folded + square[:, lane:lane + LANES]
                state[quad, row, start:stop] = value
                power[quad, row, start:stop] = jnp.broadcast_to(
                    jnp.sum(folded, axis=1, keepdims=True), (stop - start, LANES))
            upwind = updated

    @pl.when(turn < QUADS)
    def _():
        run(cells, False)

    @pl.when(turn >= QUADS)
    def _():
        run(own, True)

    @pl.when(turn == ITERS * QUADS - 1)
    def _():
        for pair in range(pairs):
            for j in range(rows_dev):
                for out_ref, side_at in ((keep_refs[pair], half), (send_refs[pair], 1 - half)):
                    row = rows_dev * side_at + j
                    both = jnp.concatenate(
                        [state[2 * pair, row, :own], state[2 * pair + 1, row, :own]], axis=0)
                    out_ref[:, j, :] = both.T[:quad_size]


def merge_kernel(own, pair, chunks, info, keep_ref, got_ref, *rest):
    out_ref, stage, sems = rest[-3:]
    half = info[ITERS * QUADS]
    part = keep_ref.shape[0] // chunks
    copies = []
    for chunk in range(chunks):
        span = pl.ds(chunk * part, part)
        keep = keep_ref[span]
        got = got_ref[span]
        left = jnp.where(half == 0, keep, got)
        right = jnp.where(half == 0, got, keep)
        low = lax.broadcasted_iota(jnp.int32, keep.shape, 2) < own
        stage[chunk, 0] = jnp.where(low, left, pltpu.roll(right, own, 2))
        stage[chunk, 1] = jnp.where(low, pltpu.roll(left, own, 2), right)
        for member in range(2):
            copies.append(pltpu.make_async_copy(
                stage.at[chunk, member], out_ref.at[2 * pair + member, span], sems.at[chunk, member]))
            copies[-1].start()
    for copy in copies:
        copy.wait()


def body(
    wind_speed,
    wind_dir,
    depth_class,
    group_speed,
    dissipation,
    input_rate,
    outer_spectra,
    dest_cell,
    refraction_inverse,
    sweep_order,
):
    rows_dev, cols_dev = wind_speed.shape
    row_count = lax.axis_size("rows")
    col_count = lax.axis_size("cols")
    assert row_count == 2
    devices = row_count * col_count
    rows = rows_dev * row_count
    own = cols_dev // 2
    cells = own + HALO
    class_count = group_speed.shape[0]
    comps = outer_spectra.shape[1]
    quad_size = refraction_inverse.shape[1]
    quarter = NDIR // QUADS
    width = -(-quad_size // LANES) * LANES
    axes = ("rows", "cols")
    half = lax.axis_index("rows")

    def device(row_at, col_at):
        return row_at * col_count + col_at

    span = range(col_count)
    swap_route = [(device(1 - h, c), device(h, c)) for h in range(2) for c in span]
    same_route = [(device(0, c - 1), device(0, c)) for c in span if c > 0]
    same_route += [(device(1, c + 1), device(1, c)) for c in span if c + 1 < col_count]
    cross_route = [(device(1, c - 1), device(0, c)) for c in span if c > 0]
    cross_route += [(device(0, c + 1), device(1, c)) for c in span if c + 1 < col_count]

    points = dest_cell.shape[0]
    load = -(-(comps + 1) // LANES) * LANES
    sizes = (cols_dev * col_count, rows_dev, cols_dev)
    shifts = tuple(size.bit_length() - 1 for size in sizes)
    assert all(size == 2**shift for size, shift in zip(sizes, shifts))
    slot_total = devices * CAP
    steps = 4
    in_vmem = pl.BlockSpec(memory_space=pltpu.VMEM)
    outgoing = pl.pallas_call(
        lambda *refs: pack_kernel(shifts, col_count, rows, comps, *refs),
        grid=(steps,),
        in_specs=[in_vmem, in_vmem],
        out_specs=pl.BlockSpec((slot_total // steps, load), lambda s: (s, 0)),
        scratch_shapes=[pltpu.VMEM((load, points), jnp.bfloat16),
                        pltpu.VMEM((load, points), jnp.bfloat16),
                        pltpu.VMEM((1, points), jnp.int32)],
        out_shape=jax.ShapeDtypeStruct((slot_total, load), jnp.float32),
        compiler_params=pltpu.CompilerParams(
            dimension_semantics=("arbitrary",), vmem_limit_bytes=48 * 2**20),
    )(dest_cell.reshape(1, points), outer_spectra.T)
    outgoing, refraction_inverse = lax.optimization_barrier((outgoing, refraction_inverse))
    scale = jnp.asarray(lane_scale(width))
    flipped = pad_to(pad_to(jnp.swapaxes(refraction_inverse, 1, 2), 1, width), 2, width)
    scaled = flipped / scale[None, :, None]
    on_diag = jnp.eye(width, dtype=bool)[None]
    matrices = jnp.where(on_diag, 0.0, scaled).astype(jnp.bfloat16)
    diagonal = jnp.sum(jnp.where(on_diag, scaled, 0.0), axis=1, keepdims=True)
    held = jnp.stack([wind_speed, wind_dir, depth_class.astype(jnp.float32)])
    arrived = lax.all_to_all(outgoing.reshape(devices, CAP, load), axes, split_axis=0,
                             concat_axis=0, tiled=True).reshape(slot_total, load)

    partner = lax.ppermute(held, axes, swap_route)
    is_low = half == 0
    chip = jnp.concatenate(
        [jnp.where(is_low, held, partner), jnp.where(is_low, partner, held)], axis=1)
    strength = (chip[0] * 0.1) ** 2
    feats = jnp.stack([chip[2], strength, jnp.cos(chip[1]), jnp.sin(chip[1])])
    far = lax.ppermute(
        jnp.where(is_low, feats[:, :, cols_dev - 1], feats[:, :, 0]), axes, same_route)
    mine = jnp.where(is_low, feats[:, :, :own], feats[:, :, own:])
    right = jnp.where(is_low, feats[:, :, own], 0.0)
    left = jnp.where(is_low, 0.0, feats[:, :, own - 1])
    grid = jnp.concatenate(
        [mine, right[:, :, None], jnp.zeros((4, rows, HALO - 2), jnp.float32), left[:, :, None]], axis=2)
    class_here, strength, cos_here, sin_here = grid[0], grid[1], grid[2], grid[3]

    angle = (jnp.arange(NDIR, dtype=jnp.float32) + 0.5) * (2.0 * math.pi / NDIR)
    cos_lane = pad_to(jnp.repeat(jnp.cos(angle), NFREQ).reshape(QUADS, quad_size), 1, width)
    sin_lane = pad_to(jnp.repeat(jnp.sin(angle), NFREQ).reshape(QUADS, quad_size), 1, width)
    rate_lane = pad_to(jnp.tile(input_rate, quarter), 0, width)
    speed_lane = pad_to(jnp.tile(group_speed, (1, quarter)), 1, width)
    loss_lane = pad_to(jnp.tile(dissipation, (1, quarter)), 1, width, 1.0)
    ax_table = jnp.abs(cos_lane)[:, None] * speed_lane[None]
    ay_table = jnp.abs(sin_lane)[:, None] * speed_lane[None]
    base_table = ax_table + ay_table + loss_lane[None]

    lane_table = jnp.stack(
        [jnp.broadcast_to(rate_lane, (QUADS, width)), cos_lane, sin_lane], axis=1)

    def by_class(table):
        chosen = jnp.broadcast_to(table[:, None, None, 0], (QUADS, rows, cells, width))
        for kind in range(1, class_count):
            chosen = jnp.where((class_here == kind)[None, :, :, None], table[:, None, None, kind], chosen)
        return chosen

    ax = by_class(ax_table)
    ay = by_class(ay_table)
    base = by_class(base_table)
    spread = jnp.maximum(
        cos_here[None, :, :, None] * cos_lane[:, None, None]
        + sin_here[None, :, :, None] * sin_lane[:, None, None], 0.0)
    wind = (rate_lane[None, None, None] * strength[None, :, :, None]) * (spread * spread)

    arrived, ax, ay, base, wind, matrices = lax.optimization_barrier(
        (arrived, ax, ay, base, wind, matrices))

    info = jnp.concatenate([sweep_order.reshape(-1), half[None].astype(jnp.int32)])
    block = cells + rows_dev
    rim_shapes = [jax.ShapeDtypeStruct((QUADS, size, width), jnp.float32)
                  for size in (block, block, HALO, HALO)]
    rim_own, rim_send, out_same, out_cross = pl.pallas_call(
        partial(rim_kernel, own, rows_dev, comps, quad_size),
        in_specs=[pl.BlockSpec(memory_space=pltpu.SMEM), in_vmem],
        out_specs=[in_vmem] * len(rim_shapes),
        out_shape=rim_shapes,
        compiler_params=pltpu.CompilerParams(vmem_limit_bytes=40 * 2**20),
    )(info, arrived)
    rim_partner = lax.ppermute(rim_send, axes, swap_route)
    rim_same = lax.ppermute(out_same, axes, same_route)
    rim_cross = lax.ppermute(out_cross, axes, cross_route)

    turns = ITERS * QUADS

    def quad_block(shape):
        zeros = (0,) * len(shape)
        return pl.BlockSpec((1,) + shape, lambda t, info: (info[t],) + zeros)

    pairs = QUADS // 2
    packed = jax.ShapeDtypeStruct((quad_size, rows_dev, cols_dev), jnp.float32)
    halves = pl.pallas_call(
        lambda *refs: sweeps_kernel(rows, own, cells, quad_size, *refs),
        grid_spec=pltpu.PrefetchScalarGridSpec(
            num_scalar_prefetch=1,
            grid=(turns,),
            in_specs=[quad_block((rows, cells, width))] * 4
            + [quad_block((width, width)), quad_block((1, width))]
            + [pl.BlockSpec((1, width), lambda t, info: (0, 0))]
            + [quad_block((class_count, width))] * 2 + [quad_block((3, width))]
            + [pl.BlockSpec(memory_space=pltpu.SMEM)]
            + [quad_block((block, width))] * 2
            + [quad_block((HALO, width))] * 2,
            out_specs=[in_vmem] * (2 * pairs),
            scratch_shapes=[
                pltpu.VMEM((QUADS, rows, cells, width), jnp.float32),
                pltpu.VMEM((QUADS, rows, cells, LANES), jnp.float32),
                pltpu.VMEM((2, cells, width), jnp.float32),
                pltpu.VMEM((rows, 2 * HALO, width), jnp.float32),
            ],
        ),
        out_shape=[packed] * (2 * pairs),
        compiler_params=pltpu.CompilerParams(
            dimension_semantics=("arbitrary",), vmem_limit_bytes=49 * 2**20),
    )(info, ax, ay, base, wind, matrices, diagonal, scale[None], ax_table, base_table,
      lane_table, far, rim_own, rim_partner, rim_same, rim_cross)

    got = [lax.ppermute(half_out, axes, swap_route) for half_out in halves[pairs:]]
    chunks = 4
    merged = []
    for pair in range(pairs):
        merged = [pl.pallas_call(
            partial(merge_kernel, own, pair, chunks),
            in_specs=[pl.BlockSpec(memory_space=pltpu.SMEM), in_vmem, in_vmem]
            + [pl.BlockSpec(memory_space=pl.ANY)] * len(merged),
            out_specs=pl.BlockSpec(memory_space=pl.ANY),
            scratch_shapes=[
                pltpu.VMEM((chunks, 2, quad_size // chunks, rows_dev, cols_dev), jnp.float32),
                pltpu.SemaphoreType.DMA((chunks, 2))],
            out_shape=jax.ShapeDtypeStruct((QUADS, quad_size, rows_dev, cols_dev), jnp.float32),
            input_output_aliases={3: 0} if merged else {},
            compiler_params=pltpu.CompilerParams(vmem_limit_bytes=16 * 2**20),
        )(info, halves[pair], got[pair], *merged)]
    return merged[0].reshape(comps, rows_dev, cols_dev)


def solution(mesh):
    placed = (
        P("rows", "cols"),
        P("rows", "cols"),
        P("rows", "cols"),
        P(),
        P(),
        P(),
        P(("rows", "cols"), None),
        P(("rows", "cols")),
        P(),
        P(),
    )
    return jax.shard_map(
        body, mesh=mesh, in_specs=placed, out_specs=P(None, "rows", "cols"), check_vma=False
    )
```

```python
from functools import partial
import math

import jax
import jax.numpy as jnp
import numpy as np
from jax import lax
from jax.experimental import pallas as pl
from jax.experimental.pallas import tpu as pltpu
from jax.sharding import PartitionSpec as P

NDIR = 36
NFREQ = 24
CAP = 16
ITERS = 2
QUADS = 4
LANES = 128
HALO = 8

whitecap_rate = 0.5


def split_bf16(value):
    high = value.astype(jnp.bfloat16)
    low = (value - high.astype(jnp.float32)).astype(jnp.bfloat16)
    return high, low


def lane_scale(width):
    golden = (math.sqrt(5.0) - 1.0) / 2.0
    return np.exp2(np.mod(np.arange(width) * golden, 1.0)).astype(np.float32)


def pad_to(array, axis, size, value=0.0):
    widths = [(0, 0)] * array.ndim
    widths[axis] = (0, size - array.shape[axis])
    return jnp.pad(array, widths, constant_values=value)


def pack_kernel(shifts, col_count, rows, comps, dest_hbm, spectra_hbm, wind_hbm, dir_hbm, class_hbm,
                out_ref, held_ref, dest_ref, spectra_ref, class_ref, high, low, slots, sems):
    step = pl.program_id(0)
    points = dest_ref.shape[1]
    load = out_ref.shape[1]
    total_bits, row_bits, col_bits = shifts

    @pl.when(step == 0)
    def _():
        pieces = ((dest_hbm, dest_ref), (spectra_hbm, spectra_ref), (wind_hbm, held_ref.at[0]),
                  (dir_hbm, held_ref.at[1]), (class_hbm, class_ref))
        copies = [pltpu.make_async_copy(source, target, sems.at[index])
                  for index, (source, target) in enumerate(pieces)]
        for copy in copies:
            copy.start()
        copies[0].wait()
        dest = dest_ref[...]
        grid_row = lax.shift_right_logical(dest, total_bits)
        grid_col = dest & (2**total_bits - 1)
        local_row = grid_row & (2**row_bits - 1)
        local_col = grid_col & (2**col_bits - 1)
        owner = (lax.shift_right_logical(grid_row, row_bits) * col_count
                 + lax.shift_right_logical(grid_col, col_bits))
        on_row = (grid_row == 0) | (grid_row == rows - 1)
        on_left = jnp.where(grid_col == 0, 2**col_bits, 2**col_bits + 2**row_bits) + local_row
        code = jnp.where(on_row, local_col, on_left) + 1
        lanes = jnp.concatenate(
            [owner.astype(jnp.float32), code.astype(jnp.float32), jnp.zeros((6, points), jnp.float32)],
            axis=0)
        columns = lanes.T
        same = columns[:, 0:1] == lanes[0:1]
        above = (lax.broadcasted_iota(jnp.int32, (points, points), 0)
                 < lax.broadcasted_iota(jnp.int32, (points, points), 1))
        rank = jnp.sum(jnp.where(same & above, 1.0, 0.0), axis=0, keepdims=True)
        slots[...] = owner * CAP + rank.astype(jnp.int32)
        for copy in copies[1:]:
            copy.wait()
        held_ref[2] = class_ref[...].astype(jnp.float32)
        spectra = jnp.concatenate(
            [spectra_ref[...], jnp.broadcast_to(lanes[1:2], (load - comps, points))], axis=0)
        high[...], low[...] = split_bf16(spectra)

    place = jnp.where(
        lax.broadcasted_iota(jnp.int32, (out_ref.shape[0], points), 0) + step * out_ref.shape[0]
        == slots[...], 1.0, 0.0).astype(jnp.bfloat16)
    over_points = (((1,), (1,)), ((), ()))
    out_ref[...] = (lax.dot_general(place, high[...], over_points, preferred_element_type=jnp.float32)
                    + lax.dot_general(place, low[...], over_points, preferred_element_type=jnp.float32))


def rim_kernel(own, rows_dev, comps, quad_size, info, arrived_ref, far_ref, own_ref, send_ref, same_ref,
               cross_ref):
    half = info[ITERS * QUADS]
    cols_dev = 2 * own
    cells = own + HALO
    block = cells + rows_dev
    width = own_ref.shape[2]
    load = arrived_ref.shape[1]
    spots = -(-(2 * block + 2 * HALO) // LANES) * LANES
    lane = lax.broadcasted_iota(jnp.int32, (1, spots), 1)
    at_send = lane >= block
    spot = jnp.where(at_send, lane - block, lane)
    side_at = jnp.where(at_send, 1 - half, half)
    want = jnp.where(spot < own, own * side_at + spot, -1)
    want = jnp.where((spot == own) & (side_at == 0), own, want)
    want = jnp.where((spot == cells - 1) & (side_at == 1), own - 1, want)
    want = jnp.where(spot >= cells, cols_dev + rows_dev * side_at + spot - cells, want)
    rest = lane - 2 * block
    to_left = jnp.where((rest == HALO - 1) & (half == 0), cols_dev - 1, -1)
    to_left = jnp.where((rest == 0) & (half == 1), 0, to_left)
    to_left = jnp.where((rest == HALO) & (half == 0), 0, to_left)
    to_left = jnp.where((rest == 2 * HALO - 1) & (half == 1), cols_dev - 1, to_left)
    want = jnp.where(rest >= 0, to_left, want)
    code = arrived_ref[:, comps:comps + 1]
    gather = jnp.where(code == (want + 1).astype(jnp.float32), 1.0, 0.0)
    gather = jnp.where(want >= 0, gather, 0.0).astype(jnp.bfloat16)
    high, low = split_bf16(arrived_ref[...])
    over_points = (((0,), (0,)), ((), ()))
    summed = (lax.dot_general(gather, high, over_points, preferred_element_type=jnp.float32)
              + lax.dot_general(gather, low, over_points, preferred_element_type=jnp.float32))
    for quad in range(QUADS):
        start = quad * quad_size
        part = summed if quad == 0 else pltpu.roll(summed, load - start, 1)
        own_ref[quad] = part[:block, :width]
        send_ref[quad] = part[block:2 * block, :width]
        same_ref[quad, :HALO] = part[2 * block:2 * block + HALO, :width]
        same_ref[quad, HALO:] = far_ref[quad]
        cross_ref[quad] = part[2 * block + HALO:2 * block + 2 * HALO, :width]


def sweeps_kernel(rows, own, cells, quad_size, class_count, info, ax_ref, ay_ref, base_ref,
                  wind_ref, mt_ref, const_ref, own_ref, par_ref, same_ref, cross_ref, *rest):
    pairs = QUADS // 2
    keep_refs, send_refs = rest[:pairs], rest[pairs:2 * pairs]
    state, power, rim, side = rest[2 * pairs:]
    turn = pl.program_id(0)
    quad = info[turn]
    half = info[ITERS * QUADS]
    width = mt_ref.shape[2]
    rows_dev = rows // 2
    ax_table = const_ref[0, :class_count]
    base_table = const_ref[0, class_count:2 * class_count]
    rate_lane, cos_lane, sin_lane, scale_lane, diag_lane = [
        const_ref[0, 2 * class_count + each:2 * class_count + each + 1] for each in range(5)]
    down = (quad == 0) | (quad == 3)
    step_x = jnp.where(down, 1, -1)
    first_row = jnp.where(down, 0, rows - 1)
    up_y = quad < 2

    @pl.when(turn == 0)
    def _():
        power[...] = jnp.zeros_like(power)

    rim[0] = own_ref[quad, 0:cells]
    rim[0, own:cells] = own_ref[quad, own:cells] + same_ref[quad, :HALO]
    rim[1] = par_ref[quad, 0:cells]
    rim[1, own:cells] = par_ref[quad, own:cells] + cross_ref[quad]
    far_at = jnp.where(half == 0, HALO - 1, 0)
    at_far = lax.broadcasted_iota(jnp.int32, (HALO, width), 0) == far_at
    edge_at = jnp.where(half == 0, 0, 2 * HALO - 1)
    at_edge = lax.broadcasted_iota(jnp.int32, (2 * HALO, width), 0) == edge_at
    for j in range(rows_dev):
        mine = jnp.where(at_edge, own_ref[quad, cells + j:cells + j + 1], 0.0)
        theirs = jnp.where(at_edge, par_ref[quad, cells + j:cells + j + 1], 0.0)
        side[j + rows_dev * half] = mine
        side[j + rows_dev * (1 - half)] = theirs

    def run(count, second):
        def patched(block, far_row):
            if second:
                return block
            return jnp.concatenate([block[:own], jnp.where(at_far, far_row, block[own:])], axis=0)

        def factors(i, low, high):
            row = first_row + i * step_x
            kind, strength, far_cos, far_sin = [
                same_ref[feat, pl.ds(HALO + row, 1), :] for feat in range(4)]
            far_ax = jnp.zeros((1, width), jnp.float32)
            far_base = jnp.zeros((1, width), jnp.float32)
            for each in range(class_count):
                far_ax = jnp.where(kind == each, ax_table[each:each + 1], far_ax)
                far_base = jnp.where(kind == each, base_table[each:each + 1], far_base)
            spread = jnp.maximum(far_cos * cos_lane + far_sin * sin_lane, 0.0)
            far_wind = (rate_lane * strength) * (spread * spread)
            total = power[0, row, low:high]
            for other in range(1, QUADS):
                total = total + power[other, row, low:high]
            level = total * (1.0 / (QUADS * quad_size))
            damping = whitecap_rate * level / (1.0 + level)
            den = patched(base_ref[0, row, low:high], far_base) + jnp.concatenate([damping] * (width // LANES), axis=1)
            inverse = scale_lane / den
            source = patched(wind_ref[0, row, low:high], far_wind)
            edge = side[row]
            parts = [source[:HALO] + edge[:HALO], source[HALO:own - HALO],
                     source[own - HALO:own] + edge[HALO:]]
            if high > own:
                parts.append(source[own:])
            source = jnp.concatenate(parts, axis=0)
            if i == 0 or i == rows - 1:
                here = jnp.where(row // rows_dev == half, 0, 1)
                source = source + rim[here, low:high]
            if second:
                before = state[quad, row]
                shifted = jnp.where(up_y, pltpu.roll(before, 1, 0), pltpu.roll(before, cells - 1, 0))
                source = source + ay_ref[0, row, low:high] * shifted[low:high]
            return patched(ax_ref[0, row, low:high], far_ax) * inverse, source * inverse

        def store(i, value):
            row = first_row + i * step_x
            square = value * value
            folded = square[:, :LANES]
            for lane in range(LANES, width, LANES):
                folded = folded + square[:, lane:lane + LANES]
            state[quad, row, :count] = value
            power[quad, row, :count] = jnp.broadcast_to(
                jnp.sum(folded, axis=1, keepdims=True), (count, LANES))

        along, known = factors(0, 0, count)
        upwind = None
        for i in range(rows):
            balance = known if upwind is None else along * upwind + known
            mixed = jnp.dot(balance.astype(jnp.bfloat16), mt_ref[0],
                            preferred_element_type=jnp.float32)
            updated = diag_lane * balance + mixed
            if i + 1 < rows:
                along, known = factors(i + 1, 0, count)
            if i > 0:
                store(i - 1, upwind)
            upwind = updated
        store(rows - 1, upwind)

    @pl.when(turn < QUADS)
    def _():
        run(cells, False)

    @pl.when(turn >= QUADS)
    def _():
        run(own, True)

    @pl.when(turn == ITERS * QUADS - 1)
    def _():
        for pair in range(pairs):
            for j in range(rows_dev):
                for out_ref, side_at in ((keep_refs[pair], half), (send_refs[pair], 1 - half)):
                    row = rows_dev * side_at + j
                    both = jnp.concatenate(
                        [state[2 * pair, row, :own], state[2 * pair + 1, row, :own]], axis=0)
                    out_ref[:, j, :] = both.T[:quad_size]


def merge_kernel(own, pair, chunks, info, keep_ref, got_ref, *rest):
    out_ref, stage, sems = rest[-3:]
    half = info[ITERS * QUADS]
    part = keep_ref.shape[0] // chunks
    copies = []
    for chunk in range(chunks):
        span = pl.ds(chunk * part, part)
        keep = keep_ref[span]
        got = got_ref[span]
        left = jnp.where(half == 0, keep, got)
        right = jnp.where(half == 0, got, keep)
        low = lax.broadcasted_iota(jnp.int32, keep.shape, 2) < own
        stage[chunk, 0] = jnp.where(low, left, pltpu.roll(right, own, 2))
        stage[chunk, 1] = jnp.where(low, pltpu.roll(left, own, 2), right)
        for member in range(2):
            copies.append(pltpu.make_async_copy(
                stage.at[chunk, member], out_ref.at[2 * pair + member, span], sems.at[chunk, member]))
            copies[-1].start()
    for copy in copies:
        copy.wait()


def body(
    wind_speed,
    wind_dir,
    depth_class,
    group_speed,
    dissipation,
    input_rate,
    outer_spectra,
    dest_cell,
    refraction_inverse,
    sweep_order,
):
    rows_dev, cols_dev = wind_speed.shape
    row_count = lax.axis_size("rows")
    col_count = lax.axis_size("cols")
    assert row_count == 2
    devices = row_count * col_count
    rows = rows_dev * row_count
    own = cols_dev // 2
    cells = own + HALO
    class_count = group_speed.shape[0]
    comps = outer_spectra.shape[1]
    quad_size = refraction_inverse.shape[1]
    quarter = NDIR // QUADS
    width = -(-quad_size // LANES) * LANES
    axes = ("rows", "cols")
    half = lax.axis_index("rows")

    def device(row_at, col_at):
        return row_at * col_count + col_at

    span = range(col_count)
    swap_route = [(device(1 - h, c), device(h, c)) for h in range(2) for c in span]
    same_route = [(device(0, c - 1), device(0, c)) for c in span if c > 0]
    same_route += [(device(1, c + 1), device(1, c)) for c in span if c + 1 < col_count]
    cross_route = [(device(1, c - 1), device(0, c)) for c in span if c > 0]
    cross_route += [(device(0, c + 1), device(1, c)) for c in span if c + 1 < col_count]

    points = dest_cell.shape[0]
    load = -(-(comps + 1) // LANES) * LANES
    sizes = (cols_dev * col_count, rows_dev, cols_dev)
    shifts = tuple(size.bit_length() - 1 for size in sizes)
    assert all(size == 2**shift for size, shift in zip(sizes, shifts))
    slot_total = devices * CAP
    steps = 4
    in_vmem = pl.BlockSpec(memory_space=pltpu.VMEM)
    anywhere = pl.BlockSpec(memory_space=pl.ANY)
    outgoing, held = pl.pallas_call(
        partial(pack_kernel, shifts, col_count, rows, comps),
        grid=(steps,),
        in_specs=[anywhere] * 5,
        out_specs=[pl.BlockSpec((slot_total // steps, load), lambda s: (s, 0)), in_vmem],
        scratch_shapes=[pltpu.VMEM((1, points), jnp.int32),
                        pltpu.VMEM((comps, points), jnp.float32),
                        pltpu.VMEM((rows_dev, cols_dev), jnp.int32),
                        pltpu.VMEM((load, points), jnp.bfloat16),
                        pltpu.VMEM((load, points), jnp.bfloat16),
                        pltpu.VMEM((1, points), jnp.int32),
                        pltpu.SemaphoreType.DMA((5,))],
        out_shape=[jax.ShapeDtypeStruct((slot_total, load), jnp.float32),
                   jax.ShapeDtypeStruct((3, rows_dev, cols_dev), jnp.float32)],
        compiler_params=pltpu.CompilerParams(
            dimension_semantics=("arbitrary",), vmem_limit_bytes=48 * 2**20),
    )(dest_cell.reshape(1, points), outer_spectra.T, wind_speed, wind_dir, depth_class)
    outgoing, refraction_inverse = lax.optimization_barrier((outgoing, refraction_inverse))
    scale = jnp.asarray(lane_scale(width))
    flipped = pad_to(pad_to(jnp.swapaxes(refraction_inverse, 1, 2), 1, width), 2, width)
    scaled = flipped / scale[None, :, None]
    on_diag = jnp.eye(width, dtype=bool)[None]
    matrices = jnp.where(on_diag, 0.0, scaled).astype(jnp.bfloat16)
    diagonal = jnp.sum(jnp.where(on_diag, scaled, 0.0), axis=1, keepdims=True)
    arrived = lax.all_to_all(outgoing.reshape(devices, CAP, load), axes, split_axis=0,
                             concat_axis=0, tiled=True).reshape(slot_total, load)

    partner = lax.ppermute(held, axes, swap_route)
    is_low = half == 0
    chip = jnp.concatenate(
        [jnp.where(is_low, held, partner), jnp.where(is_low, partner, held)], axis=1)
    strength = (chip[0] * 0.1) ** 2
    feats = jnp.stack([chip[2], strength, jnp.cos(chip[1]), jnp.sin(chip[1])])
    far_out = jnp.broadcast_to(
        jnp.where(is_low, feats[:, :, cols_dev - 1:], feats[:, :, :1]), (QUADS, rows, width))
    mine = jnp.where(is_low, feats[:, :, :own], feats[:, :, own:])
    right = jnp.where(is_low, feats[:, :, own], 0.0)
    left = jnp.where(is_low, 0.0, feats[:, :, own - 1])
    grid = jnp.concatenate(
        [mine, right[:, :, None], jnp.zeros((4, rows, HALO - 2), jnp.float32), left[:, :, None]], axis=2)
    class_here, strength, cos_here, sin_here = grid[0], grid[1], grid[2], grid[3]

    angle = (jnp.arange(NDIR, dtype=jnp.float32) + 0.5) * (2.0 * math.pi / NDIR)
    cos_lane = pad_to(jnp.repeat(jnp.cos(angle), NFREQ).reshape(QUADS, quad_size), 1, width)
    sin_lane = pad_to(jnp.repeat(jnp.sin(angle), NFREQ).reshape(QUADS, quad_size), 1, width)
    rate_lane = pad_to(jnp.tile(input_rate, quarter), 0, width)
    speed_lane = pad_to(jnp.tile(group_speed, (1, quarter)), 1, width)
    loss_lane = pad_to(jnp.tile(dissipation, (1, quarter)), 1, width, 1.0)
    ax_table = jnp.abs(cos_lane)[:, None] * speed_lane[None]
    ay_table = jnp.abs(sin_lane)[:, None] * speed_lane[None]
    base_table = ax_table + ay_table + loss_lane[None]

    lanes = jnp.stack([jnp.broadcast_to(rate_lane, (QUADS, width)), cos_lane, sin_lane,
                       jnp.broadcast_to(scale, (QUADS, width))], axis=1)
    consts = jnp.concatenate([ax_table, base_table, lanes, diagonal], axis=1)
    consts = pad_to(consts, 1, -(-consts.shape[1] // 8) * 8)

    def by_class(table):
        chosen = jnp.broadcast_to(table[:, None, None, 0], (QUADS, rows, cells, width))
        for kind in range(1, class_count):
            chosen = jnp.where((class_here == kind)[None, :, :, None], table[:, None, None, kind], chosen)
        return chosen

    ax = by_class(ax_table)
    ay = by_class(ay_table)
    base = by_class(base_table)
    spread = jnp.maximum(
        cos_here[None, :, :, None] * cos_lane[:, None, None]
        + sin_here[None, :, :, None] * sin_lane[:, None, None], 0.0)
    wind = (rate_lane[None, None, None] * strength[None, :, :, None]) * (spread * spread)

    arrived, ax, ay, base, wind, matrices = lax.optimization_barrier(
        (arrived, ax, ay, base, wind, matrices))

    info = jnp.concatenate([sweep_order.reshape(-1), half[None].astype(jnp.int32)])
    block = cells + rows_dev
    rim_shapes = [jax.ShapeDtypeStruct((QUADS, size, width), jnp.float32)
                  for size in (block, block, HALO + rows, HALO)]
    rim_own, rim_send, out_same, out_cross = pl.pallas_call(
        partial(rim_kernel, own, rows_dev, comps, quad_size),
        in_specs=[pl.BlockSpec(memory_space=pltpu.SMEM), in_vmem, in_vmem],
        out_specs=[in_vmem] * len(rim_shapes),
        out_shape=rim_shapes,
        compiler_params=pltpu.CompilerParams(vmem_limit_bytes=40 * 2**20),
    )(info, arrived, far_out)
    rim_partner = lax.ppermute(rim_send, axes, swap_route)
    rim_same = lax.ppermute(out_same, axes, same_route)
    rim_cross = lax.ppermute(out_cross, axes, cross_route)

    turns = ITERS * QUADS

    def quad_block(shape):
        zeros = (0,) * len(shape)
        return pl.BlockSpec((1,) + shape, lambda t, info: (info[t],) + zeros)

    pairs = QUADS // 2
    packed = jax.ShapeDtypeStruct((quad_size, rows_dev, cols_dev), jnp.float32)
    halves = pl.pallas_call(
        partial(sweeps_kernel, rows, own, cells, quad_size, class_count),
        grid_spec=pltpu.PrefetchScalarGridSpec(
            num_scalar_prefetch=1,
            grid=(turns,),
            in_specs=[quad_block((rows, cells, width))] * 4
            + [quad_block((width, width)), quad_block(consts.shape[1:])]
            + [in_vmem] * 4,
            out_specs=[in_vmem] * (2 * pairs),
            scratch_shapes=[
                pltpu.VMEM((QUADS, rows, cells, width), jnp.float32),
                pltpu.VMEM((QUADS, rows, cells, LANES), jnp.float32),
                pltpu.VMEM((2, cells, width), jnp.float32),
                pltpu.VMEM((rows, 2 * HALO, width), jnp.float32),
            ],
        ),
        out_shape=[packed] * (2 * pairs),
        compiler_params=pltpu.CompilerParams(
            dimension_semantics=("arbitrary",), vmem_limit_bytes=49 * 2**20),
    )(info, ax, ay, base, wind, matrices, consts, rim_own, rim_partner, rim_same, rim_cross)

    got = [lax.ppermute(half_out, axes, swap_route) for half_out in halves[pairs:]]
    chunks = 4
    merged = []
    for pair in range(pairs):
        merged = [pl.pallas_call(
            partial(merge_kernel, own, pair, chunks),
            in_specs=[pl.BlockSpec(memory_space=pltpu.SMEM), in_vmem, in_vmem]
            + [pl.BlockSpec(memory_space=pl.ANY)] * len(merged),
            out_specs=pl.BlockSpec(memory_space=pl.ANY),
            scratch_shapes=[
                pltpu.VMEM((chunks, 2, quad_size // chunks, rows_dev, cols_dev), jnp.float32),
                pltpu.SemaphoreType.DMA((chunks, 2))],
            out_shape=jax.ShapeDtypeStruct((QUADS, quad_size, rows_dev, cols_dev), jnp.float32),
            input_output_aliases={3: 0} if merged else {},
            compiler_params=pltpu.CompilerParams(vmem_limit_bytes=16 * 2**20),
        )(info, halves[pair], got[pair], *merged)]
    return merged[0].reshape(comps, rows_dev, cols_dev)


def solution(mesh):
    placed = (
        P("rows", "cols"),
        P("rows", "cols"),
        P("rows", "cols"),
        P(),
        P(),
        P(),
        P(("rows", "cols"), None),
        P(("rows", "cols")),
        P(),
        P(),
    )
    return jax.shard_map(
        body, mesh=mesh, in_specs=placed, out_specs=P(None, "rows", "cols"), check_vma=False
    )
```

```python
from functools import partial
import math

import jax
import jax.numpy as jnp
import numpy as np
from jax import lax
from jax.experimental import pallas as pl
from jax.experimental.pallas import tpu as pltpu
from jax.sharding import PartitionSpec as P

NDIR = 36
NFREQ = 24
CAP = 16
ITERS = 2
QUADS = 4
LANES = 128
HALO = 8

whitecap_rate = 0.5


def split_bf16(value):
    high = value.astype(jnp.bfloat16)
    low = (value - high.astype(jnp.float32)).astype(jnp.bfloat16)
    return high, low


def lane_scale(width):
    golden = (math.sqrt(5.0) - 1.0) / 2.0
    return np.exp2(np.mod(np.arange(width) * golden, 1.0)).astype(np.float32)


def pad_to(array, axis, size, value=0.0):
    widths = [(0, 0)] * array.ndim
    widths[axis] = (0, size - array.shape[axis])
    return jnp.pad(array, widths, constant_values=value)


def pack_kernel(total_bits, col_bits, rows, comps, dest_hbm, spectra_hbm, wind_hbm, dir_hbm, class_hbm,
                out_ref, held_ref, dest_ref, spectra_ref, class_ref, high, low, slots, sems):
    step = pl.program_id(0)
    points = dest_ref.shape[1]
    load = out_ref.shape[1]

    @pl.when(step == 0)
    def _():
        pieces = ((dest_hbm, dest_ref), (spectra_hbm, spectra_ref), (wind_hbm, held_ref.at[0]),
                  (dir_hbm, held_ref.at[1]), (class_hbm, class_ref))
        copies = [pltpu.make_async_copy(source, target, sems.at[index])
                  for index, (source, target) in enumerate(pieces)]
        for copy in copies:
            copy.start()
        copies[0].wait()
        dest = dest_ref[...]
        grid_row = lax.shift_right_logical(dest, total_bits)
        grid_col = dest & (2**total_bits - 1)
        owner = lax.shift_right_logical(grid_col, col_bits)
        cols_dev = 2**col_bits
        on_row = jnp.where(grid_row == 0, 0, cols_dev) + (grid_col & (cols_dev - 1))
        on_side = 2 * cols_dev + jnp.where(grid_col == 0, 0, rows) + grid_row
        code = jnp.where((grid_row == 0) | (grid_row == rows - 1), on_row, on_side) + 1
        lanes = jnp.concatenate(
            [owner.astype(jnp.float32), code.astype(jnp.float32), jnp.zeros((6, points), jnp.float32)],
            axis=0)
        columns = lanes.T
        same = columns[:, 0:1] == lanes[0:1]
        above = (lax.broadcasted_iota(jnp.int32, (points, points), 0)
                 < lax.broadcasted_iota(jnp.int32, (points, points), 1))
        rank = jnp.sum(jnp.where(same & above, 1.0, 0.0), axis=0, keepdims=True)
        slots[...] = owner * (2 * CAP) + rank.astype(jnp.int32)
        for copy in copies[1:]:
            copy.wait()
        held_ref[2] = class_ref[...].astype(jnp.float32)
        spectra = jnp.concatenate(
            [spectra_ref[...], jnp.broadcast_to(lanes[1:2], (load - comps, points))], axis=0)
        high[...], low[...] = split_bf16(spectra)

    place = jnp.where(
        lax.broadcasted_iota(jnp.int32, (out_ref.shape[0], points), 0) + step * out_ref.shape[0]
        == slots[...], 1.0, 0.0).astype(jnp.bfloat16)
    over_points = (((1,), (1,)), ((), ()))
    out_ref[...] = (lax.dot_general(place, high[...], over_points, preferred_element_type=jnp.float32)
                    + lax.dot_general(place, low[...], over_points, preferred_element_type=jnp.float32))


def rim_kernel(own, rows, comps, quad_size, info, arrived_ref, own_ref, send_ref):
    half = info[ITERS * QUADS]
    cells = own + HALO
    block = 2 * cells + rows
    width = own_ref.shape[2]
    load = arrived_ref.shape[1]
    spots = -(-2 * block // LANES) * LANES
    lane = lax.broadcasted_iota(jnp.int32, (1, spots), 1)
    at_send = lane >= block
    spot = jnp.where(at_send, lane - block, lane)
    side_at = jnp.where(at_send, 1 - half, half)
    second = spot >= cells
    cell = jnp.where(second, spot - cells, spot)
    col = jnp.where(cell < own, own * side_at + cell, -1)
    col = jnp.where((cell == own) & (side_at == 0), own, col)
    col = jnp.where((cell == cells - 1) & (side_at == 1), own - 1, col)
    want = jnp.where(col >= 0, col + jnp.where(second, 2 * own, 0), -1)
    want = jnp.where(spot >= 2 * cells, 4 * own + rows * side_at + spot - 2 * cells, want)
    want = jnp.where(lane < 2 * block, want, -1)
    code = arrived_ref[:, comps:comps + 1]
    gather = jnp.where(code == (want + 1).astype(jnp.float32), 1.0, 0.0)
    gather = jnp.where(want >= 0, gather, 0.0).astype(jnp.bfloat16)
    high, low = split_bf16(arrived_ref[...])
    over_points = (((0,), (0,)), ((), ()))
    summed = (lax.dot_general(gather, high, over_points, preferred_element_type=jnp.float32)
              + lax.dot_general(gather, low, over_points, preferred_element_type=jnp.float32))
    for quad in range(QUADS):
        start = quad * quad_size
        part = summed if quad == 0 else pltpu.roll(summed, load - start, 1)
        own_ref[quad] = part[:block, :width]
        send_ref[quad] = part[block:2 * block, :width]


def edge_kernel(own, info, own_ref, par_ref, far_ref, out_ref):
    low = info[ITERS * QUADS] == 0
    cells = own + HALO
    total = own_ref[...] + par_ref[...]
    out_ref[...] = jnp.zeros_like(out_ref)
    for row in range(2):
        first = total[:, cells * row:cells * row + 1]
        last = total[:, cells * row + own - 1:cells * row + own]
        out_ref[:, row:row + 1] = jnp.where(low, first, last)
    out_ref[:, HALO:] = far_ref[...]


def sweeps_kernel(rows, own, cells, quad_size, class_count, info, ax_ref, ay_ref, base_ref,
                  wind_ref, mt_ref, const_ref, own_ref, par_ref, far_ref, *rest):
    pairs = QUADS // 2
    keep_refs, send_refs = rest[:pairs], rest[pairs:2 * pairs]
    state, power, rim, side = rest[2 * pairs:]
    turn = pl.program_id(0)
    quad = info[turn]
    half = info[ITERS * QUADS]
    width = mt_ref.shape[2]
    rows_dev = rows // 2
    ax_table = const_ref[0, :class_count]
    base_table = const_ref[0, class_count:2 * class_count]
    rate_lane, cos_lane, sin_lane, scale_lane, diag_lane = [
        const_ref[0, 2 * class_count + each:2 * class_count + each + 1] for each in range(5)]
    down = (quad == 0) | (quad == 3)
    step_x = jnp.where(down, 1, -1)
    first_row = jnp.where(down, 0, rows - 1)
    up_y = quad < 2

    @pl.when(turn == 0)
    def _():
        power[...] = jnp.zeros_like(power)

    far_at = jnp.where(half == 0, HALO - 1, 0)
    at_far = lax.broadcasted_iota(jnp.int32, (HALO, width), 0) == far_at
    for j in range(2):
        here = own_ref[quad, j * cells:(j + 1) * cells] + par_ref[quad, j * cells:(j + 1) * cells]
        rim[j, :own] = here[:own]
        rim[j, own:] = here[own:] + jnp.where(at_far, far_ref[quad, j:j + 1], 0.0)
    edge_at = jnp.where(half == 0, 0, 2 * HALO - 1)
    at_edge = lax.broadcasted_iota(jnp.int32, (2 * HALO, width), 0) == edge_at
    beside_edge = own_ref[quad, 2 * cells:] + par_ref[quad, 2 * cells:]
    for j in range(rows):
        side[j] = jnp.where(at_edge, beside_edge[j:j + 1], 0.0)

    def run(count, second):
        def patched(block, far_row):
            if second:
                return block
            return jnp.concatenate([block[:own], jnp.where(at_far, far_row, block[own:])], axis=0)

        def factors(i, low, high):
            row = first_row + i * step_x
            kind, strength, far_cos, far_sin = [
                far_ref[feat, pl.ds(HALO + row, 1), :] for feat in range(4)]
            far_ax = jnp.zeros((1, width), jnp.float32)
            far_base = jnp.zeros((1, width), jnp.float32)
            for each in range(class_count):
                far_ax = jnp.where(kind == each, ax_table[each:each + 1], far_ax)
                far_base = jnp.where(kind == each, base_table[each:each + 1], far_base)
            spread = jnp.maximum(far_cos * cos_lane + far_sin * sin_lane, 0.0)
            far_wind = (rate_lane * strength) * (spread * spread)
            total = power[0, row, low:high]
            for other in range(1, QUADS):
                total = total + power[other, row, low:high]
            level = total * (1.0 / (QUADS * quad_size))
            damping = whitecap_rate * level / (1.0 + level)
            den = patched(base_ref[0, row, low:high], far_base) + jnp.concatenate([damping] * (width // LANES), axis=1)
            inverse = scale_lane / den
            source = patched(wind_ref[0, row, low:high], far_wind)
            edge = side[row]
            parts = [source[:HALO] + edge[:HALO], source[HALO:own - HALO],
                     source[own - HALO:own] + edge[HALO:]]
            if high > own:
                parts.append(source[own:])
            source = jnp.concatenate(parts, axis=0)
            if i == 0 or i == rows - 1:
                here = jnp.where(row == 0, 0, 1)
                source = source + rim[here, low:high]
            if second:
                before = state[quad, row]
                shifted = jnp.where(up_y, pltpu.roll(before, 1, 0), pltpu.roll(before, cells - 1, 0))
                source = source + ay_ref[0, row, low:high] * shifted[low:high]
            return patched(ax_ref[0, row, low:high], far_ax) * inverse, source * inverse

        def store(i, value):
            row = first_row + i * step_x
            square = value * value
            folded = square[:, :LANES]
            for lane in range(LANES, width, LANES):
                folded = folded + square[:, lane:lane + LANES]
            state[quad, row, :count] = value
            power[quad, row, :count] = jnp.broadcast_to(
                jnp.sum(folded, axis=1, keepdims=True), (count, LANES))

        along, known = factors(0, 0, count)
        upwind = None
        for i in range(rows):
            balance = known if upwind is None else along * upwind + known
            mixed = jnp.dot(balance.astype(jnp.bfloat16), mt_ref[0],
                            preferred_element_type=jnp.float32)
            updated = diag_lane * balance + mixed
            if i + 1 < rows:
                along, known = factors(i + 1, 0, count)
            if i > 0:
                store(i - 1, upwind)
            upwind = updated
        store(rows - 1, upwind)

    @pl.when(turn < QUADS)
    def _():
        run(cells, False)

    @pl.when(turn >= QUADS)
    def _():
        run(own, True)

    @pl.when(turn == ITERS * QUADS - 1)
    def _():
        for pair in range(pairs):
            for j in range(rows_dev):
                for out_ref, side_at in ((keep_refs[pair], half), (send_refs[pair], 1 - half)):
                    row = rows_dev * side_at + j
                    both = jnp.concatenate(
                        [state[2 * pair, row, :own], state[2 * pair + 1, row, :own]], axis=0)
                    out_ref[:, j, :] = both.T[:quad_size]


def merge_kernel(own, pair, chunks, info, keep_ref, got_ref, *rest):
    out_ref, stage, sems = rest[-3:]
    half = info[ITERS * QUADS]
    part = keep_ref.shape[0] // chunks
    copies = []
    for chunk in range(chunks):
        span = pl.ds(chunk * part, part)
        keep = keep_ref[span]
        got = got_ref[span]
        left = jnp.where(half == 0, keep, got)
        right = jnp.where(half == 0, got, keep)
        low = lax.broadcasted_iota(jnp.int32, keep.shape, 2) < own
        stage[chunk, 0] = jnp.where(low, left, pltpu.roll(right, own, 2))
        stage[chunk, 1] = jnp.where(low, pltpu.roll(left, own, 2), right)
        for member in range(2):
            copies.append(pltpu.make_async_copy(
                stage.at[chunk, member], out_ref.at[2 * pair + member, span], sems.at[chunk, member]))
            copies[-1].start()
    for copy in copies:
        copy.wait()


def body(
    wind_speed,
    wind_dir,
    depth_class,
    group_speed,
    dissipation,
    input_rate,
    outer_spectra,
    dest_cell,
    refraction_inverse,
    sweep_order,
):
    rows_dev, cols_dev = wind_speed.shape
    row_count = lax.axis_size("rows")
    col_count = lax.axis_size("cols")
    assert row_count == 2
    rows = rows_dev * row_count
    own = cols_dev // 2
    cells = own + HALO
    class_count = group_speed.shape[0]
    comps = outer_spectra.shape[1]
    quad_size = refraction_inverse.shape[1]
    quarter = NDIR // QUADS
    width = -(-quad_size // LANES) * LANES
    axes = ("rows", "cols")
    half = lax.axis_index("rows")

    def device(row_at, col_at):
        return row_at * col_count + col_at

    span = range(col_count)
    swap_route = [(device(1 - h, c), device(h, c)) for h in range(2) for c in span]
    cross_route = [(device(1, c - 1), device(0, c)) for c in span if c > 0]
    cross_route += [(device(0, c + 1), device(1, c)) for c in span if c + 1 < col_count]

    points = dest_cell.shape[0]
    load = -(-(comps + 1) // LANES) * LANES
    total_bits, col_bits = [(size.bit_length() - 1) for size in (cols_dev * col_count, cols_dev)]
    assert cols_dev == 2**col_bits and cols_dev * col_count == 2**total_bits
    slot_total = col_count * 2 * CAP
    steps = 4
    in_vmem = pl.BlockSpec(memory_space=pltpu.VMEM)
    anywhere = pl.BlockSpec(memory_space=pl.ANY)
    outgoing, held = pl.pallas_call(
        partial(pack_kernel, total_bits, col_bits, rows, comps),
        grid=(steps,),
        in_specs=[anywhere] * 5,
        out_specs=[pl.BlockSpec((slot_total // steps, load), lambda s: (s, 0)), in_vmem],
        scratch_shapes=[pltpu.VMEM((1, points), jnp.int32),
                        pltpu.VMEM((comps, points), jnp.float32),
                        pltpu.VMEM((rows_dev, cols_dev), jnp.int32),
                        pltpu.VMEM((load, points), jnp.bfloat16),
                        pltpu.VMEM((load, points), jnp.bfloat16),
                        pltpu.VMEM((1, points), jnp.int32),
                        pltpu.SemaphoreType.DMA((5,))],
        out_shape=[jax.ShapeDtypeStruct((slot_total, load), jnp.float32),
                   jax.ShapeDtypeStruct((3, rows_dev, cols_dev), jnp.float32)],
        compiler_params=pltpu.CompilerParams(
            dimension_semantics=("arbitrary",), vmem_limit_bytes=60 * 2**20),
    )(dest_cell.reshape(1, points), outer_spectra.T, wind_speed, wind_dir, depth_class)
    outgoing, refraction_inverse = lax.optimization_barrier((outgoing, refraction_inverse))
    scale = jnp.asarray(lane_scale(width))
    flipped = pad_to(pad_to(jnp.swapaxes(refraction_inverse, 1, 2), 1, width), 2, width)
    scaled = flipped / scale[None, :, None]
    on_diag = jnp.eye(width, dtype=bool)[None]
    matrices = jnp.where(on_diag, 0.0, scaled).astype(jnp.bfloat16)
    diagonal = jnp.sum(jnp.where(on_diag, scaled, 0.0), axis=1, keepdims=True)
    arrived = lax.all_to_all(outgoing.reshape(col_count, 2 * CAP, load), "cols", split_axis=0,
                             concat_axis=0, tiled=True).reshape(slot_total, load)

    partner = lax.ppermute(held, axes, swap_route)
    is_low = half == 0
    chip = jnp.concatenate(
        [jnp.where(is_low, held, partner), jnp.where(is_low, partner, held)], axis=1)
    strength = (chip[0] * 0.1) ** 2
    feats = jnp.stack([chip[2], strength, jnp.cos(chip[1]), jnp.sin(chip[1])])
    far_out = jnp.broadcast_to(
        jnp.where(is_low, feats[:, :, :1], feats[:, :, cols_dev - 1:]), (QUADS, rows, width))
    mine = jnp.where(is_low, feats[:, :, :own], feats[:, :, own:])
    right = jnp.where(is_low, feats[:, :, own], 0.0)
    left = jnp.where(is_low, 0.0, feats[:, :, own - 1])
    grid = jnp.concatenate(
        [mine, right[:, :, None], jnp.zeros((4, rows, HALO - 2), jnp.float32), left[:, :, None]], axis=2)
    class_here, strength, cos_here, sin_here = grid[0], grid[1], grid[2], grid[3]

    angle = (jnp.arange(NDIR, dtype=jnp.float32) + 0.5) * (2.0 * math.pi / NDIR)
    cos_lane = pad_to(jnp.repeat(jnp.cos(angle), NFREQ).reshape(QUADS, quad_size), 1, width)
    sin_lane = pad_to(jnp.repeat(jnp.sin(angle), NFREQ).reshape(QUADS, quad_size), 1, width)
    rate_lane = pad_to(jnp.tile(input_rate, quarter), 0, width)
    speed_lane = pad_to(jnp.tile(group_speed, (1, quarter)), 1, width)
    loss_lane = pad_to(jnp.tile(dissipation, (1, quarter)), 1, width, 1.0)
    ax_table = jnp.abs(cos_lane)[:, None] * speed_lane[None]
    ay_table = jnp.abs(sin_lane)[:, None] * speed_lane[None]
    base_table = ax_table + ay_table + loss_lane[None]

    lanes = jnp.stack([jnp.broadcast_to(rate_lane, (QUADS, width)), cos_lane, sin_lane,
                       jnp.broadcast_to(scale, (QUADS, width))], axis=1)
    consts = jnp.concatenate([ax_table, base_table, lanes, diagonal], axis=1)
    consts = pad_to(consts, 1, -(-consts.shape[1] // 8) * 8)

    def by_class(table):
        chosen = jnp.broadcast_to(table[:, None, None, 0], (QUADS, rows, cells, width))
        for kind in range(1, class_count):
            chosen = jnp.where((class_here == kind)[None, :, :, None], table[:, None, None, kind], chosen)
        return chosen

    ax = by_class(ax_table)
    ay = by_class(ay_table)
    base = by_class(base_table)
    spread = jnp.maximum(
        cos_here[None, :, :, None] * cos_lane[:, None, None]
        + sin_here[None, :, :, None] * sin_lane[:, None, None], 0.0)
    wind = (rate_lane[None, None, None] * strength[None, :, :, None]) * (spread * spread)

    arrived, ax, ay, base, wind, matrices = lax.optimization_barrier(
        (arrived, ax, ay, base, wind, matrices))

    info = jnp.concatenate([sweep_order.reshape(-1), half[None].astype(jnp.int32)])
    block = 2 * cells + rows
    in_smem = pl.BlockSpec(memory_space=pltpu.SMEM)
    rim_shape = jax.ShapeDtypeStruct((QUADS, block, width), jnp.float32)
    rim_own, rim_send = pl.pallas_call(
        partial(rim_kernel, own, rows, comps, quad_size),
        in_specs=[in_smem, in_vmem],
        out_specs=[in_vmem] * 2,
        out_shape=[rim_shape] * 2,
        compiler_params=pltpu.CompilerParams(vmem_limit_bytes=40 * 2**20),
    )(info, arrived)
    rim_partner = lax.ppermute(rim_send, axes, swap_route)
    edge = pl.pallas_call(
        partial(edge_kernel, own),
        in_specs=[in_smem] + [in_vmem] * 3,
        out_specs=in_vmem,
        out_shape=jax.ShapeDtypeStruct((QUADS, HALO + rows, width), jnp.float32),
    )(info, rim_own, rim_partner, far_out)
    far = lax.ppermute(edge, axes, cross_route)

    turns = ITERS * QUADS

    def quad_block(shape):
        zeros = (0,) * len(shape)
        return pl.BlockSpec((1,) + shape, lambda t, info: (info[t],) + zeros)

    pairs = QUADS // 2
    packed = jax.ShapeDtypeStruct((quad_size, rows_dev, cols_dev), jnp.float32)
    halves = pl.pallas_call(
        partial(sweeps_kernel, rows, own, cells, quad_size, class_count),
        grid_spec=pltpu.PrefetchScalarGridSpec(
            num_scalar_prefetch=1,
            grid=(turns,),
            in_specs=[quad_block((rows, cells, width))] * 4
            + [quad_block((width, width)), quad_block(consts.shape[1:])]
            + [in_vmem] * 3,
            out_specs=[in_vmem] * (2 * pairs),
            scratch_shapes=[
                pltpu.VMEM((QUADS, rows, cells, width), jnp.float32),
                pltpu.VMEM((QUADS, rows, cells, LANES), jnp.float32),
                pltpu.VMEM((2, cells, width), jnp.float32),
                pltpu.VMEM((rows, 2 * HALO, width), jnp.float32),
            ],
        ),
        out_shape=[packed] * (2 * pairs),
        compiler_params=pltpu.CompilerParams(
            dimension_semantics=("arbitrary",), vmem_limit_bytes=49 * 2**20),
    )(info, ax, ay, base, wind, matrices, consts, rim_own, rim_partner, far)

    got = [lax.ppermute(half_out, axes, swap_route) for half_out in halves[pairs:]]
    chunks = 4
    merged = []
    for pair in range(pairs):
        merged = [pl.pallas_call(
            partial(merge_kernel, own, pair, chunks),
            in_specs=[in_smem, in_vmem, in_vmem]
            + [pl.BlockSpec(memory_space=pl.ANY)] * len(merged),
            out_specs=pl.BlockSpec(memory_space=pl.ANY),
            scratch_shapes=[
                pltpu.VMEM((chunks, 2, quad_size // chunks, rows_dev, cols_dev), jnp.float32),
                pltpu.SemaphoreType.DMA((chunks, 2))],
            out_shape=jax.ShapeDtypeStruct((QUADS, quad_size, rows_dev, cols_dev), jnp.float32),
            input_output_aliases={3: 0} if merged else {},
            compiler_params=pltpu.CompilerParams(vmem_limit_bytes=16 * 2**20),
        )(info, halves[pair], got[pair], *merged)]
    return merged[0].reshape(comps, rows_dev, cols_dev)


def solution(mesh):
    placed = (
        P("rows", "cols"),
        P("rows", "cols"),
        P("rows", "cols"),
        P(),
        P(),
        P(),
        P(("rows", "cols"), None),
        P(("rows", "cols")),
        P(),
        P(),
    )
    return jax.shard_map(
        body, mesh=mesh, in_specs=placed, out_specs=P(None, "rows", "cols"), check_vma=False
    )
```

```python
from functools import partial
import math

import jax
import jax.numpy as jnp
import numpy as np
from jax import lax
from jax.experimental import pallas as pl
from jax.experimental.pallas import tpu as pltpu
from jax.sharding import PartitionSpec as P

NDIR = 36
NFREQ = 24
CAP = 16
ITERS = 2
QUADS = 4
LANES = 128
HALO = 8

whitecap_rate = 0.5


def split_bf16(value):
    high = value.astype(jnp.bfloat16)
    low = (value - high.astype(jnp.float32)).astype(jnp.bfloat16)
    return high, low


def lane_scale(width):
    golden = (math.sqrt(5.0) - 1.0) / 2.0
    return np.exp2(np.mod(np.arange(width) * golden, 1.0)).astype(np.float32)


def pad_to(array, axis, size, value=0.0):
    widths = [(0, 0)] * array.ndim
    widths[axis] = (0, size - array.shape[axis])
    return jnp.pad(array, widths, constant_values=value)


def pack_kernel(shifts, col_count, rows, comps, dest_hbm, spectra_hbm, wind_hbm, dir_hbm, class_hbm,
                out_ref, held_ref, dest_ref, spectra_ref, class_ref, high, low, slots, sems):
    step = pl.program_id(0)
    points = dest_ref.shape[1]
    load = out_ref.shape[1]
    total_bits, row_bits, col_bits = shifts

    @pl.when(step == 0)
    def _():
        pieces = ((dest_hbm, dest_ref), (spectra_hbm, spectra_ref), (wind_hbm, held_ref.at[0]),
                  (dir_hbm, held_ref.at[1]), (class_hbm, class_ref))
        copies = [pltpu.make_async_copy(source, target, sems.at[index])
                  for index, (source, target) in enumerate(pieces)]
        for copy in copies:
            copy.start()
        copies[0].wait()
        dest = dest_ref[...]
        grid_row = lax.shift_right_logical(dest, total_bits)
        grid_col = dest & (2**total_bits - 1)
        local_row = grid_row & (2**row_bits - 1)
        local_col = grid_col & (2**col_bits - 1)
        owner = (lax.shift_right_logical(grid_row, row_bits) * col_count
                 + lax.shift_right_logical(grid_col, col_bits))
        on_row = (grid_row == 0) | (grid_row == rows - 1)
        on_left = jnp.where(grid_col == 0, 2**col_bits, 2**col_bits + 2**row_bits) + local_row
        code = jnp.where(on_row, local_col, on_left) + 1
        lanes = jnp.concatenate(
            [owner.astype(jnp.float32), code.astype(jnp.float32), jnp.zeros((6, points), jnp.float32)],
            axis=0)
        columns = lanes.T
        same = columns[:, 0:1] == lanes[0:1]
        above = (lax.broadcasted_iota(jnp.int32, (points, points), 0)
                 < lax.broadcasted_iota(jnp.int32, (points, points), 1))
        rank = jnp.sum(jnp.where(same & above, 1.0, 0.0), axis=0, keepdims=True)
        slots[...] = owner * CAP + rank.astype(jnp.int32)
        for copy in copies[1:]:
            copy.wait()
        held_ref[2] = class_ref[...].astype(jnp.float32)
        spectra = jnp.concatenate(
            [spectra_ref[...], jnp.broadcast_to(lanes[1:2], (load - comps, points))], axis=0)
        high[...], low[...] = split_bf16(spectra)

    place = jnp.where(
        lax.broadcasted_iota(jnp.int32, (out_ref.shape[0], points), 0) + step * out_ref.shape[0]
        == slots[...], 1.0, 0.0).astype(jnp.bfloat16)
    over_points = (((1,), (1,)), ((), ()))
    out_ref[...] = (lax.dot_general(place, high[...], over_points, preferred_element_type=jnp.float32)
                    + lax.dot_general(place, low[...], over_points, preferred_element_type=jnp.float32))


def rim_kernel(own, rows_dev, comps, quad_size, info, arrived_ref, far_ref, own_ref, send_ref, same_ref,
               cross_ref):
    half = info[ITERS * QUADS]
    cols_dev = 2 * own
    cells = own + HALO
    block = cells + rows_dev
    width = own_ref.shape[2]
    load = arrived_ref.shape[1]
    spots = -(-(2 * block + 2 * HALO) // LANES) * LANES
    lane = lax.broadcasted_iota(jnp.int32, (1, spots), 1)
    at_send = lane >= block
    spot = jnp.where(at_send, lane - block, lane)
    side_at = jnp.where(at_send, 1 - half, half)
    want = jnp.where(spot < own, own * side_at + spot, -1)
    want = jnp.where((spot == own) & (side_at == 0), own, want)
    want = jnp.where((spot == cells - 1) & (side_at == 1), own - 1, want)
    want = jnp.where(spot >= cells, cols_dev + rows_dev * side_at + spot - cells, want)
    rest = lane - 2 * block
    to_left = jnp.where((rest == HALO - 1) & (half == 0), cols_dev - 1, -1)
    to_left = jnp.where((rest == 0) & (half == 1), 0, to_left)
    to_left = jnp.where((rest == HALO) & (half == 0), 0, to_left)
    to_left = jnp.where((rest == 2 * HALO - 1) & (half == 1), cols_dev - 1, to_left)
    want = jnp.where(rest >= 0, to_left, want)
    code = arrived_ref[:, comps:comps + 1]
    gather = jnp.where(code == (want + 1).astype(jnp.float32), 1.0, 0.0)
    gather = jnp.where(want >= 0, gather, 0.0).astype(jnp.bfloat16)
    high, low = split_bf16(arrived_ref[...])
    over_points = (((0,), (0,)), ((), ()))
    summed = (lax.dot_general(gather, high, over_points, preferred_element_type=jnp.float32)
              + lax.dot_general(gather, low, over_points, preferred_element_type=jnp.float32))
    for quad in range(QUADS):
        start = quad * quad_size
        part = summed if quad == 0 else pltpu.roll(summed, load - start, 1)
        own_ref[quad] = part[:block, :width]
        send_ref[quad] = part[block:2 * block, :width]
        halo = part[2 * block:2 * block + HALO, :width]
        free = lax.broadcasted_iota(jnp.int32, halo.shape, 1) >= quad_size
        same_ref[quad] = jnp.where(free, far_ref[quad], halo)
        cross_ref[quad] = part[2 * block + HALO:2 * block + 2 * HALO, :width]


def sweeps_kernel(rows, own, cells, quad_size, class_count, info, ax_ref, base_ref,
                  wind_ref, mt_ref, const_ref, own_ref, par_ref, same_ref, cross_ref, *rest):
    pairs = QUADS // 2
    keep_refs, send_refs = rest[:pairs], rest[pairs:2 * pairs]
    state, power, rim, side, far_rows = rest[2 * pairs:]
    turn = pl.program_id(0)
    quad = info[turn]
    half = info[ITERS * QUADS]
    width = mt_ref.shape[2]
    rows_dev = rows // 2
    ax_table = const_ref[0, :class_count]
    base_table = const_ref[0, class_count:2 * class_count]
    rate_lane, cos_lane, sin_lane, scale_lane, ratio_lane, diag_lane = [
        const_ref[0, 2 * class_count + each:2 * class_count + each + 1] for each in range(6)]
    down = (quad == 0) | (quad == 3)
    step_x = jnp.where(down, 1, -1)
    first_row = jnp.where(down, 0, rows - 1)
    up_y = quad < 2

    @pl.when(turn == 0)
    def _():
        power[...] = jnp.zeros_like(power)
        numbers = jnp.concatenate(
            [same_ref[feat, 0:1, width - LANES:] for feat in range(4)]
            + [jnp.zeros((4, LANES), jnp.float32)], axis=0).T
        for feat in range(4):
            far_rows[feat] = jnp.broadcast_to(
                numbers[LANES - rows:, feat:feat + 1], (rows, width))

    rim[0] = own_ref[quad, 0:cells]
    rim[0, own:cells] = own_ref[quad, own:cells] + same_ref[quad]
    rim[1] = par_ref[quad, 0:cells]
    rim[1, own:cells] = par_ref[quad, own:cells] + cross_ref[quad]
    far_at = jnp.where(half == 0, HALO - 1, 0)
    at_far = lax.broadcasted_iota(jnp.int32, (HALO, width), 0) == far_at
    edge_at = jnp.where(half == 0, 0, 2 * HALO - 1)
    at_edge = lax.broadcasted_iota(jnp.int32, (2 * HALO, width), 0) == edge_at
    for j in range(rows_dev):
        mine = jnp.where(at_edge, own_ref[quad, cells + j:cells + j + 1], 0.0)
        theirs = jnp.where(at_edge, par_ref[quad, cells + j:cells + j + 1], 0.0)
        side[j + rows_dev * half] = mine
        side[j + rows_dev * (1 - half)] = theirs

    def run(count, second):
        def patched(block, far_row):
            if second:
                return block
            return jnp.concatenate([block[:own], jnp.where(at_far, far_row, block[own:])], axis=0)

        def factors(i, low, high):
            row = first_row + i * step_x
            kind, strength, far_cos, far_sin = [
                far_rows[feat, pl.ds(row, 1), :] for feat in range(4)]
            far_ax = jnp.zeros((1, width), jnp.float32)
            far_base = jnp.zeros((1, width), jnp.float32)
            for each in range(class_count):
                far_ax = jnp.where(kind == each, ax_table[each:each + 1], far_ax)
                far_base = jnp.where(kind == each, base_table[each:each + 1], far_base)
            spread = jnp.maximum(far_cos * cos_lane + far_sin * sin_lane, 0.0)
            far_wind = (rate_lane * strength) * (spread * spread)
            total = power[0, row, low:high]
            for other in range(1, QUADS):
                total = total + power[other, row, low:high]
            level = total * (1.0 / (QUADS * quad_size))
            damping = whitecap_rate * level / (1.0 + level)
            den = patched(base_ref[0, row, low:high], far_base) + jnp.concatenate([damping] * (width // LANES), axis=1)
            inverse = scale_lane / den
            source = patched(wind_ref[0, row, low:high], far_wind)
            edge = side[row]
            parts = [source[:HALO] + edge[:HALO], source[HALO:own - HALO],
                     source[own - HALO:own] + edge[HALO:]]
            if high > own:
                parts.append(source[own:])
            source = jnp.concatenate(parts, axis=0)
            if i == 0 or i == rows - 1:
                here = jnp.where(row // rows_dev == half, 0, 1)
                source = source + rim[here, low:high]
            if second:
                before = state[quad, row]
                shifted = jnp.where(up_y, pltpu.roll(before, 1, 0), pltpu.roll(before, cells - 1, 0))
                source = source + ax_ref[0, row, low:high] * (ratio_lane * shifted[low:high])
            return patched(ax_ref[0, row, low:high], far_ax) * inverse, source * inverse

        def store(i, value):
            row = first_row + i * step_x
            square = value * value
            folded = square[:, :LANES]
            for lane in range(LANES, width, LANES):
                folded = folded + square[:, lane:lane + LANES]
            state[quad, row, :count] = value
            power[quad, row, :count] = jnp.broadcast_to(
                jnp.sum(folded, axis=1, keepdims=True), (count, LANES))

        balance = factors(0, 0, count)[1]
        upwind = None
        for i in range(rows):
            mixed = jnp.dot(balance.astype(jnp.bfloat16), mt_ref[0],
                            preferred_element_type=jnp.float32)
            direct = diag_lane * balance
            if i + 1 < rows:
                along, known = factors(i + 1, 0, count)
                balance = along * mixed + (along * direct + known)
            if i > 0:
                store(i - 1, upwind)
            upwind = direct + mixed
        store(rows - 1, upwind)

    @pl.when(turn < QUADS)
    def _():
        run(cells, False)

    @pl.when(turn >= QUADS)
    def _():
        run(own, True)

    @pl.when(turn == ITERS * QUADS - 1)
    def _():
        for pair in range(pairs):
            for j in range(rows_dev):
                for out_ref, side_at in ((keep_refs[pair], half), (send_refs[pair], 1 - half)):
                    row = rows_dev * side_at + j
                    both = jnp.concatenate(
                        [state[2 * pair, row, :own], state[2 * pair + 1, row, :own]], axis=0)
                    out_ref[:, j, :] = both.T[:quad_size]


def merge_kernel(own, pair, chunks, info, keep_ref, got_ref, *rest):
    out_ref, stage, sems = rest[-3:]
    half = info[ITERS * QUADS]
    part = keep_ref.shape[0] // chunks
    copies = []
    for chunk in range(chunks):
        span = pl.ds(chunk * part, part)
        keep = keep_ref[span]
        got = got_ref[span]
        left = jnp.where(half == 0, keep, got)
        right = jnp.where(half == 0, got, keep)
        low = lax.broadcasted_iota(jnp.int32, keep.shape, 2) < own
        stage[chunk, 0] = jnp.where(low, left, pltpu.roll(right, own, 2))
        stage[chunk, 1] = jnp.where(low, pltpu.roll(left, own, 2), right)
        for member in range(2):
            copies.append(pltpu.make_async_copy(
                stage.at[chunk, member], out_ref.at[2 * pair + member, span], sems.at[chunk, member]))
            copies[-1].start()
    for copy in copies:
        copy.wait()


def body(
    wind_speed,
    wind_dir,
    depth_class,
    group_speed,
    dissipation,
    input_rate,
    outer_spectra,
    dest_cell,
    refraction_inverse,
    sweep_order,
):
    rows_dev, cols_dev = wind_speed.shape
    row_count = lax.axis_size("rows")
    col_count = lax.axis_size("cols")
    assert row_count == 2
    devices = row_count * col_count
    rows = rows_dev * row_count
    own = cols_dev // 2
    cells = own + HALO
    class_count = group_speed.shape[0]
    comps = outer_spectra.shape[1]
    quad_size = refraction_inverse.shape[1]
    quarter = NDIR // QUADS
    width = -(-quad_size // LANES) * LANES
    axes = ("rows", "cols")
    half = lax.axis_index("rows")

    def device(row_at, col_at):
        return row_at * col_count + col_at

    span = range(col_count)
    swap_route = [(device(1 - h, c), device(h, c)) for h in range(2) for c in span]
    same_route = [(device(0, c - 1), device(0, c)) for c in span if c > 0]
    same_route += [(device(1, c + 1), device(1, c)) for c in span if c + 1 < col_count]
    cross_route = [(device(1, c - 1), device(0, c)) for c in span if c > 0]
    cross_route += [(device(0, c + 1), device(1, c)) for c in span if c + 1 < col_count]

    points = dest_cell.shape[0]
    load = -(-(comps + 1) // LANES) * LANES
    sizes = (cols_dev * col_count, rows_dev, cols_dev)
    shifts = tuple(size.bit_length() - 1 for size in sizes)
    assert all(size == 2**shift for size, shift in zip(sizes, shifts))
    slot_total = devices * CAP
    steps = 4
    in_vmem = pl.BlockSpec(memory_space=pltpu.VMEM)
    anywhere = pl.BlockSpec(memory_space=pl.ANY)
    outgoing, held = pl.pallas_call(
        partial(pack_kernel, shifts, col_count, rows, comps),
        grid=(steps,),
        in_specs=[anywhere] * 5,
        out_specs=[pl.BlockSpec((slot_total // steps, load), lambda s: (s, 0)), in_vmem],
        scratch_shapes=[pltpu.VMEM((1, points), jnp.int32),
                        pltpu.VMEM((comps, points), jnp.float32),
                        pltpu.VMEM((rows_dev, cols_dev), jnp.int32),
                        pltpu.VMEM((load, points), jnp.bfloat16),
                        pltpu.VMEM((load, points), jnp.bfloat16),
                        pltpu.VMEM((1, points), jnp.int32),
                        pltpu.SemaphoreType.DMA((5,))],
        out_shape=[jax.ShapeDtypeStruct((slot_total, load), jnp.float32),
                   jax.ShapeDtypeStruct((3, rows_dev, cols_dev), jnp.float32)],
        compiler_params=pltpu.CompilerParams(
            dimension_semantics=("arbitrary",), vmem_limit_bytes=60 * 2**20),
    )(dest_cell.reshape(1, points), outer_spectra.T, wind_speed, wind_dir, depth_class)
    outgoing, refraction_inverse = lax.optimization_barrier((outgoing, refraction_inverse))
    scale = jnp.asarray(lane_scale(width))
    flipped = pad_to(pad_to(jnp.swapaxes(refraction_inverse, 1, 2), 1, width), 2, width)
    scaled = flipped / scale[None, :, None]
    on_diag = jnp.eye(width, dtype=bool)[None]
    matrices = jnp.where(on_diag, 0.0, scaled).astype(jnp.bfloat16)
    diagonal = jnp.sum(jnp.where(on_diag, scaled, 0.0), axis=1, keepdims=True)
    arrived = lax.all_to_all(outgoing.reshape(devices, CAP, load), axes, split_axis=0,
                             concat_axis=0, tiled=True).reshape(slot_total, load)

    partner = lax.ppermute(held, axes, swap_route)
    is_low = half == 0
    chip = jnp.concatenate(
        [jnp.where(is_low, held, partner), jnp.where(is_low, partner, held)], axis=1)
    strength = (chip[0] * 0.1) ** 2
    feats = jnp.stack([chip[2], strength, jnp.cos(chip[1]), jnp.sin(chip[1])])
    assert width - rows >= quad_size and rows <= LANES
    far_out = jnp.pad(
        jnp.where(is_low, feats[:, :, cols_dev - 1], feats[:, :, 0])[:, None],
        ((0, 0), (0, 0), (width - rows, 0)))
    mine = jnp.where(is_low, feats[:, :, :own], feats[:, :, own:])
    right = jnp.where(is_low, feats[:, :, own], 0.0)
    left = jnp.where(is_low, 0.0, feats[:, :, own - 1])
    grid = jnp.concatenate(
        [mine, right[:, :, None], jnp.zeros((4, rows, HALO - 2), jnp.float32), left[:, :, None]], axis=2)
    class_here, strength, cos_here, sin_here = grid[0], grid[1], grid[2], grid[3]

    angle = (jnp.arange(NDIR, dtype=jnp.float32) + 0.5) * (2.0 * math.pi / NDIR)
    cos_lane = pad_to(jnp.repeat(jnp.cos(angle), NFREQ).reshape(QUADS, quad_size), 1, width)
    sin_lane = pad_to(jnp.repeat(jnp.sin(angle), NFREQ).reshape(QUADS, quad_size), 1, width)
    rate_lane = pad_to(jnp.tile(input_rate, quarter), 0, width)
    speed_lane = pad_to(jnp.tile(group_speed, (1, quarter)), 1, width)
    loss_lane = pad_to(jnp.tile(dissipation, (1, quarter)), 1, width, 1.0)
    ax_table = jnp.abs(cos_lane)[:, None] * speed_lane[None]
    ay_table = jnp.abs(sin_lane)[:, None] * speed_lane[None]
    base_table = ax_table + ay_table + loss_lane[None]

    ratio_lane = jnp.abs(sin_lane) / jnp.where(cos_lane == 0.0, 1.0, jnp.abs(cos_lane))
    lanes = jnp.stack([jnp.broadcast_to(rate_lane, (QUADS, width)), cos_lane, sin_lane,
                       jnp.broadcast_to(scale, (QUADS, width)), ratio_lane], axis=1)
    consts = jnp.concatenate([ax_table, base_table, lanes, diagonal], axis=1)
    consts = pad_to(consts, 1, -(-consts.shape[1] // 8) * 8)

    def by_class(table):
        chosen = jnp.broadcast_to(table[:, None, None, 0], (QUADS, rows, cells, width))
        for kind in range(1, class_count):
            chosen = jnp.where((class_here == kind)[None, :, :, None], table[:, None, None, kind], chosen)
        return chosen

    ax = by_class(ax_table)
    base = by_class(base_table)
    spread = jnp.maximum(
        cos_here[None, :, :, None] * cos_lane[:, None, None]
        + sin_here[None, :, :, None] * sin_lane[:, None, None], 0.0)
    wind = (rate_lane[None, None, None] * strength[None, :, :, None]) * (spread * spread)

    arrived, ax, base, wind, matrices = lax.optimization_barrier(
        (arrived, ax, base, wind, matrices))

    info = jnp.concatenate([sweep_order.reshape(-1), half[None].astype(jnp.int32)])
    block = cells + rows_dev
    rim_shapes = [jax.ShapeDtypeStruct((QUADS, size, width), jnp.float32)
                  for size in (block, block, HALO, HALO)]
    rim_own, rim_send, out_same, out_cross = pl.pallas_call(
        partial(rim_kernel, own, rows_dev, comps, quad_size),
        in_specs=[pl.BlockSpec(memory_space=pltpu.SMEM), in_vmem, in_vmem],
        out_specs=[in_vmem] * len(rim_shapes),
        out_shape=rim_shapes,
        compiler_params=pltpu.CompilerParams(vmem_limit_bytes=40 * 2**20),
    )(info, arrived, far_out)
    rim_partner = lax.ppermute(rim_send, axes, swap_route)
    rim_same = lax.ppermute(out_same, axes, same_route)
    rim_cross = lax.ppermute(out_cross, axes, cross_route)

    turns = ITERS * QUADS

    def quad_block(shape):
        zeros = (0,) * len(shape)
        return pl.BlockSpec((1,) + shape, lambda t, info: (info[t],) + zeros)

    pairs = QUADS // 2
    packed = jax.ShapeDtypeStruct((quad_size, rows_dev, cols_dev), jnp.float32)
    halves = pl.pallas_call(
        partial(sweeps_kernel, rows, own, cells, quad_size, class_count),
        grid_spec=pltpu.PrefetchScalarGridSpec(
            num_scalar_prefetch=1,
            grid=(turns,),
            in_specs=[quad_block((rows, cells, width))] * 3
            + [quad_block((width, width)), quad_block(consts.shape[1:])]
            + [in_vmem] * 4,
            out_specs=[in_vmem] * (2 * pairs),
            scratch_shapes=[
                pltpu.VMEM((QUADS, rows, cells, width), jnp.float32),
                pltpu.VMEM((QUADS, rows, cells, LANES), jnp.float32),
                pltpu.VMEM((2, cells, width), jnp.float32),
                pltpu.VMEM((rows, 2 * HALO, width), jnp.float32),
                pltpu.VMEM((4, rows, width), jnp.float32),
            ],
        ),
        out_shape=[packed] * (2 * pairs),
        compiler_params=pltpu.CompilerParams(
            dimension_semantics=("arbitrary",), vmem_limit_bytes=48 * 2**20),
    )(info, ax, base, wind, matrices, consts, rim_own, rim_partner, rim_same, rim_cross)

    got = [lax.ppermute(half_out, axes, swap_route) for half_out in halves[pairs:]]
    chunks = 4
    merged = []
    for pair in range(pairs):
        merged = [pl.pallas_call(
            partial(merge_kernel, own, pair, chunks),
            in_specs=[pl.BlockSpec(memory_space=pltpu.SMEM), in_vmem, in_vmem]
            + [pl.BlockSpec(memory_space=pl.ANY)] * len(merged),
            out_specs=pl.BlockSpec(memory_space=pl.ANY),
            scratch_shapes=[
                pltpu.VMEM((chunks, 2, quad_size // chunks, rows_dev, cols_dev), jnp.float32),
                pltpu.SemaphoreType.DMA((chunks, 2))],
            out_shape=jax.ShapeDtypeStruct((QUADS, quad_size, rows_dev, cols_dev), jnp.float32),
            input_output_aliases={3: 0} if merged else {},
            compiler_params=pltpu.CompilerParams(vmem_limit_bytes=16 * 2**20),
        )(info, halves[pair], got[pair], *merged)]
    return merged[0].reshape(comps, rows_dev, cols_dev)


def solution(mesh):
    placed = (
        P("rows", "cols"),
        P("rows", "cols"),
        P("rows", "cols"),
        P(),
        P(),
        P(),
        P(("rows", "cols"), None),
        P(("rows", "cols")),
        P(),
        P(),
    )
    return jax.shard_map(
        body, mesh=mesh, in_specs=placed, out_specs=P(None, "rows", "cols"), check_vma=False
    )
```

```python
from functools import partial
import math

import jax
import jax.numpy as jnp
import numpy as np
from jax import lax
from jax.experimental import pallas as pl
from jax.experimental.pallas import tpu as pltpu
from jax.sharding import PartitionSpec as P

NDIR = 36
NFREQ = 24
CAP = 16
ITERS = 2
QUADS = 4
LANES = 128
HALO = 8

whitecap_rate = 0.5


def split_bf16(value):
    high = value.astype(jnp.bfloat16)
    low = (value - high.astype(jnp.float32)).astype(jnp.bfloat16)
    return high, low


def lane_scale(width):
    golden = (math.sqrt(5.0) - 1.0) / 2.0
    return np.exp2(np.mod(np.arange(width) * golden, 1.0)).astype(np.float32)


def pad_to(array, axis, size, value=0.0):
    widths = [(0, 0)] * array.ndim
    widths[axis] = (0, size - array.shape[axis])
    return jnp.pad(array, widths, constant_values=value)


def pack_kernel(shifts, col_count, rows, comps, dest_hbm, spectra_hbm, wind_hbm, dir_hbm, class_hbm,
                out_ref, held_ref, dest_ref, spectra_ref, class_ref, high, low, slots, sems):
    step = pl.program_id(0)
    points = dest_ref.shape[1]
    load = out_ref.shape[1]
    total_bits, row_bits, col_bits = shifts

    @pl.when(step == 0)
    def _():
        pieces = ((dest_hbm, dest_ref), (spectra_hbm, spectra_ref), (wind_hbm, held_ref.at[0]),
                  (dir_hbm, held_ref.at[1]), (class_hbm, class_ref))
        copies = [pltpu.make_async_copy(source, target, sems.at[index])
                  for index, (source, target) in enumerate(pieces)]
        for copy in copies:
            copy.start()
        copies[0].wait()
        dest = dest_ref[...]
        grid_row = lax.shift_right_logical(dest, total_bits)
        grid_col = dest & (2**total_bits - 1)
        local_row = grid_row & (2**row_bits - 1)
        local_col = grid_col & (2**col_bits - 1)
        owner = (lax.shift_right_logical(grid_row, row_bits) * col_count
                 + lax.shift_right_logical(grid_col, col_bits))
        on_row = (grid_row == 0) | (grid_row == rows - 1)
        on_left = jnp.where(grid_col == 0, 2**col_bits, 2**col_bits + 2**row_bits) + local_row
        code = jnp.where(on_row, local_col, on_left) + 1
        lanes = jnp.concatenate(
            [owner.astype(jnp.float32), code.astype(jnp.float32), jnp.zeros((6, points), jnp.float32)],
            axis=0)
        columns = lanes.T
        same = columns[:, 0:1] == lanes[0:1]
        above = (lax.broadcasted_iota(jnp.int32, (points, points), 0)
                 < lax.broadcasted_iota(jnp.int32, (points, points), 1))
        rank = jnp.sum(jnp.where(same & above, 1.0, 0.0), axis=0, keepdims=True)
        slots[...] = owner * CAP + rank.astype(jnp.int32)
        for copy in copies[1:]:
            copy.wait()
        held_ref[2] = class_ref[...].astype(jnp.float32)
        spectra = jnp.concatenate(
            [spectra_ref[...], jnp.broadcast_to(lanes[1:2], (load - comps, points))], axis=0)
        high[...], low[...] = split_bf16(spectra)

    place = jnp.where(
        lax.broadcasted_iota(jnp.int32, (out_ref.shape[0], points), 0) + step * out_ref.shape[0]
        == slots[...], 1.0, 0.0).astype(jnp.bfloat16)
    over_points = (((1,), (1,)), ((), ()))
    out_ref[...] = (lax.dot_general(place, high[...], over_points, preferred_element_type=jnp.float32)
                    + lax.dot_general(place, low[...], over_points, preferred_element_type=jnp.float32))


def rim_kernel(own, rows_dev, comps, quad_size, info, arrived_ref, far_ref, own_ref, send_ref, same_ref,
               cross_ref):
    half = info[ITERS * QUADS]
    cols_dev = 2 * own
    cells = own + HALO
    block = cells + rows_dev
    width = own_ref.shape[2]
    load = arrived_ref.shape[1]
    spots = -(-(2 * block + 2 * HALO) // LANES) * LANES
    lane = lax.broadcasted_iota(jnp.int32, (1, spots), 1)
    at_send = lane >= block
    spot = jnp.where(at_send, lane - block, lane)
    side_at = jnp.where(at_send, 1 - half, half)
    want = jnp.where(spot < own, own * side_at + spot, -1)
    want = jnp.where((spot == own) & (side_at == 0), own, want)
    want = jnp.where((spot == cells - 1) & (side_at == 1), own - 1, want)
    want = jnp.where(spot >= cells, cols_dev + rows_dev * side_at + spot - cells, want)
    rest = lane - 2 * block
    to_left = jnp.where((rest == HALO - 1) & (half == 0), cols_dev - 1, -1)
    to_left = jnp.where((rest == 0) & (half == 1), 0, to_left)
    to_left = jnp.where((rest == HALO) & (half == 0), 0, to_left)
    to_left = jnp.where((rest == 2 * HALO - 1) & (half == 1), cols_dev - 1, to_left)
    want = jnp.where(rest >= 0, to_left, want)
    code = arrived_ref[:, comps:comps + 1]
    gather = jnp.where(code == (want + 1).astype(jnp.float32), 1.0, 0.0)
    gather = jnp.where(want >= 0, gather, 0.0).astype(jnp.bfloat16)
    high, low = split_bf16(arrived_ref[...])
    over_points = (((0,), (0,)), ((), ()))
    summed = (lax.dot_general(gather, high, over_points, preferred_element_type=jnp.float32)
              + lax.dot_general(gather, low, over_points, preferred_element_type=jnp.float32))
    for quad in range(QUADS):
        start = quad * quad_size
        part = summed if quad == 0 else pltpu.roll(summed, load - start, 1)
        own_ref[quad] = part[:block, :width]
        send_ref[quad] = part[block:2 * block, :width]
        halo = part[2 * block:2 * block + HALO, :width]
        free = lax.broadcasted_iota(jnp.int32, halo.shape, 1) >= quad_size
        same_ref[quad] = jnp.where(free, far_ref[quad], halo)
        cross_ref[quad] = part[2 * block + HALO:2 * block + 2 * HALO, :width]


def sweeps_kernel(rows, own, cells, quad_size, class_count, info, ax_ref, base_ref,
                  wind_ref, mt_ref, const_ref, own_ref, par_ref, same_ref, cross_ref, *rest):
    pairs = QUADS // 2
    keep_refs, send_refs = rest[:pairs], rest[pairs:2 * pairs]
    state, power, rim, side, far_rows = rest[2 * pairs:]
    half = info[ITERS * QUADS]
    width = mt_ref.shape[2]
    rows_dev = rows // 2
    power[...] = jnp.zeros_like(power)
    numbers = jnp.concatenate(
        [same_ref[feat, 0:1, width - LANES:] for feat in range(4)]
        + [jnp.zeros((4, LANES), jnp.float32)], axis=0).T
    for feat in range(4):
        far_rows[feat] = jnp.broadcast_to(
            numbers[LANES - rows:, feat:feat + 1], (rows, width))

    def sweep(turn, count, second):
        quad = info[turn]
        ax_table = const_ref[quad, :class_count]
        base_table = const_ref[quad, class_count:2 * class_count]
        rate_lane, cos_lane, sin_lane, scale_lane, ratio_lane, diag_lane = [
            const_ref[quad, 2 * class_count + each:2 * class_count + each + 1] for each in range(6)]
        down = (quad == 0) | (quad == 3)
        step_x = jnp.where(down, 1, -1)
        first_row = jnp.where(down, 0, rows - 1)
        up_y = quad < 2
        rim[0] = own_ref[quad, 0:cells]
        rim[0, own:cells] = own_ref[quad, own:cells] + same_ref[quad]
        rim[1] = par_ref[quad, 0:cells]
        rim[1, own:cells] = par_ref[quad, own:cells] + cross_ref[quad]
        far_at = jnp.where(half == 0, HALO - 1, 0)
        at_far = lax.broadcasted_iota(jnp.int32, (HALO, width), 0) == far_at
        edge_at = jnp.where(half == 0, 0, 2 * HALO - 1)
        at_edge = lax.broadcasted_iota(jnp.int32, (2 * HALO, width), 0) == edge_at
        for j in range(rows_dev):
            mine = jnp.where(at_edge, own_ref[quad, cells + j:cells + j + 1], 0.0)
            theirs = jnp.where(at_edge, par_ref[quad, cells + j:cells + j + 1], 0.0)
            side[j + rows_dev * half] = mine
            side[j + rows_dev * (1 - half)] = theirs

        def patched(block, far_row):
            if second:
                return block
            return jnp.concatenate([block[:own], jnp.where(at_far, far_row, block[own:])], axis=0)

        def factors(i, low, high):
            row = first_row + i * step_x
            kind, strength, far_cos, far_sin = [
                far_rows[feat, pl.ds(row, 1), :] for feat in range(4)]
            far_ax = jnp.zeros((1, width), jnp.float32)
            far_base = jnp.zeros((1, width), jnp.float32)
            for each in range(class_count):
                far_ax = jnp.where(kind == each, ax_table[each:each + 1], far_ax)
                far_base = jnp.where(kind == each, base_table[each:each + 1], far_base)
            spread = jnp.maximum(far_cos * cos_lane + far_sin * sin_lane, 0.0)
            far_wind = (rate_lane * strength) * (spread * spread)
            total = power[0, row, low:high]
            for other in range(1, QUADS):
                total = total + power[other, row, low:high]
            level = total * (1.0 / (QUADS * quad_size))
            damping = whitecap_rate * level / (1.0 + level)
            den = patched(base_ref[quad, row, low:high], far_base) + jnp.concatenate([damping] * (width // LANES), axis=1)
            inverse = scale_lane / den
            source = patched(wind_ref[quad, row, low:high], far_wind)
            edge = side[row]
            parts = [source[:HALO] + edge[:HALO], source[HALO:own - HALO],
                     source[own - HALO:own] + edge[HALO:]]
            if high > own:
                parts.append(source[own:])
            source = jnp.concatenate(parts, axis=0)
            if i == 0 or i == rows - 1:
                here = jnp.where(row // rows_dev == half, 0, 1)
                source = source + rim[here, low:high]
            if second:
                before = state[quad, row]
                shifted = jnp.where(up_y, pltpu.roll(before, 1, 0), pltpu.roll(before, cells - 1, 0))
                source = source + ax_ref[quad, row, low:high] * (ratio_lane * shifted[low:high])
            return patched(ax_ref[quad, row, low:high], far_ax) * inverse, source * inverse

        def store(i, value):
            row = first_row + i * step_x
            square = value * value
            folded = square[:, :LANES]
            for lane in range(LANES, width, LANES):
                folded = folded + square[:, lane:lane + LANES]
            state[quad, row, :count] = value
            power[quad, row, :count] = jnp.broadcast_to(
                jnp.sum(folded, axis=1, keepdims=True), (count, LANES))

        balance = factors(0, 0, count)[1]
        upwind = None
        for i in range(rows):
            mixed = jnp.dot(balance.astype(jnp.bfloat16), mt_ref[quad],
                            preferred_element_type=jnp.float32)
            direct = diag_lane * balance
            if i + 1 < rows:
                along, known = factors(i + 1, 0, count)
                balance = along * mixed + (along * direct + known)
            if i > 0:
                store(i - 1, upwind)
            upwind = direct + mixed
        store(rows - 1, upwind)

    @pl.loop(0, QUADS)
    def _(turn):
        sweep(turn, cells, False)

    @pl.loop(QUADS, ITERS * QUADS)
    def _(turn):
        sweep(turn, own, True)

    for pair in range(pairs):
        for j in range(rows_dev):
            for out_ref, side_at in ((keep_refs[pair], half), (send_refs[pair], 1 - half)):
                row = rows_dev * side_at + j
                both = jnp.concatenate(
                    [state[2 * pair, row, :own], state[2 * pair + 1, row, :own]], axis=0)
                out_ref[:, j, :] = both.T[:quad_size]


def merge_kernel(own, pair, chunks, info, keep_ref, got_ref, *rest):
    out_ref, stage, sems = rest[-3:]
    half = info[ITERS * QUADS]
    part = keep_ref.shape[0] // chunks
    copies = []
    for chunk in range(chunks):
        span = pl.ds(chunk * part, part)
        keep = keep_ref[span]
        got = got_ref[span]
        left = jnp.where(half == 0, keep, got)
        right = jnp.where(half == 0, got, keep)
        low = lax.broadcasted_iota(jnp.int32, keep.shape, 2) < own
        stage[chunk, 0] = jnp.where(low, left, pltpu.roll(right, own, 2))
        stage[chunk, 1] = jnp.where(low, pltpu.roll(left, own, 2), right)
        for member in range(2):
            copies.append(pltpu.make_async_copy(
                stage.at[chunk, member], out_ref.at[2 * pair + member, span], sems.at[chunk, member]))
            copies[-1].start()
    for copy in copies:
        copy.wait()


def body(
    wind_speed,
    wind_dir,
    depth_class,
    group_speed,
    dissipation,
    input_rate,
    outer_spectra,
    dest_cell,
    refraction_inverse,
    sweep_order,
):
    rows_dev, cols_dev = wind_speed.shape
    row_count = lax.axis_size("rows")
    col_count = lax.axis_size("cols")
    assert row_count == 2
    devices = row_count * col_count
    rows = rows_dev * row_count
    own = cols_dev // 2
    cells = own + HALO
    class_count = group_speed.shape[0]
    comps = outer_spectra.shape[1]
    quad_size = refraction_inverse.shape[1]
    quarter = NDIR // QUADS
    width = -(-quad_size // LANES) * LANES
    axes = ("rows", "cols")
    half = lax.axis_index("rows")

    def device(row_at, col_at):
        return row_at * col_count + col_at

    span = range(col_count)
    swap_route = [(device(1 - h, c), device(h, c)) for h in range(2) for c in span]
    same_route = [(device(0, c - 1), device(0, c)) for c in span if c > 0]
    same_route += [(device(1, c + 1), device(1, c)) for c in span if c + 1 < col_count]
    cross_route = [(device(1, c - 1), device(0, c)) for c in span if c > 0]
    cross_route += [(device(0, c + 1), device(1, c)) for c in span if c + 1 < col_count]

    points = dest_cell.shape[0]
    load = -(-(comps + 1) // LANES) * LANES
    sizes = (cols_dev * col_count, rows_dev, cols_dev)
    shifts = tuple(size.bit_length() - 1 for size in sizes)
    assert all(size == 2**shift for size, shift in zip(sizes, shifts))
    slot_total = devices * CAP
    steps = 4
    in_vmem = pl.BlockSpec(memory_space=pltpu.VMEM)
    anywhere = pl.BlockSpec(memory_space=pl.ANY)
    outgoing, held = pl.pallas_call(
        partial(pack_kernel, shifts, col_count, rows, comps),
        grid=(steps,),
        in_specs=[anywhere] * 5,
        out_specs=[pl.BlockSpec((slot_total // steps, load), lambda s: (s, 0)), in_vmem],
        scratch_shapes=[pltpu.VMEM((1, points), jnp.int32),
                        pltpu.VMEM((comps, points), jnp.float32),
                        pltpu.VMEM((rows_dev, cols_dev), jnp.int32),
                        pltpu.VMEM((load, points), jnp.bfloat16),
                        pltpu.VMEM((load, points), jnp.bfloat16),
                        pltpu.VMEM((1, points), jnp.int32),
                        pltpu.SemaphoreType.DMA((5,))],
        out_shape=[jax.ShapeDtypeStruct((slot_total, load), jnp.float32),
                   jax.ShapeDtypeStruct((3, rows_dev, cols_dev), jnp.float32)],
        compiler_params=pltpu.CompilerParams(
            dimension_semantics=("arbitrary",), vmem_limit_bytes=60 * 2**20),
    )(dest_cell.reshape(1, points), outer_spectra.T, wind_speed, wind_dir, depth_class)
    outgoing, refraction_inverse = lax.optimization_barrier((outgoing, refraction_inverse))
    scale = jnp.asarray(lane_scale(width))
    flipped = pad_to(pad_to(jnp.swapaxes(refraction_inverse, 1, 2), 1, width), 2, width)
    scaled = flipped / scale[None, :, None]
    on_diag = jnp.eye(width, dtype=bool)[None]
    matrices = jnp.where(on_diag, 0.0, scaled).astype(jnp.bfloat16)
    diagonal = jnp.sum(jnp.where(on_diag, scaled, 0.0), axis=1, keepdims=True)
    arrived = lax.all_to_all(outgoing.reshape(devices, CAP, load), axes, split_axis=0,
                             concat_axis=0, tiled=True).reshape(slot_total, load)

    partner = lax.ppermute(held, axes, swap_route)
    is_low = half == 0
    chip = jnp.concatenate(
        [jnp.where(is_low, held, partner), jnp.where(is_low, partner, held)], axis=1)
    strength = (chip[0] * 0.1) ** 2
    feats = jnp.stack([chip[2], strength, jnp.cos(chip[1]), jnp.sin(chip[1])])
    assert width - rows >= quad_size and rows <= LANES
    far_out = jnp.pad(
        jnp.where(is_low, feats[:, :, cols_dev - 1], feats[:, :, 0])[:, None],
        ((0, 0), (0, 0), (width - rows, 0)))
    mine = jnp.where(is_low, feats[:, :, :own], feats[:, :, own:])
    right = jnp.where(is_low, feats[:, :, own], 0.0)
    left = jnp.where(is_low, 0.0, feats[:, :, own - 1])
    grid = jnp.concatenate(
        [mine, right[:, :, None], jnp.zeros((4, rows, HALO - 2), jnp.float32), left[:, :, None]], axis=2)
    class_here, strength, cos_here, sin_here = grid[0], grid[1], grid[2], grid[3]

    angle = (jnp.arange(NDIR, dtype=jnp.float32) + 0.5) * (2.0 * math.pi / NDIR)
    cos_lane = pad_to(jnp.repeat(jnp.cos(angle), NFREQ).reshape(QUADS, quad_size), 1, width)
    sin_lane = pad_to(jnp.repeat(jnp.sin(angle), NFREQ).reshape(QUADS, quad_size), 1, width)
    rate_lane = pad_to(jnp.tile(input_rate, quarter), 0, width)
    speed_lane = pad_to(jnp.tile(group_speed, (1, quarter)), 1, width)
    loss_lane = pad_to(jnp.tile(dissipation, (1, quarter)), 1, width, 1.0)
    ax_table = jnp.abs(cos_lane)[:, None] * speed_lane[None]
    ay_table = jnp.abs(sin_lane)[:, None] * speed_lane[None]
    base_table = ax_table + ay_table + loss_lane[None]

    ratio_lane = jnp.abs(sin_lane) / jnp.where(cos_lane == 0.0, 1.0, jnp.abs(cos_lane))
    lanes = jnp.stack([jnp.broadcast_to(rate_lane, (QUADS, width)), cos_lane, sin_lane,
                       jnp.broadcast_to(scale, (QUADS, width)), ratio_lane], axis=1)
    consts = jnp.concatenate([ax_table, base_table, lanes, diagonal], axis=1)
    consts = pad_to(consts, 1, -(-consts.shape[1] // 8) * 8)

    def by_class(table):
        chosen = jnp.broadcast_to(table[:, None, None, 0], (QUADS, rows, cells, width))
        for kind in range(1, class_count):
            chosen = jnp.where((class_here == kind)[None, :, :, None], table[:, None, None, kind], chosen)
        return chosen

    ax = by_class(ax_table)
    base = by_class(base_table)
    spread = jnp.maximum(
        cos_here[None, :, :, None] * cos_lane[:, None, None]
        + sin_here[None, :, :, None] * sin_lane[:, None, None], 0.0)
    wind = (rate_lane[None, None, None] * strength[None, :, :, None]) * (spread * spread)

    arrived, ax, base, wind, matrices = lax.optimization_barrier(
        (arrived, ax, base, wind, matrices))

    info = jnp.concatenate([sweep_order.reshape(-1), half[None].astype(jnp.int32)])
    block = cells + rows_dev
    rim_shapes = [jax.ShapeDtypeStruct((QUADS, size, width), jnp.float32)
                  for size in (block, block, HALO, HALO)]
    rim_own, rim_send, out_same, out_cross = pl.pallas_call(
        partial(rim_kernel, own, rows_dev, comps, quad_size),
        in_specs=[pl.BlockSpec(memory_space=pltpu.SMEM), in_vmem, in_vmem],
        out_specs=[in_vmem] * len(rim_shapes),
        out_shape=rim_shapes,
        compiler_params=pltpu.CompilerParams(vmem_limit_bytes=24 * 2**20),
    )(info, arrived, far_out)
    rim_partner = lax.ppermute(rim_send, axes, swap_route)
    rim_same = lax.ppermute(out_same, axes, same_route)
    rim_cross = lax.ppermute(out_cross, axes, cross_route)

    pairs = QUADS // 2
    packed = jax.ShapeDtypeStruct((quad_size, rows_dev, cols_dev), jnp.float32)
    halves = pl.pallas_call(
        partial(sweeps_kernel, rows, own, cells, quad_size, class_count),
        in_specs=[pl.BlockSpec(memory_space=pltpu.SMEM)] + [in_vmem] * 9,
        out_specs=[in_vmem] * (2 * pairs),
        scratch_shapes=[
            pltpu.VMEM((QUADS, rows, cells, width), jnp.float32),
            pltpu.VMEM((QUADS, rows, cells, LANES), jnp.float32),
            pltpu.VMEM((2, cells, width), jnp.float32),
            pltpu.VMEM((rows, 2 * HALO, width), jnp.float32),
            pltpu.VMEM((4, rows, width), jnp.float32),
        ],
        out_shape=[packed] * (2 * pairs),
        compiler_params=pltpu.CompilerParams(vmem_limit_bytes=24 * 2**20),
    )(info, ax, base, wind, matrices, consts, rim_own, rim_partner, rim_same, rim_cross)

    got = [lax.ppermute(half_out, axes, swap_route) for half_out in halves[pairs:]]
    chunks = 4
    merged = []
    for pair in range(pairs):
        merged = [pl.pallas_call(
            partial(merge_kernel, own, pair, chunks),
            in_specs=[pl.BlockSpec(memory_space=pltpu.SMEM), in_vmem, in_vmem]
            + [pl.BlockSpec(memory_space=pl.ANY)] * len(merged),
            out_specs=pl.BlockSpec(memory_space=pl.ANY),
            scratch_shapes=[
                pltpu.VMEM((chunks, 2, quad_size // chunks, rows_dev, cols_dev), jnp.float32),
                pltpu.SemaphoreType.DMA((chunks, 2))],
            out_shape=jax.ShapeDtypeStruct((QUADS, quad_size, rows_dev, cols_dev), jnp.float32),
            input_output_aliases={3: 0} if merged else {},
            compiler_params=pltpu.CompilerParams(vmem_limit_bytes=16 * 2**20),
        )(info, halves[pair], got[pair], *merged)]
    return merged[0].reshape(comps, rows_dev, cols_dev)


def solution(mesh):
    placed = (
        P("rows", "cols"),
        P("rows", "cols"),
        P("rows", "cols"),
        P(),
        P(),
        P(),
        P(("rows", "cols"), None),
        P(("rows", "cols")),
        P(),
        P(),
    )
    return jax.shard_map(
        body, mesh=mesh, in_specs=placed, out_specs=P(None, "rows", "cols"), check_vma=False
    )
```

```python
from functools import partial
import math

import jax
import jax.numpy as jnp
import numpy as np
from jax import lax
from jax.experimental import pallas as pl
from jax.experimental.pallas import tpu as pltpu
from jax.sharding import PartitionSpec as P

NDIR = 36
NFREQ = 24
CAP = 16
ITERS = 2
QUADS = 4
LANES = 128
HALO = 8

whitecap_rate = 0.5


def split_bf16(value):
    high = value.astype(jnp.bfloat16)
    low = (value - high.astype(jnp.float32)).astype(jnp.bfloat16)
    return high, low


def lane_scale(width):
    golden = (math.sqrt(5.0) - 1.0) / 2.0
    return np.exp2(np.mod(np.arange(width) * golden, 1.0)).astype(np.float32)


def pad_to(array, axis, size, value=0.0):
    widths = [(0, 0)] * array.ndim
    widths[axis] = (0, size - array.shape[axis])
    return jnp.pad(array, widths, constant_values=value)


def pack_kernel(shifts, col_count, rows, comps, dest_hbm, spectra_hbm, wind_hbm, dir_hbm, class_hbm,
                out_ref, held_ref, dest_ref, spectra_ref, class_ref, high, low, slots, sems):
    step = pl.program_id(0)
    points = dest_ref.shape[1]
    load = out_ref.shape[1]
    total_bits, row_bits, col_bits = shifts

    @pl.when(step == 0)
    def _():
        pieces = ((dest_hbm, dest_ref), (spectra_hbm, spectra_ref), (wind_hbm, held_ref.at[0]),
                  (dir_hbm, held_ref.at[1]), (class_hbm, class_ref))
        copies = [pltpu.make_async_copy(source, target, sems.at[index])
                  for index, (source, target) in enumerate(pieces)]
        for copy in copies:
            copy.start()
        copies[0].wait()
        dest = dest_ref[...]
        grid_row = lax.shift_right_logical(dest, total_bits)
        grid_col = dest & (2**total_bits - 1)
        local_row = grid_row & (2**row_bits - 1)
        local_col = grid_col & (2**col_bits - 1)
        owner = (lax.shift_right_logical(grid_row, row_bits) * col_count
                 + lax.shift_right_logical(grid_col, col_bits))
        on_row = (grid_row == 0) | (grid_row == rows - 1)
        on_left = jnp.where(grid_col == 0, 2**col_bits, 2**col_bits + 2**row_bits) + local_row
        code = jnp.where(on_row, local_col, on_left) + 1
        lanes = jnp.concatenate(
            [owner.astype(jnp.float32), code.astype(jnp.float32), jnp.zeros((6, points), jnp.float32)],
            axis=0)
        columns = lanes.T
        same = columns[:, 0:1] == lanes[0:1]
        above = (lax.broadcasted_iota(jnp.int32, (points, points), 0)
                 < lax.broadcasted_iota(jnp.int32, (points, points), 1))
        rank = jnp.sum(jnp.where(same & above, 1.0, 0.0), axis=0, keepdims=True)
        slots[...] = owner * CAP + rank.astype(jnp.int32)
        for copy in copies[1:]:
            copy.wait()
        held_ref[2] = class_ref[...].astype(jnp.float32)
        spectra = jnp.concatenate(
            [spectra_ref[...], jnp.broadcast_to(lanes[1:2], (load - comps, points))], axis=0)
        high[...], low[...] = split_bf16(spectra)

    place = jnp.where(
        lax.broadcasted_iota(jnp.int32, (out_ref.shape[0], points), 0) + step * out_ref.shape[0]
        == slots[...], 1.0, 0.0).astype(jnp.bfloat16)
    over_points = (((1,), (1,)), ((), ()))
    out_ref[...] = (lax.dot_general(place, high[...], over_points, preferred_element_type=jnp.float32)
                    + lax.dot_general(place, low[...], over_points, preferred_element_type=jnp.float32))


def rim_kernel(own, rows_dev, comps, quad_size, info, arrived_ref, far_ref, own_ref, send_ref, same_ref,
               cross_ref):
    half = info[ITERS * QUADS]
    cols_dev = 2 * own
    cells = own + HALO
    block = cells + rows_dev
    width = own_ref.shape[2]
    load = arrived_ref.shape[1]
    spots = -(-(2 * block + 2 * HALO) // LANES) * LANES
    lane = lax.broadcasted_iota(jnp.int32, (1, spots), 1)
    at_send = lane >= block
    spot = jnp.where(at_send, lane - block, lane)
    side_at = jnp.where(at_send, 1 - half, half)
    want = jnp.where(spot < own, own * side_at + spot, -1)
    want = jnp.where((spot == own) & (side_at == 0), own, want)
    want = jnp.where((spot == cells - 1) & (side_at == 1), own - 1, want)
    want = jnp.where(spot >= cells, cols_dev + rows_dev * side_at + spot - cells, want)
    rest = lane - 2 * block
    to_left = jnp.where((rest == HALO - 1) & (half == 0), cols_dev - 1, -1)
    to_left = jnp.where((rest == 0) & (half == 1), 0, to_left)
    to_left = jnp.where((rest == HALO) & (half == 0), 0, to_left)
    to_left = jnp.where((rest == 2 * HALO - 1) & (half == 1), cols_dev - 1, to_left)
    want = jnp.where(rest >= 0, to_left, want)
    code = arrived_ref[:, comps:comps + 1]
    gather = jnp.where(code == (want + 1).astype(jnp.float32), 1.0, 0.0)
    gather = jnp.where(want >= 0, gather, 0.0).astype(jnp.bfloat16)
    high, low = split_bf16(arrived_ref[...])
    over_points = (((0,), (0,)), ((), ()))
    summed = (lax.dot_general(gather, high, over_points, preferred_element_type=jnp.float32)
              + lax.dot_general(gather, low, over_points, preferred_element_type=jnp.float32))
    for quad in range(QUADS):
        start = quad * quad_size
        part = summed if quad == 0 else pltpu.roll(summed, load - start, 1)
        own_ref[quad] = part[:block, :width]
        send_ref[quad] = part[block:2 * block, :width]
        halo = part[2 * block:2 * block + HALO, :width]
        free = lax.broadcasted_iota(jnp.int32, halo.shape, 1) >= quad_size
        same_ref[quad] = jnp.where(free, far_ref[quad], halo)
        cross_ref[quad] = part[2 * block + HALO:2 * block + 2 * HALO, :width]


def sweeps_kernel(rows, own, cells, quad_size, class_count, info, ax_hbm, base_hbm,
                  wind_hbm, mt_ref, const_ref, own_ref, par_ref, same_ref, cross_ref, *rest):
    pairs = QUADS // 2
    keep_refs, send_refs = rest[:pairs], rest[pairs:2 * pairs]
    state, power, rim, side, far_rows, ax_ref, base_ref, wind_ref, sems = rest[2 * pairs:]
    half = info[ITERS * QUADS]
    width = mt_ref.shape[2]
    rows_dev = rows // 2

    def fetch(turn):
        quad = info[turn]
        return [pltpu.make_async_copy(source.at[quad], target.at[quad], sems.at[index, turn])
                for index, (source, target) in enumerate(
                    ((ax_hbm, ax_ref), (base_hbm, base_ref), (wind_hbm, wind_ref)))]

    for copy in fetch(0):
        copy.start()
    power[...] = jnp.zeros_like(power)
    numbers = jnp.concatenate(
        [same_ref[feat, 0:1, width - LANES:] for feat in range(4)]
        + [jnp.zeros((4, LANES), jnp.float32)], axis=0).T
    for feat in range(4):
        far_rows[feat] = jnp.broadcast_to(
            numbers[LANES - rows:, feat:feat + 1], (rows, width))
    far_at = jnp.where(half == 0, HALO - 1, 0)
    at_far = lax.broadcasted_iota(jnp.int32, (HALO, width), 0) == far_at
    edge_at = jnp.where(half == 0, 0, 2 * HALO - 1)
    at_edge = lax.broadcasted_iota(jnp.int32, (2 * HALO, width), 0) == edge_at
    for quad in range(QUADS):
        rim[quad, 0] = own_ref[quad, 0:cells]
        rim[quad, 0, own:cells] = own_ref[quad, own:cells] + same_ref[quad]
        rim[quad, 1] = par_ref[quad, 0:cells]
        rim[quad, 1, own:cells] = par_ref[quad, own:cells] + cross_ref[quad]
        for j in range(rows_dev):
            mine = jnp.where(at_edge, own_ref[quad, cells + j:cells + j + 1], 0.0)
            theirs = jnp.where(at_edge, par_ref[quad, cells + j:cells + j + 1], 0.0)
            side[quad, j + rows_dev * half] = mine
            side[quad, j + rows_dev * (1 - half)] = theirs

    def sweep(turn, count, second):
        quad = info[turn]
        ax_table = const_ref[quad, :class_count]
        base_table = const_ref[quad, class_count:2 * class_count]
        rate_lane, cos_lane, sin_lane, scale_lane, ratio_lane, diag_lane = [
            const_ref[quad, 2 * class_count + each:2 * class_count + each + 1] for each in range(6)]
        down = (quad == 0) | (quad == 3)
        step_x = jnp.where(down, 1, -1)
        first_row = jnp.where(down, 0, rows - 1)
        up_y = quad < 2

        def patched(block, far_row):
            if second:
                return block
            return jnp.concatenate([block[:own], jnp.where(at_far, far_row, block[own:])], axis=0)

        def factors(i, low, high):
            row = first_row + i * step_x
            kind, strength, far_cos, far_sin = [
                far_rows[feat, pl.ds(row, 1), :] for feat in range(4)]
            far_ax = jnp.zeros((1, width), jnp.float32)
            far_base = jnp.zeros((1, width), jnp.float32)
            for each in range(class_count):
                far_ax = jnp.where(kind == each, ax_table[each:each + 1], far_ax)
                far_base = jnp.where(kind == each, base_table[each:each + 1], far_base)
            spread = jnp.maximum(far_cos * cos_lane + far_sin * sin_lane, 0.0)
            far_wind = (rate_lane * strength) * (spread * spread)
            total = power[0, row, low:high]
            for other in range(1, QUADS):
                total = total + power[other, row, low:high]
            level = total * (1.0 / (QUADS * quad_size))
            damping = whitecap_rate * level / (1.0 + level)
            den = patched(base_ref[quad, row, low:high], far_base) + jnp.concatenate([damping] * (width // LANES), axis=1)
            inverse = scale_lane / den
            source = patched(wind_ref[quad, row, low:high], far_wind)
            edge = side[quad, row]
            parts = [source[:HALO] + edge[:HALO], source[HALO:own - HALO],
                     source[own - HALO:own] + edge[HALO:]]
            if high > own:
                parts.append(source[own:])
            source = jnp.concatenate(parts, axis=0)
            if i == 0 or i == rows - 1:
                here = jnp.where(row // rows_dev == half, 0, 1)
                source = source + rim[quad, here, low:high]
            if second:
                before = state[quad, row]
                shifted = jnp.where(up_y, pltpu.roll(before, 1, 0), pltpu.roll(before, cells - 1, 0))
                source = source + ax_ref[quad, row, low:high] * (ratio_lane * shifted[low:high])
            return patched(ax_ref[quad, row, low:high], far_ax) * inverse, source * inverse

        def store(i, value):
            row = first_row + i * step_x
            square = value * value
            folded = square[:, :LANES]
            for lane in range(LANES, width, LANES):
                folded = folded + square[:, lane:lane + LANES]
            state[quad, row, :count] = value
            power[quad, row, :count] = jnp.broadcast_to(
                jnp.sum(folded, axis=1, keepdims=True), (count, LANES))

        balance = factors(0, 0, count)[1]
        upwind = None
        for i in range(rows):
            mixed = jnp.dot(balance.astype(jnp.bfloat16), mt_ref[quad],
                            preferred_element_type=jnp.float32)
            direct = diag_lane * balance
            if i + 1 < rows:
                along, known = factors(i + 1, 0, count)
                balance = along * mixed + (along * direct + known)
            if i > 0:
                store(i - 1, upwind)
            upwind = direct + mixed
        store(rows - 1, upwind)

    @pl.loop(0, QUADS)
    def _(turn):
        for copy in fetch(turn):
            copy.wait()

        @pl.when(turn + 1 < QUADS)
        def _():
            for copy in fetch(turn + 1):
                copy.start()

        sweep(turn, cells, False)

    @pl.loop(QUADS, ITERS * QUADS)
    def _(turn):
        sweep(turn, own, True)

    for pair in range(pairs):
        for j in range(rows_dev):
            for out_ref, side_at in ((keep_refs[pair], half), (send_refs[pair], 1 - half)):
                row = rows_dev * side_at + j
                both = jnp.concatenate(
                    [state[2 * pair, row, :own], state[2 * pair + 1, row, :own]], axis=0)
                out_ref[:, j, :] = both.T[:quad_size]


def merge_kernel(own, pair, chunks, info, keep_ref, got_ref, *rest):
    out_ref, stage, sems = rest[-3:]
    half = info[ITERS * QUADS]
    part = keep_ref.shape[0] // chunks
    copies = []
    for chunk in range(chunks):
        span = pl.ds(chunk * part, part)
        keep = keep_ref[span]
        got = got_ref[span]
        left = jnp.where(half == 0, keep, got)
        right = jnp.where(half == 0, got, keep)
        low = lax.broadcasted_iota(jnp.int32, keep.shape, 2) < own
        stage[chunk, 0] = jnp.where(low, left, pltpu.roll(right, own, 2))
        stage[chunk, 1] = jnp.where(low, pltpu.roll(left, own, 2), right)
        for member in range(2):
            copies.append(pltpu.make_async_copy(
                stage.at[chunk, member], out_ref.at[2 * pair + member, span], sems.at[chunk, member]))
            copies[-1].start()
    for copy in copies:
        copy.wait()


def body(
    wind_speed,
    wind_dir,
    depth_class,
    group_speed,
    dissipation,
    input_rate,
    outer_spectra,
    dest_cell,
    refraction_inverse,
    sweep_order,
):
    rows_dev, cols_dev = wind_speed.shape
    row_count = lax.axis_size("rows")
    col_count = lax.axis_size("cols")
    assert row_count == 2
    devices = row_count * col_count
    rows = rows_dev * row_count
    own = cols_dev // 2
    cells = own + HALO
    class_count = group_speed.shape[0]
    comps = outer_spectra.shape[1]
    quad_size = refraction_inverse.shape[1]
    quarter = NDIR // QUADS
    width = -(-quad_size // LANES) * LANES
    axes = ("rows", "cols")
    half = lax.axis_index("rows")

    def device(row_at, col_at):
        return row_at * col_count + col_at

    span = range(col_count)
    swap_route = [(device(1 - h, c), device(h, c)) for h in range(2) for c in span]
    same_route = [(device(0, c - 1), device(0, c)) for c in span if c > 0]
    same_route += [(device(1, c + 1), device(1, c)) for c in span if c + 1 < col_count]
    cross_route = [(device(1, c - 1), device(0, c)) for c in span if c > 0]
    cross_route += [(device(0, c + 1), device(1, c)) for c in span if c + 1 < col_count]

    points = dest_cell.shape[0]
    load = -(-(comps + 1) // LANES) * LANES
    sizes = (cols_dev * col_count, rows_dev, cols_dev)
    shifts = tuple(size.bit_length() - 1 for size in sizes)
    assert all(size == 2**shift for size, shift in zip(sizes, shifts))
    slot_total = devices * CAP
    steps = 4
    in_vmem = pl.BlockSpec(memory_space=pltpu.VMEM)
    anywhere = pl.BlockSpec(memory_space=pl.ANY)
    outgoing, held = pl.pallas_call(
        partial(pack_kernel, shifts, col_count, rows, comps),
        grid=(steps,),
        in_specs=[anywhere] * 5,
        out_specs=[pl.BlockSpec((slot_total // steps, load), lambda s: (s, 0)), in_vmem],
        scratch_shapes=[pltpu.VMEM((1, points), jnp.int32),
                        pltpu.VMEM((comps, points), jnp.float32),
                        pltpu.VMEM((rows_dev, cols_dev), jnp.int32),
                        pltpu.VMEM((load, points), jnp.bfloat16),
                        pltpu.VMEM((load, points), jnp.bfloat16),
                        pltpu.VMEM((1, points), jnp.int32),
                        pltpu.SemaphoreType.DMA((5,))],
        out_shape=[jax.ShapeDtypeStruct((slot_total, load), jnp.float32),
                   jax.ShapeDtypeStruct((3, rows_dev, cols_dev), jnp.float32)],
        compiler_params=pltpu.CompilerParams(
            dimension_semantics=("arbitrary",), vmem_limit_bytes=60 * 2**20),
    )(dest_cell.reshape(1, points), outer_spectra.T, wind_speed, wind_dir, depth_class)
    outgoing, refraction_inverse = lax.optimization_barrier((outgoing, refraction_inverse))
    scale = jnp.asarray(lane_scale(width))
    flipped = pad_to(pad_to(jnp.swapaxes(refraction_inverse, 1, 2), 1, width), 2, width)
    scaled = flipped / scale[None, :, None]
    on_diag = jnp.eye(width, dtype=bool)[None]
    matrices = jnp.where(on_diag, 0.0, scaled).astype(jnp.bfloat16)
    diagonal = jnp.sum(jnp.where(on_diag, scaled, 0.0), axis=1, keepdims=True)
    arrived = lax.all_to_all(outgoing.reshape(devices, CAP, load), axes, split_axis=0,
                             concat_axis=0, tiled=True).reshape(slot_total, load)

    partner = lax.ppermute(held, axes, swap_route)
    is_low = half == 0
    chip = jnp.concatenate(
        [jnp.where(is_low, held, partner), jnp.where(is_low, partner, held)], axis=1)
    strength = (chip[0] * 0.1) ** 2
    feats = jnp.stack([chip[2], strength, jnp.cos(chip[1]), jnp.sin(chip[1])])
    assert width - rows >= quad_size and rows <= LANES
    far_out = jnp.pad(
        jnp.where(is_low, feats[:, :, cols_dev - 1], feats[:, :, 0])[:, None],
        ((0, 0), (0, 0), (width - rows, 0)))
    mine = jnp.where(is_low, feats[:, :, :own], feats[:, :, own:])
    right = jnp.where(is_low, feats[:, :, own], 0.0)
    left = jnp.where(is_low, 0.0, feats[:, :, own - 1])
    grid = jnp.concatenate(
        [mine, right[:, :, None], jnp.zeros((4, rows, HALO - 2), jnp.float32), left[:, :, None]], axis=2)
    class_here, strength, cos_here, sin_here = grid[0], grid[1], grid[2], grid[3]

    angle = (jnp.arange(NDIR, dtype=jnp.float32) + 0.5) * (2.0 * math.pi / NDIR)
    cos_lane = pad_to(jnp.repeat(jnp.cos(angle), NFREQ).reshape(QUADS, quad_size), 1, width)
    sin_lane = pad_to(jnp.repeat(jnp.sin(angle), NFREQ).reshape(QUADS, quad_size), 1, width)
    rate_lane = pad_to(jnp.tile(input_rate, quarter), 0, width)
    speed_lane = pad_to(jnp.tile(group_speed, (1, quarter)), 1, width)
    loss_lane = pad_to(jnp.tile(dissipation, (1, quarter)), 1, width, 1.0)
    ax_table = jnp.abs(cos_lane)[:, None] * speed_lane[None]
    ay_table = jnp.abs(sin_lane)[:, None] * speed_lane[None]
    base_table = ax_table + ay_table + loss_lane[None]

    ratio_lane = jnp.abs(sin_lane) / jnp.where(cos_lane == 0.0, 1.0, jnp.abs(cos_lane))
    lanes = jnp.stack([jnp.broadcast_to(rate_lane, (QUADS, width)), cos_lane, sin_lane,
                       jnp.broadcast_to(scale, (QUADS, width)), ratio_lane], axis=1)
    consts = jnp.concatenate([ax_table, base_table, lanes, diagonal], axis=1)
    consts = pad_to(consts, 1, -(-consts.shape[1] // 8) * 8)

    def by_class(table):
        chosen = jnp.broadcast_to(table[:, None, None, 0], (QUADS, rows, cells, width))
        for kind in range(1, class_count):
            chosen = jnp.where((class_here == kind)[None, :, :, None], table[:, None, None, kind], chosen)
        return chosen

    ax = by_class(ax_table)
    base = by_class(base_table)
    spread = jnp.maximum(
        cos_here[None, :, :, None] * cos_lane[:, None, None]
        + sin_here[None, :, :, None] * sin_lane[:, None, None], 0.0)
    wind = (rate_lane[None, None, None] * strength[None, :, :, None]) * (spread * spread)

    arrived, ax, base, wind, matrices = lax.optimization_barrier(
        (arrived, ax, base, wind, matrices))

    info = jnp.concatenate([sweep_order.reshape(-1), half[None].astype(jnp.int32)])
    block = cells + rows_dev
    rim_shapes = [jax.ShapeDtypeStruct((QUADS, size, width), jnp.float32)
                  for size in (block, block, HALO, HALO)]
    rim_own, rim_send, out_same, out_cross = pl.pallas_call(
        partial(rim_kernel, own, rows_dev, comps, quad_size),
        in_specs=[pl.BlockSpec(memory_space=pltpu.SMEM), in_vmem, in_vmem],
        out_specs=[in_vmem] * len(rim_shapes),
        out_shape=rim_shapes,
        compiler_params=pltpu.CompilerParams(vmem_limit_bytes=40 * 2**20),
    )(info, arrived, far_out)
    rim_partner = lax.ppermute(rim_send, axes, swap_route)
    rim_same = lax.ppermute(out_same, axes, same_route)
    rim_cross = lax.ppermute(out_cross, axes, cross_route)

    pairs = QUADS // 2
    packed = jax.ShapeDtypeStruct((quad_size, rows_dev, cols_dev), jnp.float32)
    halves = pl.pallas_call(
        partial(sweeps_kernel, rows, own, cells, quad_size, class_count),
        in_specs=[pl.BlockSpec(memory_space=pltpu.SMEM)] + [anywhere] * 3 + [in_vmem] * 6,
        out_specs=[in_vmem] * (2 * pairs),
        scratch_shapes=[
            pltpu.VMEM((QUADS, rows, cells, width), jnp.float32),
            pltpu.VMEM((QUADS, rows, cells, LANES), jnp.float32),
            pltpu.VMEM((QUADS, 2, cells, width), jnp.float32),
            pltpu.VMEM((QUADS, rows, 2 * HALO, width), jnp.float32),
            pltpu.VMEM((4, rows, width), jnp.float32),
            pltpu.VMEM((QUADS, rows, cells, width), jnp.float32),
            pltpu.VMEM((QUADS, rows, cells, width), jnp.float32),
            pltpu.VMEM((QUADS, rows, cells, width), jnp.float32),
            pltpu.SemaphoreType.DMA((3, QUADS)),
        ],
        out_shape=[packed] * (2 * pairs),
        compiler_params=pltpu.CompilerParams(vmem_limit_bytes=48 * 2**20),
    )(info, ax, base, wind, matrices, consts, rim_own, rim_partner, rim_same, rim_cross)

    got = [lax.ppermute(half_out, axes, swap_route) for half_out in halves[pairs:]]
    chunks = 4
    merged = []
    for pair in range(pairs):
        merged = [pl.pallas_call(
            partial(merge_kernel, own, pair, chunks),
            in_specs=[pl.BlockSpec(memory_space=pltpu.SMEM), in_vmem, in_vmem]
            + [pl.BlockSpec(memory_space=pl.ANY)] * len(merged),
            out_specs=pl.BlockSpec(memory_space=pl.ANY),
            scratch_shapes=[
                pltpu.VMEM((chunks, 2, quad_size // chunks, rows_dev, cols_dev), jnp.float32),
                pltpu.SemaphoreType.DMA((chunks, 2))],
            out_shape=jax.ShapeDtypeStruct((QUADS, quad_size, rows_dev, cols_dev), jnp.float32),
            input_output_aliases={3: 0} if merged else {},
            compiler_params=pltpu.CompilerParams(vmem_limit_bytes=16 * 2**20),
        )(info, halves[pair], got[pair], *merged)]
    return merged[0].reshape(comps, rows_dev, cols_dev)


def solution(mesh):
    placed = (
        P("rows", "cols"),
        P("rows", "cols"),
        P("rows", "cols"),
        P(),
        P(),
        P(),
        P(("rows", "cols"), None),
        P(("rows", "cols")),
        P(),
        P(),
    )
    return jax.shard_map(
        body, mesh=mesh, in_specs=placed, out_specs=P(None, "rows", "cols"), check_vma=False
    )
```

```python
from functools import partial
import math

import jax
import jax.numpy as jnp
import numpy as np
from jax import lax
from jax.experimental import pallas as pl
from jax.experimental.pallas import tpu as pltpu
from jax.sharding import PartitionSpec as P

NDIR = 36
NFREQ = 24
CAP = 16
ITERS = 2
QUADS = 4
LANES = 128
HALO = 8

whitecap_rate = 0.5


def split_bf16(value):
    high = value.astype(jnp.bfloat16)
    low = (value - high.astype(jnp.float32)).astype(jnp.bfloat16)
    return high, low


def lane_scale(width):
    golden = (math.sqrt(5.0) - 1.0) / 2.0
    return np.exp2(np.mod(np.arange(width) * golden, 1.0)).astype(np.float32)


def pad_to(array, axis, size, value=0.0):
    widths = [(0, 0)] * array.ndim
    widths[axis] = (0, size - array.shape[axis])
    return jnp.pad(array, widths, constant_values=value)


def pack_kernel(shifts, col_count, rows, comps, dest_hbm, spectra_hbm, wind_hbm, dir_hbm, class_hbm,
                out_ref, held_ref, dest_ref, spectra_ref, class_ref, high, low, slots, sems):
    step = pl.program_id(0)
    points = dest_ref.shape[1]
    load = out_ref.shape[1]
    total_bits, row_bits, col_bits = shifts

    @pl.when(step == 0)
    def _():
        pieces = ((dest_hbm, dest_ref), (spectra_hbm, spectra_ref), (wind_hbm, held_ref.at[0]),
                  (dir_hbm, held_ref.at[1]), (class_hbm, class_ref))
        copies = [pltpu.make_async_copy(source, target, sems.at[index])
                  for index, (source, target) in enumerate(pieces)]
        for copy in copies:
            copy.start()
        copies[0].wait()
        dest = dest_ref[...]
        grid_row = lax.shift_right_logical(dest, total_bits)
        grid_col = dest & (2**total_bits - 1)
        local_row = grid_row & (2**row_bits - 1)
        local_col = grid_col & (2**col_bits - 1)
        owner = (lax.shift_right_logical(grid_row, row_bits) * col_count
                 + lax.shift_right_logical(grid_col, col_bits))
        on_row = (grid_row == 0) | (grid_row == rows - 1)
        on_left = jnp.where(grid_col == 0, 2**col_bits, 2**col_bits + 2**row_bits) + local_row
        code = jnp.where(on_row, local_col, on_left) + 1
        lanes = jnp.concatenate(
            [owner.astype(jnp.float32), code.astype(jnp.float32), jnp.zeros((6, points), jnp.float32)],
            axis=0)
        columns = lanes.T
        same = columns[:, 0:1] == lanes[0:1]
        above = (lax.broadcasted_iota(jnp.int32, (points, points), 0)
                 < lax.broadcasted_iota(jnp.int32, (points, points), 1))
        rank = jnp.sum(jnp.where(same & above, 1.0, 0.0), axis=0, keepdims=True)
        slots[...] = owner * CAP + rank.astype(jnp.int32)
        for copy in copies[1:]:
            copy.wait()
        held_ref[2] = class_ref[...].astype(jnp.float32)
        spectra = jnp.concatenate(
            [spectra_ref[...], jnp.broadcast_to(lanes[1:2], (load - comps, points))], axis=0)
        high[...], low[...] = split_bf16(spectra)

    place = jnp.where(
        lax.broadcasted_iota(jnp.int32, (out_ref.shape[0], points), 0) + step * out_ref.shape[0]
        == slots[...], 1.0, 0.0).astype(jnp.bfloat16)
    over_points = (((1,), (1,)), ((), ()))
    out_ref[...] = (lax.dot_general(place, high[...], over_points, preferred_element_type=jnp.float32)
                    + lax.dot_general(place, low[...], over_points, preferred_element_type=jnp.float32))


def rim_kernel(own, rows_dev, comps, quad_size, info, arrived_ref, far_ref, own_ref, send_ref, same_ref,
               cross_ref):
    half = info[ITERS * QUADS]
    cols_dev = 2 * own
    cells = own + HALO
    block = cells + rows_dev
    width = own_ref.shape[2]
    load = arrived_ref.shape[1]
    spots = -(-(2 * block + 2 * HALO) // LANES) * LANES
    lane = lax.broadcasted_iota(jnp.int32, (1, spots), 1)
    at_send = lane >= block
    spot = jnp.where(at_send, lane - block, lane)
    side_at = jnp.where(at_send, 1 - half, half)
    want = jnp.where(spot < own, own * side_at + spot, -1)
    want = jnp.where((spot == own) & (side_at == 0), own, want)
    want = jnp.where((spot == cells - 1) & (side_at == 1), own - 1, want)
    want = jnp.where(spot >= cells, cols_dev + rows_dev * side_at + spot - cells, want)
    rest = lane - 2 * block
    to_left = jnp.where((rest == HALO - 1) & (half == 0), cols_dev - 1, -1)
    to_left = jnp.where((rest == 0) & (half == 1), 0, to_left)
    to_left = jnp.where((rest == HALO) & (half == 0), 0, to_left)
    to_left = jnp.where((rest == 2 * HALO - 1) & (half == 1), cols_dev - 1, to_left)
    want = jnp.where(rest >= 0, to_left, want)
    code = arrived_ref[:, comps:comps + 1]
    gather = jnp.where(code == (want + 1).astype(jnp.float32), 1.0, 0.0)
    gather = jnp.where(want >= 0, gather, 0.0).astype(jnp.bfloat16)
    high, low = split_bf16(arrived_ref[...])
    over_points = (((0,), (0,)), ((), ()))
    summed = (lax.dot_general(gather, high, over_points, preferred_element_type=jnp.float32)
              + lax.dot_general(gather, low, over_points, preferred_element_type=jnp.float32))
    for quad in range(QUADS):
        start = quad * quad_size
        part = summed if quad == 0 else pltpu.roll(summed, load - start, 1)
        own_ref[quad] = part[:block, :width]
        send_ref[quad] = part[block:2 * block, :width]
        halo = part[2 * block:2 * block + HALO, :width]
        free = lax.broadcasted_iota(jnp.int32, halo.shape, 1) >= quad_size
        same_ref[quad] = jnp.where(free, far_ref[quad], halo)
        cross_ref[quad] = part[2 * block + HALO:2 * block + 2 * HALO, :width]


def sweeps_kernel(rows, own, cells, quad_size, class_count, info, ax_hbm, base_hbm,
                  wind_hbm, mt_ref, const_ref, own_ref, par_ref, same_ref, cross_ref, *rest):
    pairs = QUADS // 2
    keep_refs, send_refs = rest[:pairs], rest[pairs:2 * pairs]
    state, power, rim, side, far_rows, ax_ref, base_ref, wind_ref, sems = rest[2 * pairs:]
    half = info[ITERS * QUADS]
    width = mt_ref.shape[2]
    rows_dev = rows // 2

    def fetch(turn):
        quad = info[turn]
        return [pltpu.make_async_copy(source.at[quad], target.at[quad], sems.at[index, turn])
                for index, (source, target) in enumerate(
                    ((ax_hbm, ax_ref), (base_hbm, base_ref), (wind_hbm, wind_ref)))]

    for copy in fetch(0):
        copy.start()
    power[...] = jnp.zeros_like(power)
    numbers = jnp.concatenate(
        [same_ref[feat, 0:1, width - LANES:] for feat in range(4)]
        + [jnp.zeros((4, LANES), jnp.float32)], axis=0).T
    for feat in range(4):
        far_rows[feat] = jnp.broadcast_to(
            numbers[LANES - rows:, feat:feat + 1], (rows, width))
    far_at = jnp.where(half == 0, HALO - 1, 0)
    at_far = lax.broadcasted_iota(jnp.int32, (HALO, width), 0) == far_at
    edge_at = jnp.where(half == 0, 0, 2 * HALO - 1)
    at_edge = lax.broadcasted_iota(jnp.int32, (2 * HALO, width), 0) == edge_at
    for quad in range(QUADS):
        rim[quad, 0] = own_ref[quad, 0:cells]
        rim[quad, 0, own:cells] = own_ref[quad, own:cells] + same_ref[quad]
        rim[quad, 1] = par_ref[quad, 0:cells]
        rim[quad, 1, own:cells] = par_ref[quad, own:cells] + cross_ref[quad]
        for j in range(rows_dev):
            mine = jnp.where(at_edge, own_ref[quad, cells + j:cells + j + 1], 0.0)
            theirs = jnp.where(at_edge, par_ref[quad, cells + j:cells + j + 1], 0.0)
            side[quad, j + rows_dev * half] = mine
            side[quad, j + rows_dev * (1 - half)] = theirs

    def pack_rows(pair, j, lane, out_ref, side_at):
        row = rows_dev * side_at + j
        first, other = info[QUADS + 2 * pair], info[QUADS + 2 * pair + 1]
        span = pl.ds(lane, LANES)
        both = jnp.concatenate([state[first, row, :own, span], state[other, row, :own, span]], axis=0)
        stop = min(quad_size - lane, LANES)
        out_ref[lane:lane + stop, j, :] = both.T[:stop]

    def sweep(turn, count, second, extra=None):
        quad = info[turn]
        ax_table = const_ref[quad, :class_count]
        base_table = const_ref[quad, class_count:2 * class_count]
        rate_lane, cos_lane, sin_lane, scale_lane, ratio_lane, diag_lane = [
            const_ref[quad, 2 * class_count + each:2 * class_count + each + 1] for each in range(6)]
        down = (quad == 0) | (quad == 3)
        step_x = jnp.where(down, 1, -1)
        first_row = jnp.where(down, 0, rows - 1)
        up_y = quad < 2

        def patched(block, far_row):
            if second:
                return block
            return jnp.concatenate([block[:own], jnp.where(at_far, far_row, block[own:])], axis=0)

        def factors(i, low, high):
            row = first_row + i * step_x
            kind, strength, far_cos, far_sin = [
                far_rows[feat, pl.ds(row, 1), :] for feat in range(4)]
            far_ax = jnp.zeros((1, width), jnp.float32)
            far_base = jnp.zeros((1, width), jnp.float32)
            for each in range(class_count):
                far_ax = jnp.where(kind == each, ax_table[each:each + 1], far_ax)
                far_base = jnp.where(kind == each, base_table[each:each + 1], far_base)
            spread = jnp.maximum(far_cos * cos_lane + far_sin * sin_lane, 0.0)
            far_wind = (rate_lane * strength) * (spread * spread)
            total = power[0, row, low:high]
            for other in range(1, QUADS):
                total = total + power[other, row, low:high]
            level = total * (1.0 / (QUADS * quad_size))
            damping = whitecap_rate * level / (1.0 + level)
            den = patched(base_ref[quad, row, low:high], far_base) + jnp.concatenate([damping] * (width // LANES), axis=1)
            inverse = scale_lane / den
            source = patched(wind_ref[quad, row, low:high], far_wind)
            edge = side[quad, row]
            parts = [source[:HALO] + edge[:HALO], source[HALO:own - HALO],
                     source[own - HALO:own] + edge[HALO:]]
            if high > own:
                parts.append(source[own:])
            source = jnp.concatenate(parts, axis=0)
            if i == 0 or i == rows - 1:
                here = jnp.where(row // rows_dev == half, 0, 1)
                source = source + rim[quad, here, low:high]
            if second:
                before = state[quad, row]
                shifted = jnp.where(up_y, pltpu.roll(before, 1, 0), pltpu.roll(before, cells - 1, 0))
                source = source + ax_ref[quad, row, low:high] * (ratio_lane * shifted[low:high])
            return patched(ax_ref[quad, row, low:high], far_ax) * inverse, source * inverse

        def store(i, value):
            row = first_row + i * step_x
            square = value * value
            folded = square[:, :LANES]
            for lane in range(LANES, width, LANES):
                folded = folded + square[:, lane:lane + LANES]
            state[quad, row, :count] = value
            power[quad, row, :count] = jnp.broadcast_to(
                jnp.sum(folded, axis=1, keepdims=True), (count, LANES))

        balance = factors(0, 0, count)[1]
        upwind = None
        for i in range(rows):
            mixed = jnp.dot(balance.astype(jnp.bfloat16), mt_ref[quad],
                            preferred_element_type=jnp.float32)
            direct = diag_lane * balance
            if i + 1 < rows:
                along, known = factors(i + 1, 0, count)
                balance = along * mixed + (along * direct + known)
            if extra is not None:
                extra(i)
            if i > 0:
                store(i - 1, upwind)
            upwind = direct + mixed
        store(rows - 1, upwind)

    @pl.loop(0, QUADS)
    def _(turn):
        for copy in fetch(turn):
            copy.wait()

        @pl.when(turn + 1 < QUADS)
        def _():
            for copy in fetch(turn + 1):
                copy.start()

        sweep(turn, cells, False)

    @pl.loop(QUADS, ITERS * QUADS - 2)
    def _(turn):
        sweep(turn, own, True)

    tiles = width // LANES
    assert rows == rows_dev * tiles

    def between(out_ref, side_at):
        return lambda i: pack_rows(0, i // tiles, i % tiles * LANES, out_ref, side_at)

    sweep(ITERS * QUADS - 2, own, True, between(keep_refs[0], half))
    sweep(ITERS * QUADS - 1, own, True, between(send_refs[0], 1 - half))
    for j in range(rows_dev):
        for lane in range(0, width, LANES):
            pack_rows(1, j, lane, keep_refs[1], half)
            pack_rows(1, j, lane, send_refs[1], 1 - half)


def merge_kernel(own, pair, chunks, info, keep_ref, got_ref, *rest):
    out_ref, stage, sems = rest[-3:]
    half = info[ITERS * QUADS]
    part = keep_ref.shape[0] // chunks
    copies = []
    for chunk in range(chunks):
        span = pl.ds(chunk * part, part)
        keep = keep_ref[span]
        got = got_ref[span]
        left = jnp.where(half == 0, keep, got)
        right = jnp.where(half == 0, got, keep)
        low = lax.broadcasted_iota(jnp.int32, keep.shape, 2) < own
        stage[chunk, 0] = jnp.where(low, left, pltpu.roll(right, own, 2))
        stage[chunk, 1] = jnp.where(low, pltpu.roll(left, own, 2), right)
        for member in range(2):
            copies.append(pltpu.make_async_copy(
                stage.at[chunk, member], out_ref.at[info[QUADS + 2 * pair + member], span], sems.at[chunk, member]))
            copies[-1].start()
    for copy in copies:
        copy.wait()


def body(
    wind_speed,
    wind_dir,
    depth_class,
    group_speed,
    dissipation,
    input_rate,
    outer_spectra,
    dest_cell,
    refraction_inverse,
    sweep_order,
):
    rows_dev, cols_dev = wind_speed.shape
    row_count = lax.axis_size("rows")
    col_count = lax.axis_size("cols")
    assert row_count == 2
    devices = row_count * col_count
    rows = rows_dev * row_count
    own = cols_dev // 2
    cells = own + HALO
    class_count = group_speed.shape[0]
    comps = outer_spectra.shape[1]
    quad_size = refraction_inverse.shape[1]
    quarter = NDIR // QUADS
    width = -(-quad_size // LANES) * LANES
    axes = ("rows", "cols")
    half = lax.axis_index("rows")

    def device(row_at, col_at):
        return row_at * col_count + col_at

    span = range(col_count)
    swap_route = [(device(1 - h, c), device(h, c)) for h in range(2) for c in span]
    same_route = [(device(0, c - 1), device(0, c)) for c in span if c > 0]
    same_route += [(device(1, c + 1), device(1, c)) for c in span if c + 1 < col_count]
    cross_route = [(device(1, c - 1), device(0, c)) for c in span if c > 0]
    cross_route += [(device(0, c + 1), device(1, c)) for c in span if c + 1 < col_count]

    points = dest_cell.shape[0]
    load = -(-(comps + 1) // LANES) * LANES
    sizes = (cols_dev * col_count, rows_dev, cols_dev)
    shifts = tuple(size.bit_length() - 1 for size in sizes)
    assert all(size == 2**shift for size, shift in zip(sizes, shifts))
    slot_total = devices * CAP
    steps = 2
    in_vmem = pl.BlockSpec(memory_space=pltpu.VMEM)
    anywhere = pl.BlockSpec(memory_space=pl.ANY)
    outgoing, held = pl.pallas_call(
        partial(pack_kernel, shifts, col_count, rows, comps),
        grid=(steps,),
        in_specs=[anywhere] * 5,
        out_specs=[pl.BlockSpec((slot_total // steps, load), lambda s: (s, 0)), in_vmem],
        scratch_shapes=[pltpu.VMEM((1, points), jnp.int32),
                        pltpu.VMEM((comps, points), jnp.float32),
                        pltpu.VMEM((rows_dev, cols_dev), jnp.int32),
                        pltpu.VMEM((load, points), jnp.bfloat16),
                        pltpu.VMEM((load, points), jnp.bfloat16),
                        pltpu.VMEM((1, points), jnp.int32),
                        pltpu.SemaphoreType.DMA((5,))],
        out_shape=[jax.ShapeDtypeStruct((slot_total, load), jnp.float32),
                   jax.ShapeDtypeStruct((3, rows_dev, cols_dev), jnp.float32)],
        compiler_params=pltpu.CompilerParams(
            dimension_semantics=("arbitrary",), vmem_limit_bytes=60 * 2**20),
    )(dest_cell.reshape(1, points), outer_spectra.T, wind_speed, wind_dir, depth_class)
    outgoing, refraction_inverse = lax.optimization_barrier((outgoing, refraction_inverse))
    scale = jnp.asarray(lane_scale(width))
    flipped = pad_to(pad_to(jnp.swapaxes(refraction_inverse, 1, 2), 1, width), 2, width)
    scaled = flipped / scale[None, :, None]
    on_diag = jnp.eye(width, dtype=bool)[None]
    matrices = jnp.where(on_diag, 0.0, scaled).astype(jnp.bfloat16)
    diagonal = jnp.sum(jnp.where(on_diag, scaled, 0.0), axis=1, keepdims=True)
    arrived = lax.all_to_all(outgoing.reshape(devices, CAP, load), axes, split_axis=0,
                             concat_axis=0, tiled=True).reshape(slot_total, load)

    partner = lax.ppermute(held, axes, swap_route)
    is_low = half == 0
    chip = jnp.concatenate(
        [jnp.where(is_low, held, partner), jnp.where(is_low, partner, held)], axis=1)
    strength = (chip[0] * 0.1) ** 2
    feats = jnp.stack([chip[2], strength, jnp.cos(chip[1]), jnp.sin(chip[1])])
    assert width - rows >= quad_size and rows <= LANES
    far_out = jnp.pad(
        jnp.where(is_low, feats[:, :, cols_dev - 1], feats[:, :, 0])[:, None],
        ((0, 0), (0, 0), (width - rows, 0)))
    mine = jnp.where(is_low, feats[:, :, :own], feats[:, :, own:])
    right = jnp.where(is_low, feats[:, :, own], 0.0)
    left = jnp.where(is_low, 0.0, feats[:, :, own - 1])
    grid = jnp.concatenate(
        [mine, right[:, :, None], jnp.zeros((4, rows, HALO - 2), jnp.float32), left[:, :, None]], axis=2)
    class_here, strength, cos_here, sin_here = grid[0], grid[1], grid[2], grid[3]

    angle = (jnp.arange(NDIR, dtype=jnp.float32) + 0.5) * (2.0 * math.pi / NDIR)
    cos_lane = pad_to(jnp.repeat(jnp.cos(angle), NFREQ).reshape(QUADS, quad_size), 1, width)
    sin_lane = pad_to(jnp.repeat(jnp.sin(angle), NFREQ).reshape(QUADS, quad_size), 1, width)
    rate_lane = pad_to(jnp.tile(input_rate, quarter), 0, width)
    speed_lane = pad_to(jnp.tile(group_speed, (1, quarter)), 1, width)
    loss_lane = pad_to(jnp.tile(dissipation, (1, quarter)), 1, width, 1.0)
    ax_table = jnp.abs(cos_lane)[:, None] * speed_lane[None]
    ay_table = jnp.abs(sin_lane)[:, None] * speed_lane[None]
    base_table = ax_table + ay_table + loss_lane[None]

    ratio_lane = jnp.abs(sin_lane) / jnp.where(cos_lane == 0.0, 1.0, jnp.abs(cos_lane))
    lanes = jnp.stack([jnp.broadcast_to(rate_lane, (QUADS, width)), cos_lane, sin_lane,
                       jnp.broadcast_to(scale, (QUADS, width)), ratio_lane], axis=1)
    consts = jnp.concatenate([ax_table, base_table, lanes, diagonal], axis=1)
    consts = pad_to(consts, 1, -(-consts.shape[1] // 8) * 8)

    def by_class(table):
        chosen = jnp.broadcast_to(table[:, None, None, 0], (QUADS, rows, cells, width))
        for kind in range(1, class_count):
            chosen = jnp.where((class_here == kind)[None, :, :, None], table[:, None, None, kind], chosen)
        return chosen

    ax = by_class(ax_table)
    base = by_class(base_table)
    spread = jnp.maximum(
        cos_here[None, :, :, None] * cos_lane[:, None, None]
        + sin_here[None, :, :, None] * sin_lane[:, None, None], 0.0)
    wind = (rate_lane[None, None, None] * strength[None, :, :, None]) * (spread * spread)

    arrived, ax, base, wind, matrices = lax.optimization_barrier(
        (arrived, ax, base, wind, matrices))

    info = jnp.concatenate([sweep_order.reshape(-1), half[None].astype(jnp.int32)])
    block = cells + rows_dev
    rim_shapes = [jax.ShapeDtypeStruct((QUADS, size, width), jnp.float32)
                  for size in (block, block, HALO, HALO)]
    rim_own, rim_send, out_same, out_cross = pl.pallas_call(
        partial(rim_kernel, own, rows_dev, comps, quad_size),
        in_specs=[pl.BlockSpec(memory_space=pltpu.SMEM), in_vmem, in_vmem],
        out_specs=[in_vmem] * len(rim_shapes),
        out_shape=rim_shapes,
        compiler_params=pltpu.CompilerParams(vmem_limit_bytes=40 * 2**20),
    )(info, arrived, far_out)
    rim_partner = lax.ppermute(rim_send, axes, swap_route)
    rim_same = lax.ppermute(out_same, axes, same_route)
    rim_cross = lax.ppermute(out_cross, axes, cross_route)

    pairs = QUADS // 2
    packed = jax.ShapeDtypeStruct((quad_size, rows_dev, cols_dev), jnp.float32)
    halves = pl.pallas_call(
        partial(sweeps_kernel, rows, own, cells, quad_size, class_count),
        in_specs=[pl.BlockSpec(memory_space=pltpu.SMEM)] + [anywhere] * 3 + [in_vmem] * 6,
        out_specs=[in_vmem] * (2 * pairs),
        scratch_shapes=[
            pltpu.VMEM((QUADS, rows, cells, width), jnp.float32),
            pltpu.VMEM((QUADS, rows, cells, LANES), jnp.float32),
            pltpu.VMEM((QUADS, 2, cells, width), jnp.float32),
            pltpu.VMEM((QUADS, rows, 2 * HALO, width), jnp.float32),
            pltpu.VMEM((4, rows, width), jnp.float32),
            pltpu.VMEM((QUADS, rows, cells, width), jnp.float32),
            pltpu.VMEM((QUADS, rows, cells, width), jnp.float32),
            pltpu.VMEM((QUADS, rows, cells, width), jnp.float32),
            pltpu.SemaphoreType.DMA((3, QUADS)),
        ],
        out_shape=[packed] * (2 * pairs),
        compiler_params=pltpu.CompilerParams(vmem_limit_bytes=48 * 2**20),
    )(info, ax, base, wind, matrices, consts, rim_own, rim_partner, rim_same, rim_cross)

    got = [lax.ppermute(half_out, axes, swap_route) for half_out in halves[pairs:]]
    chunks = 4
    merged = []
    for pair in range(pairs):
        merged = [pl.pallas_call(
            partial(merge_kernel, own, pair, chunks),
            in_specs=[pl.BlockSpec(memory_space=pltpu.SMEM), in_vmem, in_vmem]
            + [pl.BlockSpec(memory_space=pl.ANY)] * len(merged),
            out_specs=pl.BlockSpec(memory_space=pl.ANY),
            scratch_shapes=[
                pltpu.VMEM((chunks, 2, quad_size // chunks, rows_dev, cols_dev), jnp.float32),
                pltpu.SemaphoreType.DMA((chunks, 2))],
            out_shape=jax.ShapeDtypeStruct((QUADS, quad_size, rows_dev, cols_dev), jnp.float32),
            input_output_aliases={3: 0} if merged else {},
            compiler_params=pltpu.CompilerParams(vmem_limit_bytes=16 * 2**20),
        )(info, halves[pair], got[pair], *merged)]
    return merged[0].reshape(comps, rows_dev, cols_dev)


def solution(mesh):
    placed = (
        P("rows", "cols"),
        P("rows", "cols"),
        P("rows", "cols"),
        P(),
        P(),
        P(),
        P(("rows", "cols"), None),
        P(("rows", "cols")),
        P(),
        P(),
    )
    return jax.shard_map(
        body, mesh=mesh, in_specs=placed, out_specs=P(None, "rows", "cols"), check_vma=False
    )
```
